128 devices in a mesh: ctx: 32 (over y, z, x_hi), tp: 4 (over x_lo, core).
Axes of the slice: x: 4 (x_hi: 2, x_lo: 2; x = x_hi * 2 + x_lo), y: 4, z: 4, core: 2. Of those that a mesh axis runs over, the one named last changes fastest.
Arguments:
- kv_product: bfloat16 [2048, 32768], P('tp', 'ctx'), may hold values from -6 to 6
- query: bfloat16 [2048, 32768], P('tp', 'ctx'), may hold values from -6 to 6
- decay_rate: float32 [2048, 16], P('tp'), as said below
- residue: float32 [2048, 16], P('tp'), may hold values from -1.5 to 1.5
- out_weight: bfloat16 [2048, 2048], P('tp'), may hold values from -0.125 to 0.125
Outputs:
- output: bfloat16 [32768, 2048], P(('ctx', 'tp'))
The draws below stay inside these ranges and needn't reach their ends.
Inputs may be any that keep to these rules, and one draw needn't show every extreme that they name: `decay_rate`: every rate is positive and at most 0.08.
All inputs are finite; a program needn't handle non-finite values.
Results may differ from the reference program's by a relative error of at most 0.0058.
Values may be sent and summed in bfloat16 or wider, within the bound.
A program may use at most 128 MiB of HBM per device.

```python
import math
import jax
import jax.numpy as jnp
from jax import lax

D_WIN = 2048
MODES = 16
SEQ = 32768


def draw_decay_rate(key, part):
    key = jax.random.fold_in(key, 7)
    lowest = math.log(0.25 / SEQ)
    highest = math.log(0.08)
    log_rates = jax.random.uniform(key, (D_WIN, MODES), jnp.float32, lowest, highest)
    return jnp.exp(log_rates).astype(jnp.float32)


def steps_of(rng, shape, cuts, low, top_value):
    level, own = 1.0, jax.random.fold_in(rng, 6)
    for axis_at, shards_of in cuts:
        heights = jnp.exp(jax.random.uniform(jax.random.fold_in(own, axis_at), (shards_of,), jnp.float32, low / len(cuts), top_value / len(cuts)))
        level = level * jnp.repeat(heights, shape[axis_at] // shards_of).reshape([-1 if axis == axis_at else 1 for axis in range(len(shape))])
    return level


def gaussian(rng, shape, scale, limit, pieces=(), kind=jnp.bfloat16):
    factor_of = steps_of(rng, shape, pieces, -0.22, 0.18) if pieces else 1.0
    drawn = jax.random.normal(rng, shape, jnp.float32) * scale * factor_of
    return jnp.minimum(jnp.maximum(drawn, -limit), limit).astype(kind)


def setup_inputs(seed: int = 0) -> dict:
    key_list = jax.random.split(jax.random.key(seed), 6)
    return {
        "kv_product": gaussian(key_list[0], (D_WIN, SEQ), 1.0, 6.0, ((0, 4), (1, 32))),
        "query": gaussian(key_list[1], (D_WIN, SEQ), 1.0, 6.0, ((0, 4), (1, 32))),
        "decay_rate": draw_decay_rate(jax.random.fold_in(key_list[5], 71), 0),
        "residue": gaussian(key_list[3], (D_WIN, MODES), 0.25, 1.5, ((0, 4),), jnp.float32),
        "out_weight": gaussian(key_list[4], (D_WIN, D_WIN), D_WIN ** -0.5, 0.125, ((0, 4),)),
    }


def reference(kv_product, query, decay_rate, residue, out_weight):
    block_size = min(128, D_WIN)
    block_count = D_WIN // block_size
    positions = jnp.arange(SEQ, dtype=jnp.float32)

    def convolve(operands):
        signal, gate_rows, decays, weights = operands
        impulse = jnp.zeros((block_size, SEQ), jnp.float32)
        for mode_index in range(MODES):
            mode_rate = decays[:, mode_index:mode_index + 1]
            impulse = impulse + weights[:, mode_index:mode_index + 1] * jnp.sqrt(-jnp.expm1(-2.0 * mode_rate)) * jnp.exp(-mode_rate * positions[None, :])
        spectrum = jnp.fft.rfft(signal.astype(jnp.float32), axis=-1) * jnp.fft.rfft(impulse, axis=-1)
        convolved = jnp.fft.irfft(spectrum, n=SEQ, axis=-1).astype(jnp.bfloat16)
        convolved = lax.optimization_barrier(convolved)
        return (gate_rows.astype(jnp.float32) * convolved.astype(jnp.float32)).astype(jnp.bfloat16)
    gated_all = lax.map(convolve, (kv_product.reshape(block_count, block_size, SEQ), query.reshape(block_count, block_size, SEQ), decay_rate.reshape(block_count, block_size, MODES), residue.reshape(block_count, block_size, MODES)))
    gated_all = gated_all.reshape(D_WIN, SEQ)
    projected = lax.dot_general(gated_all, out_weight, (((0,), (0,)), ((), ())), preferred_element_type=jnp.float32)
    return projected.astype(jnp.bfloat16)
```

```python
import jax
import jax.numpy as jnp
from jax import lax
from jax.experimental import pallas as pl
from jax.experimental.pallas import tpu as pltpu
from jax.sharding import PartitionSpec as P

NY, NZ, NX, NTP = 4, 4, 2, 4
SUBS, LANES = 8, 128
W_PIECES, W_DIRECT = 8, 3
MESH = pl.DeviceIdType.MESH


def one_minus_exp(z):
    series = jnp.ones_like(z)
    for n in range(10, 1, -1):
        series = 1.0 - (z * (1.0 / n)) * series
    return jnp.where(z < 0.5, z * series, 1.0 - jnp.exp(-z))


def shift_rows(value, by, row):
    return jnp.where(row >= by, pltpu.roll(value, by, 0), 0.0)


def kernel(
    kv_hbm, q_hbm, dec_hbm, res_hbm, w_hbm, out_ref,
    kv_v, q_v, dec_v, res_v, wf, xs, qs, ys, dec_t, lam_t, wgt_t, wc_t, ends,
    s_own, s_x, g_z, h_y, inc, gb, gin, acc,
    loc_sem, x_sem, z_send, z_recv, y_send, y_recv,
    wsib_sem, wp_send, wp_recv, wf_send, wf_recv, g_send, g_recv,
):
    chans, toks = kv_v.shape
    modes = dec_v.shape[1]
    groups = chans // LANES
    sub_len = toks // SUBS
    out_toks, cols = out_ref.shape
    seq = float(toks * NY * NZ * NX)

    ctx, tp = lax.axis_index("ctx"), lax.axis_index("tp")
    x_hi = lax.rem(ctx, NX)
    z = lax.rem(ctx // NX, NZ)
    y = ctx // (NX * NZ)
    x_lo, core = tp // 2, lax.rem(tp, 2)

    def ctx_of(yy, zz, xx):
        return (yy * NZ + zz) * NX + xx

    partner_tp = [tp, x_lo * 2 + (1 - core), (1 - x_lo) * 2 + core, (1 - x_lo) * 2 + (1 - core)]
    to_x = {"ctx": ctx_of(y, z, 1 - x_hi), "tp": tp}
    to_z = [{"ctx": ctx_of(y, lax.rem(z + j, NZ), x_hi), "tp": tp} for j in range(NZ)]
    to_y = [{"ctx": ctx_of(lax.rem(y + j, NY), z, x_hi), "tp": tp} for j in range(NY)]
    to_tp = [{"ctx": ctx, "tp": t} for t in partner_tp]
    to_wrap = {"ctx": ctx_of(y, z, 1 - x_hi), "tp": partner_tp[2]}

    loads = [
        pltpu.make_async_copy(dec_hbm, dec_v, loc_sem.at[0]),
        pltpu.make_async_copy(res_hbm, res_v, loc_sem.at[1]),
        pltpu.make_async_copy(kv_hbm, kv_v, loc_sem.at[2]),
        pltpu.make_async_copy(q_hbm, q_v, loc_sem.at[3]),
        pltpu.make_async_copy(w_hbm, wf.at[0], loc_sem.at[4]),
    ]
    for load in loads:
        load.start()

    barrier = pltpu.get_barrier_semaphore()
    partners = [to_x] + to_z[1:] + to_y[1:] + to_tp[1:] + [to_wrap]
    for partner in partners:
        pl.semaphore_signal(barrier, inc=1, device_id=partner, device_id_type=MESH)
    pl.semaphore_wait(barrier, len(partners))

    def remote(src, dst, send, recv, to):
        return pltpu.make_async_remote_copy(
            src_ref=src, dst_ref=dst, send_sem=send, recv_sem=recv, device_id=to, device_id_type=MESH
        )

    w_sib = remote(w_hbm, wf.at[1], wsib_sem.at[0], wsib_sem.at[1], to_tp[1])
    w_rows = chans // W_PIECES
    w_cross, w_fwd = [], []
    for p in range(W_PIECES):
        rows = pl.ds(p * w_rows, w_rows)
        to = to_tp[2] if p < W_DIRECT else to_wrap
        w_cross.append(remote(w_hbm.at[rows], wf.at[2, rows], wp_send.at[p], wp_recv.at[p], to))
        w_fwd.append(remote(wf.at[2, rows], wf.at[3, rows], wf_send.at[p], wf_recv.at[p], to_tp[1]))
    w_order = []
    for i in range(W_PIECES):
        for p in (W_DIRECT + i, i):
            if (p < W_DIRECT if p == i else p < W_PIECES):
                w_order.append(p)
    for p in w_order:
        w_cross[p].start()
    w_sib.start()

    loads[0].wait()
    loads[1].wait()
    for g in range(groups):
        rows = slice(g * LANES, (g + 1) * LANES)
        dec = dec_v[rows, :].T
        res = res_v[rows, :].T
        wgt = res * jnp.sqrt(one_minus_exp(2.0 * dec))
        dec_t[g] = dec
        lam_t[g] = jnp.exp(-dec)
        wgt_t[g] = wgt
        wc_t[g] = wgt * one_minus_exp(seq * dec)

    tile = 2 * LANES
    eye = (
        lax.broadcasted_iota(jnp.int32, (tile, tile), 0) == lax.broadcasted_iota(jnp.int32, (tile, tile), 1)
    ).astype(jnp.bfloat16)

    def turn(src, dst):
        for cb in range(chans // tile):
            for tb in range(toks // tile):
                block = src[cb * tile:(cb + 1) * tile, tb * tile:(tb + 1) * tile]
                turned = lax.dot_general(
                    eye, block, (((1,), (1,)), ((), ())), preferred_element_type=jnp.float32
                )
                dst[2 * cb, tb * tile:(tb + 1) * tile, :] = turned[:, :LANES]
                dst[2 * cb + 1, tb * tile:(tb + 1) * tile, :] = turned[:, LANES:]

    loads[2].wait()
    turn(kv_v, xs)

    row = lax.broadcasted_iota(jnp.int32, (SUBS, LANES), 0)
    left = (SUBS - 1 - row).astype(jnp.float32) * float(sub_len)

    def wide(ref, g, m):
        return jnp.broadcast_to(ref[g, m:m + 1, :], (SUBS, LANES))

    def first_pass(g, carry):
        lam = [wide(lam_t, g, m) for m in range(modes)]

        def step(t, states):
            x = xs[g, pl.ds(t, SUBS, stride=sub_len), :]
            return tuple(l * u + x for l, u in zip(lam, states))

        states = lax.fori_loop(
            0, sub_len, step, tuple(jnp.zeros((SUBS, LANES), jnp.float32) for _ in range(modes)), unroll=8
        )
        for m in range(modes):
            ends[g, m] = states[m]
            decayed = states[m] * jnp.exp(-wide(dec_t, g, m) * left)
            s_own[g, m:m + 1, :] = jnp.sum(decayed, axis=0, keepdims=True)
        return carry

    lax.fori_loop(0, groups, first_pass, 0)

    block = float(toks)
    send_x = remote(s_own, s_x, x_sem.at[0], x_sem.at[1], to_x)
    send_x.start()
    loads[3].wait()
    turn(q_v, qs)
    send_x.wait_recv()
    dec = dec_t[...]
    lam1 = jnp.exp(-block * dec)
    mine, other = s_own[...], s_x[...]
    g_z[0] = jnp.where(x_hi == 0, other + lam1 * mine, mine + lam1 * other)
    sends_z = [remote(g_z.at[0], g_z.at[j], z_send.at[j], z_recv.at[j], to_z[j]) for j in range(1, NZ)]
    for send in sends_z:
        send.start()
    for send in sends_z:
        send.wait_recv()
    total = jnp.zeros_like(dec)
    before = jnp.zeros_like(dec)
    for j in range(NZ):
        part = g_z[j]
        after = (NZ - 1 - lax.rem(z + NZ - j, NZ)).astype(jnp.float32) * (block * NX)
        total += jnp.exp(-after * dec) * part
        if j:
            before += jnp.where(z >= j, jnp.exp(-(block * NX * (j - 1)) * dec) * part, 0.0)
    h_y[0] = total
    sends_y = [remote(h_y.at[0], h_y.at[j], y_send.at[j], y_recv.at[j], to_y[j]) for j in range(1, NY)]
    for send in sends_y:
        send.start()
    for send in sends_y:
        send.wait_recv()
    came = jnp.zeros_like(dec)
    for j in range(1, NY + 1):
        came += jnp.exp(-(block * NX * NZ * (j - 1)) * dec) * h_y[j % NY]
    once = one_minus_exp(seq * dec)
    came = jnp.exp(-(z.astype(jnp.float32) * (block * NX)) * dec) * came + once * before
    inc[...] = jnp.where(x_hi == 0, came, lam1 * came + once * other)

    g_sends = [
        [
            remote(
                gb.at[g, pl.ds(pl.multiple_of(partner_tp[r] * out_toks, out_toks), out_toks)],
                gin.at[r - 1, g], g_send.at[r - 1, g], g_recv.at[r - 1, g], to_tp[r],
            )
            for r in range(1, NTP)
        ]
        for g in range(groups)
    ]
    for g in range(groups):
        start = []
        for m in range(modes):
            decs = wide(dec_t, g, m)
            state = jnp.where(row == 0, wide(inc, g, m), 0.0)
            state += shift_rows(ends[g, m] * one_minus_exp(seq * decs), 1, row)
            for by in (1, 2, 4):
                state += jnp.exp(-float(by * sub_len) * decs) * shift_rows(state, by, row)
            start.append(wide(wgt_t, g, m) * state)
        lam = [wide(lam_t, g, m) for m in range(modes)]
        gain = [wide(wc_t, g, m) for m in range(modes)]

        def step(t, states):
            x = xs[g, pl.ds(t, SUBS, stride=sub_len), :]
            states = tuple(l * u + c * x for l, u, c in zip(lam, states, gain))
            level = list(states)
            while len(level) > 1:
                level = [a + b for a, b in zip(level[::2], level[1::2])]
            ys[g, pl.ds(t, SUBS, stride=sub_len), :] = level[0]
            return states

        lax.fori_loop(0, sub_len, step, tuple(start), unroll=4)
        conv = ys[g].astype(jnp.bfloat16).astype(jnp.float32)
        gb[g] = (qs[g] * conv).astype(jnp.bfloat16)
        for send in (g_sends[g][1], g_sends[g][2], g_sends[g][0]):
            send.start()

    n_tile = 512

    def project(r, lhs_of, last):
        lhs = jnp.concatenate([lhs_of(g) for g in range(groups)], axis=1)

        def body(n, carry):
            at = pl.ds(pl.multiple_of(n * n_tile, n_tile), n_tile)
            part = jnp.dot(lhs, wf[r, :, at], preferred_element_type=jnp.float32)
            if r > 0:
                part += acc[:, at]
            if last:
                out_ref[:, at] = part.astype(jnp.bfloat16)
            else:
                acc[:, at] = part
            return carry

        lax.fori_loop(0, cols // n_tile, body, 0)

    loads[4].wait()
    own_rows = pl.ds(pl.multiple_of(tp * out_toks, out_toks), out_toks)
    project(0, lambda g: gb[g, own_rows, :], False)
    for p in w_order:
        w_cross[p].wait_recv()
        w_fwd[p].start()
    w_sib.wait_recv()
    for g in range(groups):
        g_sends[g][0].wait_recv()
    project(1, lambda g: gin[0, g], False)
    for g in range(groups):
        g_sends[g][1].wait_recv()
    project(2, lambda g: gin[1, g], False)
    for p in w_order:
        w_fwd[p].wait_recv()
    for g in range(groups):
        g_sends[g][2].wait_recv()
    project(3, lambda g: gin[2, g], True)

    w_sib.wait_send()
    send_x.wait_send()
    for send in sends_z + sends_y + w_cross + w_fwd:
        send.wait_send()
    for per_group in g_sends:
        for send in per_group:
            send.wait_send()


def shards(kv_product, query, decay_rate, residue, out_weight):
    chans, toks = kv_product.shape
    modes = decay_rate.shape[1]
    cols = out_weight.shape[1]
    groups = chans // LANES
    out_toks = toks // NTP
    bf16, f32 = jnp.bfloat16, jnp.float32
    small = (groups, modes, LANES)
    dma = pltpu.SemaphoreType.DMA
    return pl.pallas_call(
        kernel,
        out_shape=jax.ShapeDtypeStruct((out_toks, cols), bf16),
        in_specs=[pl.BlockSpec(memory_space=pl.ANY)] * 5,
        out_specs=pl.BlockSpec(memory_space=pltpu.VMEM),
        scratch_shapes=[
            pltpu.VMEM((chans, toks), bf16),
            pltpu.VMEM((chans, toks), bf16),
            pltpu.VMEM((chans, modes), f32),
            pltpu.VMEM((chans, modes), f32),
            pltpu.VMEM((NTP, chans, cols), bf16),
            pltpu.VMEM((groups, toks, LANES), f32),
            pltpu.VMEM((groups, toks, LANES), f32),
            pltpu.VMEM((groups, toks, LANES), f32),
            pltpu.VMEM(small, f32),
            pltpu.VMEM(small, f32),
            pltpu.VMEM(small, f32),
            pltpu.VMEM(small, f32),
            pltpu.VMEM((groups, modes, SUBS, LANES), f32),
            pltpu.VMEM(small, f32),
            pltpu.VMEM(small, f32),
            pltpu.VMEM((NZ,) + small, f32),
            pltpu.VMEM((NY,) + small, f32),
            pltpu.VMEM(small, f32),
            pltpu.VMEM((groups, toks, LANES), bf16),
            pltpu.VMEM((NTP - 1, groups, out_toks, LANES), bf16),
            pltpu.VMEM((out_toks, cols), f32),
            dma((5,)),
            dma((2,)),
            dma((NZ,)),
            dma((NZ,)),
            dma((NY,)),
            dma((NY,)),
            dma((2,)),
            dma((W_PIECES,)),
            dma((W_PIECES,)),
            dma((W_PIECES,)),
            dma((W_PIECES,)),
            dma((NTP - 1, groups)),
            dma((NTP - 1, groups)),
        ],
        compiler_params=pltpu.CompilerParams(
            collective_id=0, has_side_effects=True, vmem_limit_bytes=48 * 1024 * 1024
        ),
        cost_estimate=pl.CostEstimate(
            flops=2 * out_toks * cols * chans * NTP, bytes_accessed=6 * 1024 * 1024, transcendentals=0
        ),
    )(kv_product, query, decay_rate, residue, out_weight)


def solution(mesh):
    in_specs = (P("tp", "ctx"), P("tp", "ctx"), P("tp", None), P("tp", None), P("tp", None))
    out_specs = P(("ctx", "tp"), None)
    return jax.shard_map(shards, mesh=mesh, in_specs=in_specs, out_specs=out_specs, check_vma=False)
```

```python
import jax
import jax.numpy as jnp
from jax import lax
from jax.experimental import pallas as pl
from jax.experimental.pallas import tpu as pltpu
from jax.sharding import PartitionSpec as P

NY, NZ, NX, NTP = 4, 4, 2, 4
SUBS, LANES = 8, 128
W_IMPORT = ("wrap", "direct", "wrap", "direct", "wrap", "direct", "wrap", "wrap")
UNROLL = 16
MESH = pl.DeviceIdType.MESH


def one_minus_exp(z):
    series = jnp.ones_like(z)
    for n in range(10, 1, -1):
        series = 1.0 - (z * (1.0 / n)) * series
    return jnp.where(z < 0.5, z * series, 1.0 - jnp.exp(-z))


def shift_rows(value, by, row):
    return jnp.where(row >= by, pltpu.roll(value, by, 0), 0.0)


def tree_sum(terms):
    while len(terms) > 1:
        terms = [a + b for a, b in zip(terms[::2], terms[1::2])]
    return terms[0]


def kernel(
    kv_hbm, q_hbm, dec_hbm, res_hbm, w_hbm, out_ref,
    kv_v, q_v, dec_v, res_v, wf, xs, qs, ys, yn, dec_t, lam_t, wgt_t, wc_t, ends,
    s_own, s_x, g_z, h_y, inc, gb, gin, acc,
    loc_sem, x_sem, z_send, z_recv, y_send, y_recv,
    wsib_sem, wi_send, wi_recv, wn_send, wn_recv, wf_send, wf_recv, g_send, g_recv,
):
    chans, toks = kv_v.shape
    modes = dec_v.shape[0]
    groups = chans // LANES
    sub_len = toks // SUBS
    out_toks, cols = out_ref.shape
    seq = float(toks * NY * NZ * NX)

    ctx, tp = lax.axis_index("ctx"), lax.axis_index("tp")
    x_hi = lax.rem(ctx, NX)
    z = lax.rem(ctx // NX, NZ)
    y = ctx // (NX * NZ)
    x_lo, core = tp // 2, lax.rem(tp, 2)

    def ctx_of(yy, zz, xx):
        return (yy * NZ + zz) * NX + xx

    partner_tp = [tp, x_lo * 2 + (1 - core), (1 - x_lo) * 2 + core, (1 - x_lo) * 2 + (1 - core)]
    to_x = {"ctx": ctx_of(y, z, 1 - x_hi), "tp": tp}
    to_z = [{"ctx": ctx_of(y, lax.rem(z + j, NZ), x_hi), "tp": tp} for j in range(NZ)]
    to_y = [{"ctx": ctx_of(lax.rem(y + j, NY), z, x_hi), "tp": tp} for j in range(NY)]
    to_tp = [{"ctx": ctx, "tp": t} for t in partner_tp]
    to_wrap = {"ctx": ctx_of(y, z, 1 - x_hi), "tp": partner_tp[2]}

    loads = [
        pltpu.make_async_copy(kv_hbm, kv_v, loc_sem.at[0]),
        pltpu.make_async_copy(dec_hbm, dec_v, loc_sem.at[1]),
        pltpu.make_async_copy(res_hbm, res_v, loc_sem.at[2]),
        pltpu.make_async_copy(q_hbm, q_v, loc_sem.at[3]),
        pltpu.make_async_copy(w_hbm, wf.at[0], loc_sem.at[4]),
    ]
    for load in loads:
        load.start()

    barrier = pltpu.get_barrier_semaphore()
    partners = [to_x] + to_z[1:] + to_y[1:] + to_tp[1:] + [to_wrap]
    for partner in partners:
        pl.semaphore_signal(barrier, inc=1, device_id=partner, device_id_type=MESH)

    loads[1].wait()
    loads[2].wait()
    for g in range(groups):
        lanes = slice(g * LANES, (g + 1) * LANES)
        dec = dec_v[:, lanes]
        wgt = res_v[:, lanes] * jnp.sqrt(one_minus_exp(2.0 * dec))
        dec_t[g] = dec
        lam_t[g] = jnp.exp(-dec)
        wgt_t[g] = wgt
        wc_t[g] = wgt * one_minus_exp(seq * dec)

    def turn(src, dst, runs):
        for g in range(groups):
            for s in range(SUBS):
                turned = src[g * LANES:(g + 1) * LANES, s * sub_len:(s + 1) * sub_len].T.astype(jnp.float32)
                if runs:
                    dst[g, pl.ds(s, sub_len, stride=SUBS), :] = turned
                else:
                    dst[g, s * sub_len:(s + 1) * sub_len, :] = turned

    loads[0].wait()
    turn(kv_v, xs, True)

    pl.semaphore_wait(barrier, len(partners))

    def remote(src, dst, send, recv, to):
        return pltpu.make_async_remote_copy(
            src_ref=src, dst_ref=dst, send_sem=send, recv_sem=recv, device_id=to, device_id_type=MESH
        )

    half = chans // 2
    parity = lax.rem(y + z, 2)
    pieces = len(W_IMPORT)
    rows_in = half // pieces

    def rows_of(which, p):
        return pl.ds(pl.multiple_of(which * half + p * rows_in, rows_in), rows_in)

    around = [to_y[1], to_y[NY - 1], to_z[1], to_z[NZ - 1]]
    w_sib = remote(w_hbm, wf.at[1], wsib_sem.at[0], wsib_sem.at[1], to_tp[1])
    w_import, w_near, w_across = [], [], []
    for p in range(pieces):
        rows = rows_of(parity, p)
        to = to_wrap if W_IMPORT[p] == "wrap" else to_tp[2]
        w_import.append(remote(w_hbm.at[rows], wf.at[2, rows], wi_send.at[p], wi_recv.at[p], to))
        w_near.append(remote(wf.at[2, rows], wf.at[2, rows], wn_send.at[p], wn_recv.at[p], around[p % 4]))
        w_across.append(remote(wf.at[2, rows], wf.at[3, rows], wf_send.at[p], wf_recv.at[p], to_tp[1]))
    w_got = []
    for p in range(pieces):
        rows = rows_of(1 - parity, p)
        w_got.append(remote(wf.at[2, rows], wf.at[2, rows], wn_send.at[p], wn_recv.at[p], around[p % 4]))
        w_across.append(
            remote(wf.at[2, rows], wf.at[3, rows], wf_send.at[pieces + p], wf_recv.at[pieces + p], to_tp[1])
        )
    for copy in w_import:
        copy.start()
    w_sib.start()

    def hand_on(*which):
        for p in which:
            w_import[p].wait_recv()
            w_near[p].start()
            w_across[p].start()

    row = lax.broadcasted_iota(jnp.int32, (SUBS, LANES), 0)
    left = (SUBS - 1 - row).astype(jnp.float32) * float(sub_len)

    def wide(ref, g, m):
        return jnp.broadcast_to(ref[g, m:m + 1, :], (SUBS, LANES))

    def at(t):
        return pl.ds(pl.multiple_of(t * SUBS, SUBS), SUBS)

    zeros = tuple(jnp.zeros((SUBS, LANES), jnp.float32) for _ in range(modes))

    def first_pass(g, carry):
        lam = [wide(lam_t, g, m) for m in range(modes)]

        def step(t, states):
            x = xs[g, at(t), :]
            return tuple(l * u + x for l, u in zip(lam, states))

        states = lax.fori_loop(0, sub_len, step, zeros, unroll=UNROLL)
        for m in range(modes):
            ends[g, m] = states[m]
            decayed = states[m] * jnp.exp(-wide(dec_t, g, m) * left)
            s_own[g, m:m + 1, :] = jnp.sum(decayed, axis=0, keepdims=True)
        return carry

    lax.fori_loop(0, groups, first_pass, 0)

    def second_pass(g):
        lam = [wide(lam_t, g, m) for m in range(modes)]
        gain = [wide(wc_t, g, m) for m in range(modes)]

        def step(t, states):
            x = xs[g, at(t), :]
            states = tuple(l * u + x for l, u in zip(lam, states))
            ys[g, at(t), :] = tree_sum([c * u for c, u in zip(gain, states)])
            return states

        lax.fori_loop(0, sub_len, step, zeros, unroll=UNROLL)

    block = float(toks)
    send_x = remote(s_own, s_x, x_sem.at[0], x_sem.at[1], to_x)
    send_x.start()
    loads[3].wait()
    turn(q_v, qs, False)
    second_pass(0)
    hand_on(0, 1)
    second_pass(1)
    send_x.wait_recv()
    dec = dec_t[...]
    lam1 = jnp.exp(-block * dec)
    mine, other = s_own[...], s_x[...]
    g_z[0] = jnp.where(x_hi == 0, other + lam1 * mine, mine + lam1 * other)
    sends_z = [remote(g_z.at[0], g_z.at[j], z_send.at[j], z_recv.at[j], to_z[j]) for j in range(1, NZ)]
    for send in sends_z:
        send.start()
    hand_on(2, 3)
    second_pass(2)
    hand_on(4, 5)
    second_pass(3)
    for send in sends_z:
        send.wait_recv()
    total = jnp.zeros_like(dec)
    before = jnp.zeros_like(dec)
    for j in range(NZ):
        part = g_z[j]
        after = (NZ - 1 - lax.rem(z + NZ - j, NZ)).astype(jnp.float32) * (block * NX)
        total += jnp.exp(-after * dec) * part
        if j:
            before += jnp.where(z >= j, jnp.exp(-(block * NX * (j - 1)) * dec) * part, 0.0)
    h_y[0] = total
    sends_y = [remote(h_y.at[0], h_y.at[j], y_send.at[j], y_recv.at[j], to_y[j]) for j in range(1, NY)]
    for send in sends_y:
        send.start()
    hand_on(6, 7)
    for send in sends_y:
        send.wait_recv()
    came = jnp.zeros_like(dec)
    for j in range(1, NY + 1):
        came += jnp.exp(-(block * NX * NZ * (j - 1)) * dec) * h_y[j % NY]
    once = one_minus_exp(seq * dec)
    came = jnp.exp(-(z.astype(jnp.float32) * (block * NX)) * dec) * came + once * before
    inc[...] = jnp.where(x_hi == 0, came, lam1 * came + once * other)

    g_sends = [
        [
            remote(
                gb.at[g, pl.ds(pl.multiple_of(partner_tp[r] * out_toks, out_toks), out_toks)],
                gin.at[r - 1, g], g_send.at[r - 1, g], g_recv.at[r - 1, g], to_tp[r],
            )
            for r in range(1, NTP)
        ]
        for g in range(groups)
    ]
    for g in range(groups):
        start = []
        for m in range(modes):
            decs = wide(dec_t, g, m)
            state = jnp.where(row == 0, wide(inc, g, m), 0.0)
            state += shift_rows(ends[g, m] * one_minus_exp(seq * decs), 1, row)
            for by in (1, 2, 4):
                state += jnp.exp(-float(by * sub_len) * decs) * shift_rows(state, by, row)
            start.append(wide(wgt_t, g, m) * state)
        lam = [wide(lam_t, g, m) for m in range(modes)]

        def step(t, states):
            states = tuple(l * u for l, u in zip(lam, states))
            yn[g, pl.ds(t, SUBS, stride=sub_len), :] = ys[g, at(t), :] + tree_sum(list(states))
            return states

        lax.fori_loop(0, sub_len, step, tuple(start), unroll=UNROLL)
        conv = yn[g].astype(jnp.bfloat16).astype(jnp.float32)
        gb[g] = (qs[g] * conv).astype(jnp.bfloat16)
        for send in (g_sends[g][1], g_sends[g][2], g_sends[g][0]):
            send.start()

    for p in range(pieces):
        w_got[p].wait_recv()
        w_across[pieces + p].start()

    own_rows = pl.ds(pl.multiple_of(tp * out_toks, out_toks), out_toks)
    loads[4].wait()
    w_sib.wait_recv()
    for g in range(groups):
        g_sends[g][0].wait_recv()
    lhs = jnp.concatenate(
        [gb[g, own_rows, :] for g in range(groups)] + [gin[0, g] for g in range(groups)], axis=1
    )
    acc[...] = jnp.dot(
        lhs, jnp.concatenate([wf[0], wf[1]], axis=0), preferred_element_type=jnp.float32
    )
    for copy in w_across:
        copy.wait_recv()
    for g in range(groups):
        rows = slice(g * LANES, (g + 1) * LANES)
        g_sends[g][1].wait_recv()
        g_sends[g][2].wait_recv()
        lhs = jnp.concatenate([gin[1, g], gin[2, g]], axis=1)
        rhs = jnp.concatenate([wf[2, rows, :], wf[3, rows, :]], axis=0)
        part = acc[...] + jnp.dot(lhs, rhs, preferred_element_type=jnp.float32)
        if g == groups - 1:
            out_ref[...] = part.astype(jnp.bfloat16)
        else:
            acc[...] = part

    for copy in [w_sib, send_x] + sends_z + sends_y + w_import + w_near + w_across:
        copy.wait_send()
    for per_group in g_sends:
        for send in per_group:
            send.wait_send()


def shards(kv_product, query, decay_rate, residue, out_weight):
    chans, toks = kv_product.shape
    modes = decay_rate.shape[1]
    cols = out_weight.shape[1]
    groups = chans // LANES
    out_toks = toks // NTP
    pieces = len(W_IMPORT)
    bf16, f32 = jnp.bfloat16, jnp.float32
    small = (groups, modes, LANES)
    dma = pltpu.SemaphoreType.DMA
    return pl.pallas_call(
        kernel,
        out_shape=jax.ShapeDtypeStruct((out_toks, cols), bf16),
        in_specs=[pl.BlockSpec(memory_space=pltpu.HBM)] * 5,
        out_specs=pl.BlockSpec(memory_space=pltpu.VMEM),
        scratch_shapes=[
            pltpu.VMEM((chans, toks), bf16),
            pltpu.VMEM((chans, toks), bf16),
            pltpu.VMEM((modes, chans), f32),
            pltpu.VMEM((modes, chans), f32),
            pltpu.VMEM((NTP, chans, cols), bf16),
            pltpu.VMEM((groups, toks, LANES), f32),
            pltpu.VMEM((groups, toks, LANES), f32),
            pltpu.VMEM((groups, toks, LANES), f32),
            pltpu.VMEM((groups, toks, LANES), f32),
            pltpu.VMEM(small, f32),
            pltpu.VMEM(small, f32),
            pltpu.VMEM(small, f32),
            pltpu.VMEM(small, f32),
            pltpu.VMEM((groups, modes, SUBS, LANES), f32),
            pltpu.VMEM(small, f32),
            pltpu.VMEM(small, f32),
            pltpu.VMEM((NZ,) + small, f32),
            pltpu.VMEM((NY,) + small, f32),
            pltpu.VMEM(small, f32),
            pltpu.VMEM((groups, toks, LANES), bf16),
            pltpu.VMEM((NTP - 1, groups, out_toks, LANES), bf16),
            pltpu.VMEM((out_toks, cols), f32),
            dma((5,)),
            dma((2,)),
            dma((NZ,)),
            dma((NZ,)),
            dma((NY,)),
            dma((NY,)),
            dma((2,)),
            dma((pieces,)),
            dma((pieces,)),
            dma((pieces,)),
            dma((pieces,)),
            dma((2 * pieces,)),
            dma((2 * pieces,)),
            dma((NTP - 1, groups)),
            dma((NTP - 1, groups)),
        ],
        compiler_params=pltpu.CompilerParams(
            collective_id=0, has_side_effects=True, vmem_limit_bytes=52 * 1024 * 1024
        ),
        cost_estimate=pl.CostEstimate(
            flops=2 * out_toks * cols * chans * NTP, bytes_accessed=6 * 1024 * 1024, transcendentals=0
        ),
    )(kv_product, query, decay_rate.T, residue.T, out_weight)


def solution(mesh):
    in_specs = (P("tp", "ctx"), P("tp", "ctx"), P("tp", None), P("tp", None), P("tp", None))
    out_specs = P(("ctx", "tp"), None)
    return jax.shard_map(shards, mesh=mesh, in_specs=in_specs, out_specs=out_specs, check_vma=False)
```

```python
import jax
import jax.numpy as jnp
from jax import lax
from jax.experimental import pallas as pl
from jax.experimental.pallas import tpu as pltpu
from jax.sharding import PartitionSpec as P

NY, NZ, NX, NTP = 4, 4, 2, 4
SUBS, LANES = 8, 128
W_PIECES = (
    ("near", 2), ("wrap", 3), ("near", 2), ("wrap", 3), ("near", 0), ("wrap", 1), ("wrap", 0), ("wrap", 1),
)
UNROLL = 16
MESH = pl.DeviceIdType.MESH


def one_minus_exp(z):
    series = jnp.ones_like(z)
    for n in range(10, 1, -1):
        series = 1.0 - (z * (1.0 / n)) * series
    return jnp.where(z < 0.5, z * series, 1.0 - jnp.exp(-z))


def shift_rows(value, by, row):
    return jnp.where(row >= by, pltpu.roll(value, by, 0), 0.0)


def tree_sum(terms):
    while len(terms) > 1:
        terms = [a + b for a, b in zip(terms[::2], terms[1::2])]
    return terms[0]


def kernel(
    kv_hbm, q_hbm, dec_hbm, res_hbm, w_hbm, out_ref,
    kv_v, q_v, dec_v, res_v, wf, xs, qs, ys, yn, dec_t, lam_t, wgt_t, wc_t, ends,
    s_own, s_x, g_z, h_y, inc, gb, gin, acc,
    loc_sem, x_sem, z_send, z_recv, y_send, y_recv,
    wsib_sem, wi_send, wi_recv, wn_send, wn_recv, wf_send, wf_recv, g_send, g_recv,
):
    chans, toks = kv_v.shape
    modes = dec_v.shape[0]
    groups = chans // LANES
    sub_len = toks // SUBS
    out_toks, cols = out_ref.shape
    seq = float(toks * NY * NZ * NX)

    ctx, tp = lax.axis_index("ctx"), lax.axis_index("tp")
    x_hi = lax.rem(ctx, NX)
    z = lax.rem(ctx // NX, NZ)
    y = ctx // (NX * NZ)
    x_lo, core = tp // 2, lax.rem(tp, 2)

    def ctx_of(yy, zz, xx):
        return (yy * NZ + zz) * NX + xx

    partner_tp = [tp, x_lo * 2 + (1 - core), (1 - x_lo) * 2 + core, (1 - x_lo) * 2 + (1 - core)]
    to_x = {"ctx": ctx_of(y, z, 1 - x_hi), "tp": tp}
    to_z = [{"ctx": ctx_of(y, lax.rem(z + j, NZ), x_hi), "tp": tp} for j in range(NZ)]
    to_y = [{"ctx": ctx_of(lax.rem(y + j, NY), z, x_hi), "tp": tp} for j in range(NY)]
    to_tp = [{"ctx": ctx, "tp": t} for t in partner_tp]
    to_wrap = {"ctx": ctx_of(y, z, 1 - x_hi), "tp": partner_tp[2]}

    loads = [
        pltpu.make_async_copy(kv_hbm, kv_v, loc_sem.at[0]),
        pltpu.make_async_copy(dec_hbm, dec_v, loc_sem.at[1]),
        pltpu.make_async_copy(res_hbm, res_v, loc_sem.at[2]),
        pltpu.make_async_copy(q_hbm, q_v, loc_sem.at[3]),
        pltpu.make_async_copy(w_hbm, wf.at[0], loc_sem.at[4]),
    ]
    for load in loads:
        load.start()

    barrier = pltpu.get_barrier_semaphore()
    partners = [to_x] + to_z[1:] + to_y[1:] + to_tp[1:] + [to_wrap]
    for partner in partners:
        pl.semaphore_signal(barrier, inc=1, device_id=partner, device_id_type=MESH)

    loads[1].wait()
    loads[2].wait()
    for g in range(groups):
        lanes = slice(g * LANES, (g + 1) * LANES)
        dec = dec_v[:, lanes]
        wgt = res_v[:, lanes] * jnp.sqrt(one_minus_exp(2.0 * dec))
        dec_t[g] = dec
        lam_t[g] = jnp.exp(-dec)
        wgt_t[g] = wgt
        wc_t[g] = wgt * one_minus_exp(seq * dec)

    def turn(src, dst, runs):
        for g in range(groups):
            for s in range(SUBS):
                turned = src[g * LANES:(g + 1) * LANES, s * sub_len:(s + 1) * sub_len].T.astype(jnp.float32)
                if runs:
                    dst[g, pl.ds(s, sub_len, stride=SUBS), :] = turned
                else:
                    dst[g, s * sub_len:(s + 1) * sub_len, :] = turned

    loads[0].wait()
    turn(kv_v, xs, True)

    pl.semaphore_wait(barrier, len(partners))

    def remote(src, dst, send, recv, to):
        return pltpu.make_async_remote_copy(
            src_ref=src, dst_ref=dst, send_sem=send, recv_sem=recv, device_id=to, device_id_type=MESH
        )

    half = chans // 2
    parity = lax.rem(y + z, 2)
    pieces = len(W_PIECES)
    rows_in = half // pieces

    def rows_of(which, p):
        return pl.ds(pl.multiple_of(which * half + p * rows_in, rows_in), rows_in)

    around = [to_y[1], to_y[NY - 1], to_z[1], to_z[NZ - 1]]
    w_sib = remote(w_hbm, wf.at[1], wsib_sem.at[0], wsib_sem.at[1], to_tp[1])
    w_import, w_near, w_across = [], [], []
    for p in range(pieces):
        rows = rows_of(parity, p)
        to = to_wrap if W_PIECES[p][0] == "wrap" else to_tp[2]
        onward = around[W_PIECES[p][1]]
        w_import.append(remote(w_hbm.at[rows], wf.at[2, rows], wi_send.at[p], wi_recv.at[p], to))
        w_near.append(remote(wf.at[2, rows], wf.at[2, rows], wn_send.at[p], wn_recv.at[p], onward))
        w_across.append(remote(wf.at[2, rows], wf.at[3, rows], wf_send.at[p], wf_recv.at[p], to_tp[1]))
    w_got = []
    for p in range(pieces):
        rows = rows_of(1 - parity, p)
        w_got.append(remote(wf.at[2, rows], wf.at[2, rows], wn_send.at[p], wn_recv.at[p], onward))
        w_across.append(
            remote(wf.at[2, rows], wf.at[3, rows], wf_send.at[pieces + p], wf_recv.at[pieces + p], to_tp[1])
        )
    for copy in w_import[:2]:
        copy.start()
    w_sib.start()

    def hand_on(*which):
        for p in which:
            w_import[p].wait_recv()
            w_near[p].start()
            w_across[p].start()

    row = lax.broadcasted_iota(jnp.int32, (SUBS, LANES), 0)
    left = (SUBS - 1 - row).astype(jnp.float32) * float(sub_len)

    def wide(ref, g, m):
        return jnp.broadcast_to(ref[g, m:m + 1, :], (SUBS, LANES))

    def at(t):
        return pl.ds(pl.multiple_of(t * SUBS, SUBS), SUBS)

    zeros = tuple(jnp.zeros((SUBS, LANES), jnp.float32) for _ in range(modes))

    def first_pass(g, carry):
        lam = [wide(lam_t, g, m) for m in range(modes)]

        def step(t, states):
            x = xs[g, at(t), :]
            return tuple(l * u + x for l, u in zip(lam, states))

        states = lax.fori_loop(0, sub_len, step, zeros, unroll=UNROLL)
        for m in range(modes):
            ends[g, m] = states[m]
            decayed = states[m] * jnp.exp(-wide(dec_t, g, m) * left)
            s_own[g, m:m + 1, :] = jnp.sum(decayed, axis=0, keepdims=True)
        return carry

    lax.fori_loop(0, groups, first_pass, 0)

    def second_pass(g):
        lam = [wide(lam_t, g, m) for m in range(modes)]
        gain = [wide(wc_t, g, m) for m in range(modes)]

        def step(t, states):
            x = xs[g, at(t), :]
            states = tuple(l * u + x for l, u in zip(lam, states))
            ys[g, at(t), :] = tree_sum([c * u for c, u in zip(gain, states)])
            return states

        lax.fori_loop(0, sub_len, step, zeros, unroll=UNROLL)

    block = float(toks)
    send_x = remote(s_own, s_x, x_sem.at[0], x_sem.at[1], to_x)
    send_x.start()
    for copy in w_import[2:]:
        copy.start()
    loads[3].wait()
    turn(q_v, qs, False)
    second_pass(0)
    second_pass(1)
    send_x.wait_recv()
    dec = dec_t[...]
    lam1 = jnp.exp(-block * dec)
    mine, other = s_own[...], s_x[...]
    g_z[0] = jnp.where(x_hi == 0, other + lam1 * mine, mine + lam1 * other)
    sends_z = [remote(g_z.at[0], g_z.at[j], z_send.at[j], z_recv.at[j], to_z[j]) for j in range(1, NZ)]
    for send in sends_z:
        send.start()
    hand_on(0, 1)
    second_pass(2)
    second_pass(3)
    hand_on(2, 3)
    for send in sends_z:
        send.wait_recv()
    total = jnp.zeros_like(dec)
    before = jnp.zeros_like(dec)
    for j in range(NZ):
        part = g_z[j]
        after = (NZ - 1 - lax.rem(z + NZ - j, NZ)).astype(jnp.float32) * (block * NX)
        total += jnp.exp(-after * dec) * part
        if j:
            before += jnp.where(z >= j, jnp.exp(-(block * NX * (j - 1)) * dec) * part, 0.0)
    h_y[0] = total
    sends_y = [remote(h_y.at[0], h_y.at[j], y_send.at[j], y_recv.at[j], to_y[j]) for j in range(1, NY)]
    for send in sends_y:
        send.start()
    for send in sends_y:
        send.wait_recv()
    came = jnp.zeros_like(dec)
    for j in range(1, NY + 1):
        came += jnp.exp(-(block * NX * NZ * (j - 1)) * dec) * h_y[j % NY]
    once = one_minus_exp(seq * dec)
    came = jnp.exp(-(z.astype(jnp.float32) * (block * NX)) * dec) * came + once * before
    inc[...] = jnp.where(x_hi == 0, came, lam1 * came + once * other)

    g_sends = [
        [
            remote(
                gb.at[g, pl.ds(pl.multiple_of(partner_tp[r] * out_toks, out_toks), out_toks)],
                gin.at[r - 1, g], g_send.at[r - 1, g], g_recv.at[r - 1, g], to_tp[r],
            )
            for r in range(1, NTP)
        ]
        for g in range(groups)
    ]
    for g in range(groups):
        start = []
        for m in range(modes):
            decs = wide(dec_t, g, m)
            state = jnp.where(row == 0, wide(inc, g, m), 0.0)
            state += shift_rows(ends[g, m] * one_minus_exp(seq * decs), 1, row)
            for by in (1, 2, 4):
                state += jnp.exp(-float(by * sub_len) * decs) * shift_rows(state, by, row)
            start.append(wide(wgt_t, g, m) * state)
        lam = [wide(lam_t, g, m) for m in range(modes)]

        def step(t, states):
            states = tuple(l * u for l, u in zip(lam, states))
            yn[g, pl.ds(t, SUBS, stride=sub_len), :] = ys[g, at(t), :] + tree_sum(list(states))
            return states

        lax.fori_loop(0, sub_len, step, tuple(start), unroll=UNROLL)
        conv = yn[g].astype(jnp.bfloat16).astype(jnp.float32)
        gb[g] = (qs[g] * conv).astype(jnp.bfloat16)
        for send in (g_sends[g][1], g_sends[g][2], g_sends[g][0]):
            send.start()
        hand_on(*((4, 5), (), (6,), (7,))[g])

    for p in range(pieces):
        w_got[p].wait_recv()
        w_across[pieces + p].start()

    own_rows = pl.ds(pl.multiple_of(tp * out_toks, out_toks), out_toks)
    loads[4].wait()
    w_sib.wait_recv()
    for g in range(groups):
        g_sends[g][0].wait_recv()
    lhs = jnp.concatenate(
        [gb[g, own_rows, :] for g in range(groups)] + [gin[0, g] for g in range(groups)], axis=1
    )
    acc[...] = jnp.dot(
        lhs, jnp.concatenate([wf[0], wf[1]], axis=0), preferred_element_type=jnp.float32
    )
    for copy in w_across:
        copy.wait_recv()
    for g in range(groups):
        rows = slice(g * LANES, (g + 1) * LANES)
        g_sends[g][1].wait_recv()
        g_sends[g][2].wait_recv()
        lhs = jnp.concatenate([gin[1, g], gin[2, g]], axis=1)
        rhs = jnp.concatenate([wf[2, rows, :], wf[3, rows, :]], axis=0)
        part = acc[...] + jnp.dot(lhs, rhs, preferred_element_type=jnp.float32)
        if g == groups - 1:
            out_ref[...] = part.astype(jnp.bfloat16)
        else:
            acc[...] = part

    for copy in [w_sib, send_x] + sends_z + sends_y + w_import + w_near + w_across:
        copy.wait_send()
    for per_group in g_sends:
        for send in per_group:
            send.wait_send()


def shards(kv_product, query, decay_rate, residue, out_weight):
    chans, toks = kv_product.shape
    modes = decay_rate.shape[1]
    cols = out_weight.shape[1]
    groups = chans // LANES
    out_toks = toks // NTP
    pieces = len(W_PIECES)
    bf16, f32 = jnp.bfloat16, jnp.float32
    small = (groups, modes, LANES)
    dma = pltpu.SemaphoreType.DMA
    operands = (kv_product, query, decay_rate.T, residue.T, out_weight)
    return pl.pallas_call(
        kernel,
        out_shape=jax.ShapeDtypeStruct((out_toks, cols), bf16),
        in_specs=[pl.BlockSpec(memory_space=pltpu.HBM)] * 5,
        out_specs=pl.BlockSpec(memory_space=pltpu.VMEM),
        scratch_shapes=[
            pltpu.VMEM((chans, toks), bf16),
            pltpu.VMEM((chans, toks), bf16),
            pltpu.VMEM((modes, chans), f32),
            pltpu.VMEM((modes, chans), f32),
            pltpu.VMEM((NTP, chans, cols), bf16),
            pltpu.VMEM((groups, toks, LANES), f32),
            pltpu.VMEM((groups, toks, LANES), f32),
            pltpu.VMEM((groups, toks, LANES), f32),
            pltpu.VMEM((groups, toks, LANES), f32),
            pltpu.VMEM(small, f32),
            pltpu.VMEM(small, f32),
            pltpu.VMEM(small, f32),
            pltpu.VMEM(small, f32),
            pltpu.VMEM((groups, modes, SUBS, LANES), f32),
            pltpu.VMEM(small, f32),
            pltpu.VMEM(small, f32),
            pltpu.VMEM((NZ,) + small, f32),
            pltpu.VMEM((NY,) + small, f32),
            pltpu.VMEM(small, f32),
            pltpu.VMEM((groups, toks, LANES), bf16),
            pltpu.VMEM((NTP - 1, groups, out_toks, LANES), bf16),
            pltpu.VMEM((out_toks, cols), f32),
            dma((5,)),
            dma((2,)),
            dma((NZ,)),
            dma((NZ,)),
            dma((NY,)),
            dma((NY,)),
            dma((2,)),
            dma((pieces,)),
            dma((pieces,)),
            dma((pieces,)),
            dma((pieces,)),
            dma((2 * pieces,)),
            dma((2 * pieces,)),
            dma((NTP - 1, groups)),
            dma((NTP - 1, groups)),
        ],
        compiler_params=pltpu.CompilerParams(
            collective_id=0, has_side_effects=True, vmem_limit_bytes=52 * 1024 * 1024
        ),
        cost_estimate=pl.CostEstimate(
            flops=2 * out_toks * cols * chans * NTP, bytes_accessed=6 * 1024 * 1024, transcendentals=0
        ),
    )(*(pltpu.with_memory_space_constraint(a, pltpu.HBM) for a in operands))


def solution(mesh):
    in_specs = (P("tp", "ctx"), P("tp", "ctx"), P("tp", None), P("tp", None), P("tp", None))
    out_specs = P(("ctx", "tp"), None)
    return jax.shard_map(shards, mesh=mesh, in_specs=in_specs, out_specs=out_specs, check_vma=False)
```

```python
import jax
import jax.numpy as jnp
from jax import lax
from jax.experimental import pallas as pl
from jax.experimental.pallas import tpu as pltpu
from jax.sharding import PartitionSpec as P

NY, NZ, NX, NTP = 4, 4, 2, 4
SUBS, LANES = 8, 128
W_ROWS = (32, 48, 32, 16)
UNROLL = 16
MESH = pl.DeviceIdType.MESH


def one_minus_exp(z):
    series = jnp.ones_like(z)
    for n in range(10, 1, -1):
        series = 1.0 - (z * (1.0 / n)) * series
    return jnp.where(z < 0.5, z * series, 1.0 - jnp.exp(-z))


def shift_rows(value, by, row):
    return jnp.where(row >= by, pltpu.roll(value, by, 0), 0.0)


def tree_sum(terms):
    while len(terms) > 1:
        terms = [a + b for a, b in zip(terms[::2], terms[1::2])]
    return terms[0]


def at(t):
    return pl.ds(pl.multiple_of(t * SUBS, SUBS), SUBS)


def kernel(
    kv_hbm, q_hbm, dec_hbm, res_hbm, w_hbm, out_ref,
    kv_v, q_v, dec_v, res_v, kv_far, q_far, dec_far, res_far, wf,
    xs, qs, ys, yn, dec_t, lam_t, wgt_t, wc_t, ends, loc, pw,
    s_all, h_y, inc, t_rows, t_out, t_in,
    xd, qd, yd, ynd, dec_d, lam_d, wgt_d, wc_d, loc_d, pw_d,
    gb, gin, gd, acc,
    loc_sem, s_send, s_recv, y_send, y_recv, far_send, far_recv, t_send, t_recv,
    wsib_sem, wi_send, wi_recv, wn_send, wn_recv, wa_send, wa_recv, g_send, g_recv,
):
    chans, toks = kv_v.shape
    modes = dec_v.shape[0]
    groups = chans // LANES
    near_groups = groups // 2
    far_chans = chans // 2
    far_groups = groups - near_groups
    sub_len = toks // SUBS
    out_toks, cols = out_ref.shape
    far_len = out_toks // SUBS
    seq = float(toks * NY * NZ * NX)
    block = float(toks)
    f32, bf16 = jnp.float32, jnp.bfloat16

    ctx, tp = lax.axis_index("ctx"), lax.axis_index("tp")
    x_hi = lax.rem(ctx, NX)
    z = lax.rem(ctx // NX, NZ)
    y = ctx // (NX * NZ)
    x_lo, core = tp // 2, lax.rem(tp, 2)

    def ctx_of(yy, zz, xx):
        return (yy * NZ + zz) * NX + xx

    partner_tp = [tp, x_lo * 2 + (1 - core), (1 - x_lo) * 2 + core, (1 - x_lo) * 2 + (1 - core)]
    to_plane = [
        [{"ctx": ctx_of(y, lax.rem(z + j, NZ), xx), "tp": tp} for xx in (x_hi, 1 - x_hi)] for j in range(NZ)
    ]
    to_y = [{"ctx": ctx_of(lax.rem(y + j, NY), z, x_hi), "tp": tp} for j in range(NY)]
    to_tp = [{"ctx": ctx, "tp": t} for t in partner_tp]
    to_wrap = {"ctx": ctx_of(y, z, 1 - x_hi), "tp": partner_tp[2]}
    plane = [(j, k) for j in range(NZ) for k in range(NX) if j or k]

    loads = [
        pltpu.make_async_copy(kv_hbm, kv_v, loc_sem.at[0]),
        pltpu.make_async_copy(dec_hbm, dec_v, loc_sem.at[1]),
        pltpu.make_async_copy(res_hbm, res_v, loc_sem.at[2]),
        pltpu.make_async_copy(q_hbm, q_v, loc_sem.at[3]),
        pltpu.make_async_copy(w_hbm, wf.at[0], loc_sem.at[4]),
    ]
    for load in loads:
        load.start()

    barrier = pltpu.get_barrier_semaphore()
    partners = [to_plane[j][k] for j, k in plane] + to_y[1:] + to_tp[1:] + [to_wrap]
    for partner in partners:
        pl.semaphore_signal(barrier, inc=1, device_id=partner, device_id_type=MESH)

    def remote(src, dst, send, recv, to):
        return pltpu.make_async_remote_copy(
            src_ref=src, dst_ref=dst, send_sem=send, recv_sem=recv, device_id=to, device_id_type=MESH
        )

    far_rows, far_cols = pl.ds(far_chans, far_chans), pl.ds(near_groups * LANES, far_chans)
    far = []
    for r in range(1, NTP):
        there = pl.ds(pl.multiple_of(partner_tp[r] * out_toks, out_toks), out_toks)
        pairs = (
            (kv_hbm.at[far_rows, there], kv_far), (q_hbm.at[far_rows, there], q_far),
            (dec_hbm.at[:, far_cols], dec_far), (res_hbm.at[:, far_cols], res_far),
        )
        far.append(
            [
                remote(src, dst.at[r - 1], far_send.at[r - 1, i], far_recv.at[r - 1, i], to_tp[r])
                for i, (src, dst) in enumerate(pairs)
            ]
        )

    quarter = chans // 4
    mine = lax.rem(z + 2 * y, 4)

    def rows_of(which, i):
        return pl.ds(pl.multiple_of(which * quarter + sum(W_ROWS[:i]), 16), W_ROWS[i])

    w_sib = remote(w_hbm, wf.at[1], wsib_sem.at[0], wsib_sem.at[1], to_tp[1])
    w_import, w_on, w_got, w_across = [], [], [], []
    for i in range(len(W_ROWS)):
        rows = rows_of(mine, i)
        w_import.append(remote(w_hbm.at[rows], wf.at[2, rows], wi_send.at[i], wi_recv.at[i], to_wrap))
        ways = (to_plane[1][0], to_plane[NZ - 1][0], to_y[1] if i % 2 == 0 else to_y[NY - 1])
        w_on.append([])
        w_got.append([])
        w_across.append([remote(wf.at[2, rows], wf.at[3, rows], wa_send.at[3, i], wa_recv.at[3, i], to_tp[1])])
        for way, (to, theirs) in enumerate(zip(ways, (lax.rem(mine + 3, 4), lax.rem(mine + 1, 4), lax.rem(mine + 2, 4)))):
            rows = rows_of(mine, i)
            w_on[i].append(remote(wf.at[2, rows], wf.at[2, rows], wn_send.at[way, i], wn_recv.at[way, i], to))
            rows = rows_of(theirs, i)
            w_got[i].append(remote(wf.at[2, rows], wf.at[2, rows], wn_send.at[way, i], wn_recv.at[way, i], to))
            w_across[i].append(
                remote(wf.at[2, rows], wf.at[3, rows], wa_send.at[way, i], wa_recv.at[way, i], to_tp[1])
            )

    def hand_on(i):
        w_import[i].wait_recv()
        w_on[i][0].start()
        w_on[i][1].start()
        w_across[i][0].start()

    def hand_across(i, *ways):
        for way in ways:
            w_got[i][way].wait_recv()
            w_across[i][1 + way].start()

    def coefficients(dec, res, dec_to, lam_to, wgt_to, wc_to, *where):
        wgt = res * jnp.sqrt(one_minus_exp(2.0 * dec))
        dec_to[where] = dec
        lam_to[where] = jnp.exp(-dec)
        wgt_to[where] = wgt
        wc_to[where] = wgt * one_minus_exp(seq * dec)

    loads[1].wait()
    loads[2].wait()
    for g in range(groups):
        lanes = slice(g * LANES, (g + 1) * LANES)
        coefficients(dec_v[:, lanes], res_v[:, lanes], dec_t, lam_t, wgt_t, wc_t, g)

    loads[0].wait()
    for g in range(groups):
        for s in range(SUBS):
            turned = kv_v[g * LANES:(g + 1) * LANES, s * sub_len:(s + 1) * sub_len].T.astype(f32)
            xs[g, pl.ds(s, sub_len, stride=SUBS), :] = turned

    pl.semaphore_wait(barrier, len(partners))
    w_import[0].start()
    far[1][0].start()
    for copy in far[0]:
        copy.start()
    w_sib.start()

    row = lax.broadcasted_iota(jnp.int32, (SUBS, LANES), 0)
    row_f = row.astype(f32)

    def wide(ref, *where):
        *lead, m = where
        return jnp.broadcast_to(ref[(*lead, slice(m, m + 1), slice(None))], (SUBS, LANES))

    zeros = tuple(jnp.zeros((SUBS, LANES), f32) for _ in range(modes))

    def first_pass(g, carry):
        lam = [wide(lam_t, g, m) for m in range(modes)]

        def step(t, states):
            x = xs[g, at(t), :]
            return tuple(l * u + x for l, u in zip(lam, states))

        states = lax.fori_loop(0, sub_len, step, zeros, unroll=UNROLL)
        for m in range(modes):
            ends[g, m] = states[m]
            decayed = states[m] * jnp.exp(-wide(dec_t, g, m) * ((SUBS - 1 - row_f) * float(sub_len)))
            s_all[0, 0, g, m:m + 1, :] = jnp.sum(decayed, axis=0, keepdims=True)
        return carry

    lax.fori_loop(0, groups, first_pass, 0)

    sends_s = [
        remote(
            s_all.at[0, 0], s_all.at[j, k], s_send.at[j, k], s_recv.at[j, k], to_plane[j][k]
        )
        for j, k in plane
    ]
    for send in sends_s:
        send.start()
    for r in (1, 2):
        far[r][2].start()
        far[r][3].start()
    far[2][0].start()
    far[1][1].start()
    far[2][1].start()
    for copy in w_import[1:]:
        copy.start()

    def run_starts(states, decs, length):
        state = shift_rows(states * one_minus_exp(seq * decs), 1, row)
        for by in (1, 2, 4):
            state += jnp.exp(-float(by * length) * decs) * shift_rows(state, by, row)
        return state, jnp.exp(-(row_f * float(length)) * decs)

    def prepare(g, carry):
        for m in range(modes):
            loc[g, m], pw[g, m] = run_starts(ends[g, m], wide(dec_t, g, m), sub_len)
        return carry

    def second_pass(g):
        lam = [wide(lam_t, g, m) for m in range(modes)]
        gain = [wide(wc_t, g, m) for m in range(modes)]

        def step(t, states):
            x = xs[g, at(t), :]
            states = tuple(l * u + x for l, u in zip(lam, states))
            ys[g, at(t), :] = tree_sum([c * u for c, u in zip(gain, states)])
            return states

        lax.fori_loop(0, sub_len, step, zeros, unroll=UNROLL)

    own_toks = pl.ds(pl.multiple_of(tp * out_toks, out_toks), out_toks)

    def far_pass(r):
        if r:
            for i in (0, 2, 3):
                far[r - 1][i].wait_recv()
        halves = out_toks // LANES
        for g in range(far_groups):
            lanes = slice(g * LANES, (g + 1) * LANES)
            if r:
                dec, res = dec_far[r - 1, :, lanes], res_far[r - 1, :, lanes]
            else:
                own = slice(far_chans + g * LANES, far_chans + (g + 1) * LANES)
                dec, res = dec_v[:, own], res_v[:, own]
            coefficients(dec, res, dec_d, lam_d, wgt_d, wc_d, r, g)
            for h in range(halves):
                if r:
                    tile = kv_far[r - 1, lanes, h * LANES:(h + 1) * LANES]
                else:
                    tile = kv_v[own, pl.ds(pl.multiple_of(tp * out_toks + h * LANES, LANES), LANES)]
                turned = tile.T.astype(f32)
                for s in range(SUBS // halves):
                    xd[r, g, pl.ds(h * (SUBS // halves) + s, far_len, stride=SUBS), :] = (
                        turned[s * far_len:(s + 1) * far_len]
                    )

        def of_group(g, carry):
            lam = [wide(lam_d, r, g, m) for m in range(modes)]
            gain = [wide(wc_d, r, g, m) for m in range(modes)]

            def step(t, states):
                x = xd[r, g, at(t), :]
                states = tuple(l * u + x for l, u in zip(lam, states))
                yd[r, g, at(t), :] = tree_sum([c * u for c, u in zip(gain, states)])
                return states

            states = lax.fori_loop(0, far_len, step, zeros, unroll=UNROLL)
            for m in range(modes):
                loc_d[r, g, m], pw_d[r, g, m] = run_starts(states[m], wide(dec_d, r, g, m), far_len)
            return carry

        lax.fori_loop(0, far_groups, of_group, 0)

    def turn_query(r):
        for g in range(far_groups):
            for h in range(out_toks // LANES):
                if r:
                    tile = q_far[r - 1, g * LANES:(g + 1) * LANES, h * LANES:(h + 1) * LANES]
                else:
                    own = slice(far_chans + g * LANES, far_chans + (g + 1) * LANES)
                    tile = q_v[own, pl.ds(pl.multiple_of(tp * out_toks + h * LANES, LANES), LANES)]
                qd[r, g, h * LANES:(h + 1) * LANES, :] = tile.T.astype(f32)

    for g in range(near_groups):
        second_pass(g)
    hand_on(0)
    far_pass(0)
    lax.fori_loop(0, groups, prepare, 0)
    loads[3].wait()
    for g in range(near_groups):
        for s in range(SUBS):
            turned = q_v[g * LANES:(g + 1) * LANES, s * sub_len:(s + 1) * sub_len].T.astype(f32)
            qs[g, s * sub_len:(s + 1) * sub_len, :] = turned
    turn_query(0)

    dec = dec_t[...]
    lam1 = jnp.exp(-block * dec)
    once = one_minus_exp(seq * dec)
    for send in sends_s:
        send.wait_recv()
    total = jnp.zeros_like(dec)
    before = jnp.zeros_like(dec)
    for j in range(NZ):
        same, across = s_all[j, 0], s_all[j, 1]
        part = jnp.where(x_hi == 0, across + lam1 * same, same + lam1 * across)
        after = (NZ - 1 - lax.rem(z + NZ - j, NZ)).astype(f32) * (block * NX)
        total += jnp.exp(-after * dec) * part
        if j:
            before += jnp.where(z >= j, jnp.exp(-(block * NX * (j - 1)) * dec) * part, 0.0)
    h_y[0] = total
    sends_y = [remote(h_y.at[0], h_y.at[j], y_send.at[j], y_recv.at[j], to_y[j]) for j in range(1, NY)]
    for send in sends_y:
        send.start()

    w_on[0][2].start()
    far_pass(1)
    hand_on(1)
    w_on[1][2].start()
    far_pass(2)
    far_pass(3)
    hand_across(0, 0, 1)

    for send in sends_y:
        send.wait_recv()
    came = jnp.zeros_like(dec)
    for j in range(1, NY + 1):
        came += jnp.exp(-(block * NX * NZ * (j - 1)) * dec) * h_y[j % NY]
    came = jnp.exp(-(z.astype(f32) * (block * NX)) * dec) * came + once * before
    inc[...] = jnp.where(x_hi == 0, came, lam1 * came + once * s_all[0, 1])

    for g in range(far_groups):
        for m in range(modes):
            all_g = near_groups + g
            t_rows[g, m * SUBS:(m + 1) * SUBS, :] = loc[all_g, m] + pw[all_g, m] * wide(inc, all_g, m)
        for k in range(NTP):
            t_out[k, g] = t_rows[g, pl.ds(k * (SUBS // NTP), modes, stride=SUBS), :]
    t_sends = [
        remote(t_out.at[partner_tp[r]], t_in.at[r - 1], t_send.at[r - 1], t_recv.at[r - 1], to_tp[r])
        for r in range(1, NTP)
    ]
    for r in (2, 3, 1):
        t_sends[r - 1].start()

    g_sends = [
        [
            remote(
                gb.at[g, pl.ds(pl.multiple_of(partner_tp[r] * out_toks, out_toks), out_toks)],
                gin.at[r - 1, g], g_send.at[r - 1, g], g_recv.at[r - 1, g], to_tp[r],
            )
            for r in range(1, NTP)
        ]
        for g in range(near_groups)
    ]
    for g in range(near_groups):
        start = [wide(wgt_t, g, m) * (loc[g, m] + pw[g, m] * wide(inc, g, m)) for m in range(modes)]
        lam = [wide(lam_t, g, m) for m in range(modes)]

        def step(t, states):
            states = tuple(l * u for l, u in zip(lam, states))
            yn[g, pl.ds(t, SUBS, stride=sub_len), :] = ys[g, at(t), :] + tree_sum(list(states))
            return states

        lax.fori_loop(0, sub_len, step, tuple(start), unroll=UNROLL)
        gb[g] = (qs[g] * yn[g].astype(bf16).astype(f32)).astype(bf16)
        for r in (2, 3, 1):
            g_sends[g][r - 1].start()

    hand_on(2)
    w_on[2][2].start()
    hand_across(0, 2)
    hand_across(1, 0, 1)

    def far_correct(r):
        if r:
            t_sends[r - 1].wait_recv()
            far[r - 1][1].wait_recv()
            turn_query(r)

        def of_group(g, carry):
            came = (lambda m: wide(t_in, r - 1, g, m)) if r else (lambda m: wide(t_out, tp, g, m))
            start = [
                wide(wgt_d, r, g, m) * (loc_d[r, g, m] + pw_d[r, g, m] * came(m)) for m in range(modes)
            ]
            lam = [wide(lam_d, r, g, m) for m in range(modes)]

            def step(t, states):
                states = tuple(l * u for l, u in zip(lam, states))
                ynd[pl.ds(t, SUBS, stride=far_len), :] = yd[r, g, at(t), :] + tree_sum(list(states))
                return states

            lax.fori_loop(0, far_len, step, tuple(start), unroll=UNROLL)
            gd[r, g] = (qd[r, g] * ynd[...].astype(bf16).astype(f32)).astype(bf16)
            return carry

        lax.fori_loop(0, far_groups, of_group, 0)

    far_correct(0)
    far_correct(1)
    hand_on(3)
    w_on[3][2].start()
    far_correct(2)
    hand_across(1, 2)
    hand_across(2, 0, 1, 2)
    far_correct(3)

    loads[4].wait()
    w_sib.wait_recv()
    for g in range(near_groups):
        g_sends[g][0].wait_recv()
    lhs = jnp.concatenate(
        [gb[g, own_toks, :] for g in range(near_groups)] + [gd[0, g] for g in range(far_groups)]
        + [gin[0, g] for g in range(near_groups)] + [gd[1, g] for g in range(far_groups)], axis=1
    )
    acc[...] = jnp.dot(lhs, jnp.concatenate([wf[0], wf[1]], axis=0), preferred_element_type=f32)
    hand_across(3, 0, 1, 2)
    for per_piece in w_across:
        for copy in per_piece:
            copy.wait_recv()
    lhs = jnp.concatenate([gd[r, g] for r in (2, 3) for g in range(far_groups)], axis=1)
    rhs = jnp.concatenate([wf[r, far_chans:, :] for r in (2, 3)], axis=0)
    acc[...] += jnp.dot(lhs, rhs, preferred_element_type=f32)
    for g in range(near_groups):
        rows = slice(g * LANES, (g + 1) * LANES)
        g_sends[g][1].wait_recv()
        g_sends[g][2].wait_recv()
        lhs = jnp.concatenate([gin[1, g], gin[2, g]], axis=1)
        rhs = jnp.concatenate([wf[2, rows, :], wf[3, rows, :]], axis=0)
        part = acc[...] + jnp.dot(lhs, rhs, preferred_element_type=f32)
        if g == near_groups - 1:
            out_ref[...] = part.astype(bf16)
        else:
            acc[...] = part

    for copy in [w_sib] + sends_s + sends_y + t_sends + w_import:
        copy.wait_send()
    for family in (far, w_on, w_across, g_sends):
        for part in family:
            for copy in part:
                copy.wait_send()


def shards(kv_product, query, decay_rate, residue, out_weight):
    chans, toks = kv_product.shape
    modes = decay_rate.shape[1]
    cols = out_weight.shape[1]
    groups = chans // LANES
    near, far = groups // 2, groups - groups // 2
    out_toks = toks // NTP
    bf16, f32 = jnp.bfloat16, jnp.float32
    small = (groups, modes, LANES)
    runs = (groups, modes, SUBS, LANES)
    far_block = (NTP - 1, chans // 2, out_toks)
    far_coef = (NTP - 1, modes, chans // 2)
    pieces = len(W_ROWS)
    vmem, dma = pltpu.VMEM, pltpu.SemaphoreType.DMA
    operands = (kv_product, query, decay_rate.T, residue.T, out_weight)
    return pl.pallas_call(
        kernel,
        out_shape=jax.ShapeDtypeStruct((out_toks, cols), bf16),
        in_specs=[pl.BlockSpec(memory_space=pltpu.HBM)] * 5,
        out_specs=pl.BlockSpec(memory_space=pltpu.VMEM),
        scratch_shapes=[
            vmem((chans, toks), bf16), vmem((chans, toks), bf16), vmem((modes, chans), f32), vmem((modes, chans), f32),
            vmem(far_block, bf16), vmem(far_block, bf16), vmem(far_coef, f32), vmem(far_coef, f32),
            vmem((NTP, chans, cols), bf16),
            vmem((groups, toks, LANES), f32), vmem((near, toks, LANES), f32),
            vmem((near, toks, LANES), f32), vmem((near, toks, LANES), f32),
            vmem(small, f32), vmem(small, f32), vmem(small, f32), vmem(small, f32),
            vmem(runs, f32), vmem(runs, f32), vmem(runs, f32),
            vmem((NZ, NX) + small, f32), vmem((NY,) + small, f32), vmem(small, f32),
            vmem((far, modes * SUBS, LANES), f32),
            vmem((NTP, far, modes, LANES), f32), vmem((NTP - 1, far, modes, LANES), f32),
            vmem((NTP, far, out_toks, LANES), f32), vmem((NTP, far, out_toks, LANES), f32),
            vmem((NTP, far, out_toks, LANES), f32), vmem((out_toks, LANES), f32),
            vmem((NTP, far, modes, LANES), f32), vmem((NTP, far, modes, LANES), f32),
            vmem((NTP, far, modes, LANES), f32), vmem((NTP, far, modes, LANES), f32),
            vmem((NTP, far, modes, SUBS, LANES), f32), vmem((NTP, far, modes, SUBS, LANES), f32),
            vmem((near, toks, LANES), bf16), vmem((NTP - 1, near, out_toks, LANES), bf16),
            vmem((NTP, far, out_toks, LANES), bf16), vmem((out_toks, cols), f32),
            dma((5,)), dma((NZ, NX)), dma((NZ, NX)), dma((NY,)), dma((NY,)),
            dma((NTP - 1, 4)), dma((NTP - 1, 4)), dma((NTP - 1,)), dma((NTP - 1,)),
            dma((2,)), dma((pieces,)), dma((pieces,)), dma((3, pieces)), dma((3, pieces)),
            dma((4, pieces)), dma((4, pieces)), dma((NTP - 1, near)), dma((NTP - 1, near)),
        ],
        compiler_params=pltpu.CompilerParams(
            collective_id=0, has_side_effects=True, vmem_limit_bytes=50 * 1024 * 1024
        ),
        cost_estimate=pl.CostEstimate(
            flops=2 * out_toks * cols * chans * NTP, bytes_accessed=6 * 1024 * 1024, transcendentals=0
        ),
    )(*(pltpu.with_memory_space_constraint(a, pltpu.HBM) for a in operands))


def solution(mesh):
    in_specs = (P("tp", "ctx"), P("tp", "ctx"), P("tp", None), P("tp", None), P("tp", None))
    out_specs = P(("ctx", "tp"), None)
    return jax.shard_map(shards, mesh=mesh, in_specs=in_specs, out_specs=out_specs, check_vma=False)
```

```python
import jax
import jax.numpy as jnp
from jax import lax
from jax.experimental import pallas as pl
from jax.experimental.pallas import tpu as pltpu
from jax.sharding import PartitionSpec as P

NY, NZ, NX, NTP = 4, 4, 2, 4
SUBS, LANES = 8, 128
W_PIECES = 8
W_UNITS_Y = ((0, 2), (2, 2), (4, 1), (5, 1), (6, 1), (7, 1))
W_UNITS_CORE = ((0, 4), (4, 2), (6, 1), (7, 1))
UNROLL = 16
MESH = pl.DeviceIdType.MESH


def one_minus_exp(z):
    series = jnp.ones_like(z)
    for n in range(10, 1, -1):
        series = 1.0 - (z * (1.0 / n)) * series
    return jnp.where(z < 0.5, z * series, 1.0 - jnp.exp(-z))


def shift_rows(value, by, row):
    return jnp.where(row >= by, pltpu.roll(value, by, 0), 0.0)


def tree_sum(terms):
    while len(terms) > 1:
        terms = [a + b for a, b in zip(terms[::2], terms[1::2])]
    return terms[0]


def at(t):
    return pl.ds(pl.multiple_of(t * SUBS, SUBS), SUBS)


def kernel(
    kv_hbm, q_hbm, dec_hbm, res_hbm, w_hbm, out_ref,
    kv_v, q_v, dec_v, res_v, kv_far, q_far, dec_far, res_far, wf,
    xs, qs, ys, yn, dec_t, lam_t, wgt_t, wc_t, once_t, run_t, ends, loc, pw,
    s_own, s_x, g_z, h_y, inc, t_rows, t_out, t_in,
    xd, qd, yd, ynd, dec_d, lam_d, wgt_d, wc_d, once_d, run_d, loc_d, pw_d,
    gb, gin, gd, acc,
    loc_sem, x_sem, z_send, z_recv, y_send, y_recv, far_send, far_recv, t_send, t_recv,
    wsib_sem, wi_send, wi_recv, wn_send, wn_recv, wa_send, wa_recv, g_send, g_recv,
):
    chans, toks = kv_v.shape
    modes = dec_v.shape[0]
    groups = chans // LANES
    near_groups = groups // 2
    far_chans = chans // 2
    far_groups = groups - near_groups
    sub_len = toks // SUBS
    out_toks, cols = out_ref.shape
    far_len = out_toks // SUBS
    seq = float(toks * NY * NZ * NX)
    block = float(toks)
    f32, bf16 = jnp.float32, jnp.bfloat16

    ctx, tp = lax.axis_index("ctx"), lax.axis_index("tp")
    x_hi = lax.rem(ctx, NX)
    z = lax.rem(ctx // NX, NZ)
    y = ctx // (NX * NZ)
    x_lo, core = tp // 2, lax.rem(tp, 2)

    def ctx_of(yy, zz, xx):
        return (yy * NZ + zz) * NX + xx

    partner_tp = [tp, x_lo * 2 + (1 - core), (1 - x_lo) * 2 + core, (1 - x_lo) * 2 + (1 - core)]
    to_x = {"ctx": ctx_of(y, z, 1 - x_hi), "tp": tp}
    to_z = [{"ctx": ctx_of(y, lax.rem(z + j, NZ), x_hi), "tp": tp} for j in range(NZ)]
    to_y = [{"ctx": ctx_of(lax.rem(y + j, NY), z, x_hi), "tp": tp} for j in range(NY)]
    to_tp = [{"ctx": ctx, "tp": t} for t in partner_tp]
    to_wrap = {"ctx": ctx_of(y, z, 1 - x_hi), "tp": partner_tp[2]}

    loads = [
        pltpu.make_async_copy(kv_hbm, kv_v, loc_sem.at[0]),
        pltpu.make_async_copy(dec_hbm, dec_v, loc_sem.at[1]),
        pltpu.make_async_copy(res_hbm, res_v, loc_sem.at[2]),
        pltpu.make_async_copy(q_hbm, q_v, loc_sem.at[3]),
        pltpu.make_async_copy(w_hbm, wf.at[0], loc_sem.at[4]),
    ]
    for load in loads:
        load.start()

    barrier = pltpu.get_barrier_semaphore()
    partners = [to_x] + to_z[1:] + to_y[1:] + to_tp[1:] + [to_wrap]
    for partner in partners:
        pl.semaphore_signal(barrier, inc=1, device_id=partner, device_id_type=MESH)

    def remote(src, dst, send, recv, to):
        return pltpu.make_async_remote_copy(
            src_ref=src, dst_ref=dst, send_sem=send, recv_sem=recv, device_id=to, device_id_type=MESH
        )

    far_rows, far_cols = pl.ds(far_chans, far_chans), pl.ds(near_groups * LANES, far_chans)
    far = []
    for r in range(1, NTP):
        there = pl.ds(pl.multiple_of(partner_tp[r] * out_toks, out_toks), out_toks)
        pairs = [
            (kv_hbm.at[pl.ds(far_chans + g * LANES, LANES), there], kv_far.at[r - 1, pl.ds(g * LANES, LANES)])
            for g in range(far_groups)
        ] + [
            (dec_hbm.at[:, far_cols], dec_far.at[r - 1]), (res_hbm.at[:, far_cols], res_far.at[r - 1]),
            (q_hbm.at[far_rows, there], q_far.at[r - 1]),
        ]
        far.append(
            [
                remote(src, dst, far_send.at[r - 1, i], far_recv.at[r - 1, i], to_tp[r])
                for i, (src, dst) in enumerate(pairs)
            ]
        )
    f_dec, f_res, f_q = far_groups, far_groups + 1, far_groups + 2

    for i, array in ((f_dec, dec_far), (f_res, res_far)):
        far[2][i] = remote(array.at[1], array.at[2], far_send.at[2, i], far_recv.at[2, i], to_tp[1])

    quarter = chans // 4
    piece = quarter // W_PIECES
    mine = lax.rem(z + 2 * y, 4)
    theirs = (lax.rem(mine + 3, 4), lax.rem(mine + 1, 4), lax.rem(mine + 2, 4))

    def rows_of(which, first, count):
        return pl.ds(pl.multiple_of(which * quarter + first * piece, 16), count * piece)

    def pass_on(way, which, first, count, to):
        rows = rows_of(which, first, count)
        return remote(wf.at[2, rows], wf.at[2, rows], wn_send.at[way, first], wn_recv.at[way, first], to)

    w_sib = remote(w_hbm, wf.at[1], wsib_sem.at[0], wsib_sem.at[1], to_tp[1])
    w_import, w_on_z, w_got_z = [], [], []
    for i in range(W_PIECES):
        rows = rows_of(mine, i, 1)
        w_import.append(remote(w_hbm.at[rows], wf.at[2, rows], wi_send.at[i], wi_recv.at[i], to_wrap))
        ways = (to_z[1], to_z[NZ - 1])
        w_on_z.append([pass_on(way, mine, i, 1, ways[way]) for way in (0, 1)])
        w_got_z.append([pass_on(way, theirs[way], i, 1, ways[way]) for way in (0, 1)])
    w_on_y, w_got_y = {}, {}
    for u, (first, count) in enumerate(W_UNITS_Y):
        to = to_y[1] if u % 2 == 0 else to_y[NY - 1]
        w_on_y[first] = pass_on(2, mine, first, count, to)
        w_got_y[first] = pass_on(2, theirs[2], first, count, to)
    w_across = []
    for u, (first, count) in enumerate(W_UNITS_CORE):
        w_across.append([])
        for way, which in enumerate(theirs + (mine,)):
            rows = rows_of(which, first, count)
            w_across[u].append(
                remote(wf.at[2, rows], wf.at[3, rows], wa_send.at[way, u], wa_recv.at[way, u], to_tp[1])
            )

    def hand_on(i):
        w_import[i].wait_recv()
        w_on_z[i][0].start()
        w_on_z[i][1].start()
        for u, (first, count) in enumerate(W_UNITS_CORE):
            if i == first + count - 1:
                w_across[u][3].start()

    def hand_across(u, *ways):
        first, count = W_UNITS_CORE[u]
        for way in ways:
            for i in range(first, first + count):
                if way < 2:
                    w_got_z[i][way].wait_recv()
                elif i in w_got_y:
                    w_got_y[i].wait_recv()
            w_across[u][way].start()

    def coefficients(dec, res, length, *where):
        refs, where = where[0], where[1:]
        dec_to, lam_to, wgt_to, wc_to, once_to, run_to = refs
        wgt = res * jnp.sqrt(one_minus_exp(2.0 * dec))
        once = one_minus_exp(seq * dec)
        run = jnp.exp(-float(length) * dec)
        dec_to[where] = dec
        lam_to[where] = jnp.exp(-dec)
        wgt_to[where] = wgt
        wc_to[where] = wgt * once
        once_to[where] = once
        for i in range(3):
            run_to[(i, *where)] = run
            run = run * run

    near_coefs = (dec_t, lam_t, wgt_t, wc_t, once_t, run_t)
    far_coefs = (dec_d, lam_d, wgt_d, wc_d, once_d, run_d)
    loads[1].wait()
    loads[2].wait()
    for g in range(groups):
        lanes = slice(g * LANES, (g + 1) * LANES)
        coefficients(dec_v[:, lanes], res_v[:, lanes], sub_len, near_coefs, g)

    loads[0].wait()
    for g in range(groups):
        for s in range(SUBS):
            turned = kv_v[g * LANES:(g + 1) * LANES, s * sub_len:(s + 1) * sub_len].T.astype(f32)
            xs[g, pl.ds(s, sub_len, stride=SUBS), :] = turned

    row = lax.broadcasted_iota(jnp.int32, (SUBS, LANES), 0)
    row_f = row.astype(f32)

    def wide(ref, *where):
        *lead, m = where
        return jnp.broadcast_to(ref[(*lead, slice(m, m + 1), slice(None))], (SUBS, LANES))

    zeros = tuple(jnp.zeros((SUBS, LANES), f32) for _ in range(modes))

    def first_pass(g, carry):
        lam = [wide(lam_t, g, m) for m in range(modes)]

        def step(t, states):
            x = xs[g, at(t), :]
            return tuple(l * u + x for l, u in zip(lam, states))

        states = lax.fori_loop(0, sub_len, step, zeros, unroll=UNROLL)
        for m in range(modes):
            ends[g, m] = states[m]
            decayed = states[m] * jnp.exp(-wide(dec_t, g, m) * ((SUBS - 1 - row_f) * float(sub_len)))
            s_own[g, m:m + 1, :] = jnp.sum(decayed, axis=0, keepdims=True)
        return carry

    lax.fori_loop(0, groups // 2, first_pass, 0)
    pl.semaphore_wait(barrier, len(partners))
    w_import[0].start()
    far[1][0].start()
    for copy in far[0]:
        copy.start()
    w_sib.start()
    lax.fori_loop(groups // 2, groups, first_pass, 0)

    send_x = remote(s_own, s_x, x_sem.at[0], x_sem.at[1], to_x)
    send_x.start()
    for copy in (far[1][1], far[1][f_dec], far[1][f_res], far[2][0], far[2][1], far[1][f_q], far[2][f_q]):
        copy.start()
    for copy in w_import[1:]:
        copy.start()

    def run_starts(states, coefs, length, *where):
        dec_of, _, _, _, once_of, run_of = coefs
        state = shift_rows(states * wide(once_of, *where), 1, row)
        for i, by in enumerate((1, 2, 4)):
            state += wide(run_of, i, *where) * shift_rows(state, by, row)
        return state, jnp.exp(wide(dec_of, *where) * (row_f * -float(length)))

    def prepare(g, carry):
        for m in range(modes):
            loc[g, m], pw[g, m] = run_starts(ends[g, m], near_coefs, sub_len, g, m)
        return carry

    def second_pass(g):
        lam = [wide(lam_t, g, m) for m in range(modes)]
        gain = [wide(wc_t, g, m) for m in range(modes)]

        def step(t, states):
            x = xs[g, at(t), :]
            states = tuple(l * u + x for l, u in zip(lam, states))
            ys[g, at(t), :] = tree_sum([c * u for c, u in zip(gain, states)])
            return states

        lax.fori_loop(0, sub_len, step, zeros, unroll=UNROLL)

    own_toks = pl.ds(pl.multiple_of(tp * out_toks, out_toks), out_toks)

    def far_pass(r):
        if r:
            for i in (0, 1) if r == 2 else (0, 1, f_dec, f_res):
                far[r - 1][i].wait_recv()
        halves = out_toks // LANES
        for g in range(far_groups):
            lanes = slice(g * LANES, (g + 1) * LANES)
            if r:
                dec, res = dec_far[r - 1, :, lanes], res_far[r - 1, :, lanes]
            else:
                own = slice(far_chans + g * LANES, far_chans + (g + 1) * LANES)
                dec, res = dec_v[:, own], res_v[:, own]
            coefficients(dec, res, far_len, far_coefs, r, g)
            for h in range(halves):
                if r:
                    tile = kv_far[r - 1, lanes, h * LANES:(h + 1) * LANES]
                else:
                    tile = kv_v[own, pl.ds(pl.multiple_of(tp * out_toks + h * LANES, LANES), LANES)]
                turned = tile.T.astype(f32)
                for s in range(SUBS // halves):
                    xd[r, g, pl.ds(h * (SUBS // halves) + s, far_len, stride=SUBS), :] = (
                        turned[s * far_len:(s + 1) * far_len]
                    )

        def of_group(g, carry):
            lam = [wide(lam_d, r, g, m) for m in range(modes)]
            gain = [wide(wc_d, r, g, m) for m in range(modes)]

            def step(t, states):
                x = xd[r, g, at(t), :]
                states = tuple(l * u + x for l, u in zip(lam, states))
                yd[r, g, at(t), :] = tree_sum([c * u for c, u in zip(gain, states)])
                return states

            states = lax.fori_loop(0, far_len, step, zeros, unroll=UNROLL)
            for m in range(modes):
                loc_d[r, g, m], pw_d[r, g, m] = run_starts(states[m], far_coefs, far_len, r, g, m)
            return carry

        lax.fori_loop(0, far_groups, of_group, 0)

    def turn_query(r):
        for g in range(far_groups):
            for h in range(out_toks // LANES):
                if r:
                    tile = q_far[r - 1, g * LANES:(g + 1) * LANES, h * LANES:(h + 1) * LANES]
                else:
                    own = slice(far_chans + g * LANES, far_chans + (g + 1) * LANES)
                    tile = q_v[own, pl.ds(pl.multiple_of(tp * out_toks + h * LANES, LANES), LANES)]
                qd[r, g, h * LANES:(h + 1) * LANES, :] = tile.T.astype(f32)

    dec = dec_t[...]
    lam1 = jnp.exp(-block * dec)
    second_pass(0)
    second_pass(1)
    far_pass(0)
    lax.fori_loop(0, groups, prepare, 0)
    hand_on(0)
    send_x.wait_recv()
    same, across = s_own[...], s_x[...]
    g_z[0] = jnp.where(x_hi == 0, across + lam1 * same, same + lam1 * across)
    sends_z = [remote(g_z.at[0], g_z.at[j], z_send.at[j], z_recv.at[j], to_z[j]) for j in range(1, NZ)]
    for send in sends_z:
        send.start()

    loads[3].wait()
    for g in range(near_groups):
        for s in range(SUBS):
            turned = q_v[g * LANES:(g + 1) * LANES, s * sub_len:(s + 1) * sub_len].T.astype(f32)
            qs[g, s * sub_len:(s + 1) * sub_len, :] = turned
    turn_query(0)
    hand_on(1)
    far_pass(1)
    far[1][f_dec].wait_recv()
    far[1][f_res].wait_recv()
    far[2][f_dec].start()
    far[2][f_res].start()
    hand_on(2)
    far_pass(2)
    after = [(NZ - 1 - lax.rem(z + NZ - j, NZ)).astype(f32) * (block * NX) for j in range(NZ)]
    by_total = [jnp.exp(-a * dec) for a in after]
    by_before = [None] + [
        jnp.where(z >= j, jnp.exp(-(block * NX * (j - 1)) * dec), 0.0) for j in range(1, NZ)
    ]
    for send in sends_z:
        send.wait_recv()
    total = by_total[0] * g_z[0]
    before = jnp.zeros_like(dec)
    for j in range(1, NZ):
        part = g_z[j]
        total += by_total[j] * part
        before += by_before[j] * part
    h_y[0] = total
    sends_y = [remote(h_y.at[0], h_y.at[j], y_send.at[j], y_recv.at[j], to_y[j]) for j in range(1, NY)]
    for send in sends_y:
        send.start()

    w_on_y[0].start()
    hand_on(3)
    w_on_y[2].start()
    hand_on(4)
    w_on_y[4].start()
    far_pass(3)
    hand_on(5)
    w_on_y[5].start()

    start_z = z.astype(f32) * (block * NX)
    by_y = [jnp.exp(-(block * NX * NZ * (j - 1) + start_z) * dec) for j in range(1, NY + 1)]
    once = once_t[...]
    before = once * before
    beside = once * s_x[...]
    for send in sends_y:
        send.wait_recv()
    came = before
    for j in range(1, NY + 1):
        came += by_y[j - 1] * h_y[j % NY]
    inc[...] = jnp.where(x_hi == 0, came, lam1 * came + beside)

    for g in range(far_groups):
        for m in range(modes):
            all_g = near_groups + g
            t_rows[g, m * SUBS:(m + 1) * SUBS, :] = loc[all_g, m] + pw[all_g, m] * wide(inc, all_g, m)
        for k in range(NTP):
            t_out[k, g] = t_rows[g, pl.ds(k * (SUBS // NTP), modes, stride=SUBS), :]
    t_sends = [
        remote(t_out.at[partner_tp[r]], t_in.at[r - 1], t_send.at[r - 1], t_recv.at[r - 1], to_tp[r])
        for r in range(1, NTP)
    ]
    for r in (2, 3, 1):
        t_sends[r - 1].start()

    g_sends = [
        [
            remote(
                gb.at[g, pl.ds(pl.multiple_of(partner_tp[r] * out_toks, out_toks), out_toks)],
                gin.at[r - 1, g], g_send.at[r - 1, g], g_recv.at[r - 1, g], to_tp[r],
            )
            for r in range(1, NTP)
        ]
        for g in range(near_groups)
    ]
    for g in range(near_groups):
        start = [wide(wgt_t, g, m) * (loc[g, m] + pw[g, m] * wide(inc, g, m)) for m in range(modes)]
        lam = [wide(lam_t, g, m) for m in range(modes)]

        def step(t, states):
            states = tuple(l * u for l, u in zip(lam, states))
            yn[g, pl.ds(t, SUBS, stride=sub_len), :] = ys[g, at(t), :] + tree_sum(list(states))
            return states

        lax.fori_loop(0, sub_len, step, tuple(start), unroll=UNROLL)
        gb[g] = (qs[g] * yn[g].astype(bf16).astype(f32)).astype(bf16)
        for r in (2, 3, 1):
            g_sends[g][r - 1].start()
        hand_on(6 + g)
        w_on_y[6 + g].start()

    def far_correct(r):
        if r:
            t_sends[r - 1].wait_recv()
            far[r - 1][f_q].wait_recv()
            turn_query(r)

        def of_group(g, carry):
            came = (lambda m: wide(t_in, r - 1, g, m)) if r else (lambda m: wide(t_out, tp, g, m))
            start = [
                wide(wgt_d, r, g, m) * (loc_d[r, g, m] + pw_d[r, g, m] * came(m)) for m in range(modes)
            ]
            lam = [wide(lam_d, r, g, m) for m in range(modes)]

            def step(t, states):
                states = tuple(l * u for l, u in zip(lam, states))
                ynd[pl.ds(t, SUBS, stride=far_len), :] = yd[r, g, at(t), :] + tree_sum(list(states))
                return states

            lax.fori_loop(0, far_len, step, tuple(start), unroll=UNROLL)
            gd[r, g] = (qd[r, g] * ynd[...].astype(bf16).astype(f32)).astype(bf16)
            return carry

        lax.fori_loop(0, far_groups, of_group, 0)

    far_correct(0)
    hand_across(0, 0, 1, 2)
    far_correct(1)
    hand_across(1, 0, 1)
    far_correct(2)
    hand_across(1, 2)
    far_correct(3)
    hand_across(2, 0, 1, 2)

    loads[4].wait()
    w_sib.wait_recv()
    for g in range(near_groups):
        g_sends[g][0].wait_recv()
    lhs = jnp.concatenate(
        [gb[g, own_toks, :] for g in range(near_groups)] + [gd[0, g] for g in range(far_groups)]
        + [gin[0, g] for g in range(near_groups)] + [gd[1, g] for g in range(far_groups)], axis=1
    )
    acc[...] = jnp.dot(lhs, jnp.concatenate([wf[0], wf[1]], axis=0), preferred_element_type=f32)
    hand_across(3, 0, 1, 2)
    for per_piece in w_across:
        for copy in per_piece:
            copy.wait_recv()
    lhs = jnp.concatenate([gd[r, g] for r in (2, 3) for g in range(far_groups)], axis=1)
    rhs = jnp.concatenate([wf[r, far_chans:, :] for r in (2, 3)], axis=0)
    acc[...] += jnp.dot(lhs, rhs, preferred_element_type=f32)
    for g in range(near_groups):
        rows = slice(g * LANES, (g + 1) * LANES)
        g_sends[g][1].wait_recv()
        g_sends[g][2].wait_recv()
        lhs = jnp.concatenate([gin[1, g], gin[2, g]], axis=1)
        rhs = jnp.concatenate([wf[2, rows, :], wf[3, rows, :]], axis=0)
        part = acc[...] + jnp.dot(lhs, rhs, preferred_element_type=f32)
        if g == near_groups - 1:
            out_ref[...] = part.astype(bf16)
        else:
            acc[...] = part

    for copy in [w_sib, send_x] + sends_z + sends_y + t_sends + w_import + list(w_on_y.values()):
        copy.wait_send()
    for family in (far, w_on_z, w_across, g_sends):
        for part in family:
            for copy in part:
                copy.wait_send()


def shards(kv_product, query, decay_rate, residue, out_weight):
    chans, toks = kv_product.shape
    modes = decay_rate.shape[1]
    cols = out_weight.shape[1]
    groups = chans // LANES
    near, far = groups // 2, groups - groups // 2
    out_toks = toks // NTP
    bf16, f32 = jnp.bfloat16, jnp.float32
    small = (groups, modes, LANES)
    runs = (groups, modes, SUBS, LANES)
    far_block = (NTP - 1, chans // 2, out_toks)
    far_coef = (NTP - 1, modes, chans // 2)
    pieces = W_PIECES
    vmem, dma = pltpu.VMEM, pltpu.SemaphoreType.DMA
    operands = (kv_product, query, decay_rate.T, residue.T, out_weight)
    return pl.pallas_call(
        kernel,
        out_shape=jax.ShapeDtypeStruct((out_toks, cols), bf16),
        in_specs=[pl.BlockSpec(memory_space=pltpu.HBM)] * 5,
        out_specs=pl.BlockSpec(memory_space=pltpu.VMEM),
        scratch_shapes=[
            vmem((chans, toks), bf16), vmem((chans, toks), bf16), vmem((modes, chans), f32), vmem((modes, chans), f32),
            vmem(far_block, bf16), vmem(far_block, bf16), vmem(far_coef, f32), vmem(far_coef, f32),
            vmem((NTP, chans, cols), bf16),
            vmem((groups, toks, LANES), f32), vmem((near, toks, LANES), f32),
            vmem((near, toks, LANES), f32), vmem((near, toks, LANES), f32),
            vmem(small, f32), vmem(small, f32), vmem(small, f32), vmem(small, f32), vmem(small, f32),
            vmem((3,) + small, f32),
            vmem(runs, f32), vmem(runs, f32), vmem(runs, f32),
            vmem(small, f32), vmem(small, f32), vmem((NZ,) + small, f32), vmem((NY,) + small, f32), vmem(small, f32),
            vmem((far, modes * SUBS, LANES), f32),
            vmem((NTP, far, modes, LANES), f32), vmem((NTP - 1, far, modes, LANES), f32),
            vmem((NTP, far, out_toks, LANES), f32), vmem((NTP, far, out_toks, LANES), f32),
            vmem((NTP, far, out_toks, LANES), f32), vmem((out_toks, LANES), f32),
            vmem((NTP, far, modes, LANES), f32), vmem((NTP, far, modes, LANES), f32),
            vmem((NTP, far, modes, LANES), f32), vmem((NTP, far, modes, LANES), f32),
            vmem((NTP, far, modes, LANES), f32), vmem((3, NTP, far, modes, LANES), f32),
            vmem((NTP, far, modes, SUBS, LANES), f32), vmem((NTP, far, modes, SUBS, LANES), f32),
            vmem((near, toks, LANES), bf16), vmem((NTP - 1, near, out_toks, LANES), bf16),
            vmem((NTP, far, out_toks, LANES), bf16), vmem((out_toks, cols), f32),
            dma((5,)), dma((2,)), dma((NZ,)), dma((NZ,)), dma((NY,)), dma((NY,)),
            dma((NTP - 1, far + 3)), dma((NTP - 1, far + 3)), dma((NTP - 1,)), dma((NTP - 1,)),
            dma((2,)), dma((pieces,)), dma((pieces,)), dma((3, pieces)), dma((3, pieces)),
            dma((4, len(W_UNITS_CORE))), dma((4, len(W_UNITS_CORE))), dma((NTP - 1, near)), dma((NTP - 1, near)),
        ],
        compiler_params=pltpu.CompilerParams(
            collective_id=0, has_side_effects=True, vmem_limit_bytes=50 * 1024 * 1024
        ),
        cost_estimate=pl.CostEstimate(
            flops=2 * out_toks * cols * chans * NTP, bytes_accessed=6 * 1024 * 1024, transcendentals=0
        ),
    )(*(pltpu.with_memory_space_constraint(a, pltpu.HBM) for a in operands))


def solution(mesh):
    in_specs = (P("tp", "ctx"), P("tp", "ctx"), P("tp", None), P("tp", None), P("tp", None))
    out_specs = P(("ctx", "tp"), None)
    return jax.shard_map(shards, mesh=mesh, in_specs=in_specs, out_specs=out_specs, check_vma=False)
```

```python
import jax
import jax.numpy as jnp
from jax import lax
from jax.experimental import pallas as pl
from jax.experimental.pallas import tpu as pltpu
from jax.sharding import PartitionSpec as P

NY, NZ, NX, NTP = 4, 4, 2, 4
SUBS, LANES = 8, 128
W_PIECES = 8
W_UNITS_Y = ((0, 2), (2, 2), (4, 1), (5, 1), (6, 1), (7, 1))
W_UNITS_CORE = ((0, 4), (4, 2), (6, 1), (7, 1))
UNROLL = 16
MESH = pl.DeviceIdType.MESH


def one_minus_exp(z):
    series = jnp.ones_like(z)
    for n in range(10, 1, -1):
        series = 1.0 - (z * (1.0 / n)) * series
    return jnp.where(z < 0.5, z * series, 1.0 - jnp.exp(-z))


def shift_rows(value, by, row):
    return jnp.where(row >= by, pltpu.roll(value, by, 0), 0.0)


def tree_sum(terms):
    while len(terms) > 1:
        terms = [a + b for a, b in zip(terms[::2], terms[1::2])]
    return terms[0]


def at(t):
    return pl.ds(pl.multiple_of(t * SUBS, SUBS), SUBS)


def kernel(
    kv_hbm, q_hbm, dec_hbm, res_hbm, w_hbm, out_ref,
    kv_v, q_v, dec_v, res_v, kv_far, q_far, dec_far, res_far, wf,
    xs, qs, ys, yn, dec_t, lam_t, wgt_t, wc_t, once_t, run_t, ends, loc, pw,
    s_own, s_x, g_z, h_y, inc, t_rows, t_out, t_in,
    xd, qd, yd, ynd, dec_d, lam_d, wgt_d, wc_d, once_d, run_d, loc_d, pw_d,
    gb, gin, gd, acc,
    loc_sem, x_sem, z_send, z_recv, y_send, y_recv, far_send, far_recv, t_send, t_recv,
    wsib_sem, wi_send, wi_recv, wn_send, wn_recv, wa_send, wa_recv, g_send, g_recv,
):
    chans, toks = kv_v.shape
    modes = dec_v.shape[0]
    groups = chans // LANES
    near_groups = groups // 2
    far_chans = chans // 2
    far_groups = groups - near_groups
    sub_len = toks // SUBS
    out_toks, cols = out_ref.shape
    far_len = out_toks // SUBS
    seq = float(toks * NY * NZ * NX)
    block = float(toks)
    f32, bf16 = jnp.float32, jnp.bfloat16

    ctx, tp = lax.axis_index("ctx"), lax.axis_index("tp")
    x_hi = lax.rem(ctx, NX)
    z = lax.rem(ctx // NX, NZ)
    y = ctx // (NX * NZ)
    x_lo, core = tp // 2, lax.rem(tp, 2)

    def ctx_of(yy, zz, xx):
        return (yy * NZ + zz) * NX + xx

    partner_tp = [tp, x_lo * 2 + (1 - core), (1 - x_lo) * 2 + core, (1 - x_lo) * 2 + (1 - core)]
    to_x = {"ctx": ctx_of(y, z, 1 - x_hi), "tp": tp}
    to_z = [{"ctx": ctx_of(y, lax.rem(z + j, NZ), x_hi), "tp": tp} for j in range(NZ)]
    to_y = [{"ctx": ctx_of(lax.rem(y + j, NY), z, x_hi), "tp": tp} for j in range(NY)]
    to_tp = [{"ctx": ctx, "tp": t} for t in partner_tp]
    to_wrap = {"ctx": ctx_of(y, z, 1 - x_hi), "tp": partner_tp[2]}

    loads = [
        pltpu.make_async_copy(dec_hbm, dec_v, loc_sem.at[0]),
        pltpu.make_async_copy(res_hbm, res_v, loc_sem.at[1]),
        pltpu.make_async_copy(q_hbm, q_v, loc_sem.at[2]),
        pltpu.make_async_copy(w_hbm, wf.at[0], loc_sem.at[3]),
    ]
    kv_rows = [pl.ds(g * LANES, LANES) for g in range(groups)]
    kv_loads = [
        pltpu.make_async_copy(kv_hbm.at[rows], kv_v.at[rows], loc_sem.at[4 + g]) for g, rows in enumerate(kv_rows)
    ]
    for load in loads[:2] + kv_loads + loads[2:]:
        load.start()

    barrier = pltpu.get_barrier_semaphore()
    partners = [to_x] + to_z[1:] + to_y[1:] + to_tp[1:] + [to_wrap]
    for partner in partners:
        pl.semaphore_signal(barrier, inc=1, device_id=partner, device_id_type=MESH)

    def remote(src, dst, send, recv, to):
        return pltpu.make_async_remote_copy(
            src_ref=src, dst_ref=dst, send_sem=send, recv_sem=recv, device_id=to, device_id_type=MESH
        )

    far_rows, far_cols = pl.ds(far_chans, far_chans), pl.ds(near_groups * LANES, far_chans)
    far = []
    for r in range(1, NTP):
        there = pl.ds(pl.multiple_of(partner_tp[r] * out_toks, out_toks), out_toks)
        pairs = [
            (kv_hbm.at[pl.ds(far_chans + g * LANES, LANES), there], kv_far.at[r - 1, pl.ds(g * LANES, LANES)])
            for g in range(far_groups)
        ] + [
            (dec_hbm.at[:, far_cols], dec_far.at[r - 1]), (res_hbm.at[:, far_cols], res_far.at[r - 1]),
            (q_hbm.at[far_rows, there], q_far.at[r - 1]),
        ]
        far.append(
            [
                remote(src, dst, far_send.at[r - 1, i], far_recv.at[r - 1, i], to_tp[r])
                for i, (src, dst) in enumerate(pairs)
            ]
        )
    f_dec, f_res, f_q = far_groups, far_groups + 1, far_groups + 2

    for i, array in ((f_dec, dec_far), (f_res, res_far)):
        far[2][i] = remote(array.at[1], array.at[2], far_send.at[2, i], far_recv.at[2, i], to_tp[1])

    quarter = chans // 4
    piece = quarter // W_PIECES
    mine = lax.rem(z + 2 * y, 4)
    theirs = (lax.rem(mine + 3, 4), lax.rem(mine + 1, 4), lax.rem(mine + 2, 4))

    def rows_of(which, first, count):
        return pl.ds(pl.multiple_of(which * quarter + first * piece, 16), count * piece)

    def pass_on(way, which, first, count, to):
        rows = rows_of(which, first, count)
        return remote(wf.at[2, rows], wf.at[2, rows], wn_send.at[way, first], wn_recv.at[way, first], to)

    w_sib = remote(w_hbm, wf.at[1], wsib_sem.at[0], wsib_sem.at[1], to_tp[1])
    w_import, w_on_z, w_got_z = [], [], []
    for i in range(W_PIECES):
        rows = rows_of(mine, i, 1)
        w_import.append(remote(w_hbm.at[rows], wf.at[2, rows], wi_send.at[i], wi_recv.at[i], to_wrap))
        ways = (to_z[1], to_z[NZ - 1])
        w_on_z.append([pass_on(way, mine, i, 1, ways[way]) for way in (0, 1)])
        w_got_z.append([pass_on(way, theirs[way], i, 1, ways[way]) for way in (0, 1)])
    w_on_y, w_got_y = {}, {}
    for u, (first, count) in enumerate(W_UNITS_Y):
        to = to_y[1] if u % 2 == 0 else to_y[NY - 1]
        w_on_y[first] = pass_on(2, mine, first, count, to)
        w_got_y[first] = pass_on(2, theirs[2], first, count, to)
    w_across = []
    for u, (first, count) in enumerate(W_UNITS_CORE):
        w_across.append([])
        for way, which in enumerate(theirs + (mine,)):
            rows = rows_of(which, first, count)
            w_across[u].append(
                remote(wf.at[2, rows], wf.at[3, rows], wa_send.at[way, u], wa_recv.at[way, u], to_tp[1])
            )

    def hand_on(i):
        w_import[i].wait_recv()
        w_on_z[i][0].start()
        w_on_z[i][1].start()
        for u, (first, count) in enumerate(W_UNITS_CORE):
            if i == first + count - 1:
                w_across[u][3].start()

    def hand_across(u, *ways):
        first, count = W_UNITS_CORE[u]
        for way in ways:
            for i in range(first, first + count):
                if way < 2:
                    w_got_z[i][way].wait_recv()
                elif i in w_got_y:
                    w_got_y[i].wait_recv()
            w_across[u][way].start()

    def coefficients(dec, res, length, *where):
        refs, where = where[0], where[1:]
        dec_to, lam_to, wgt_to, wc_to, once_to, run_to = refs
        wgt = res * jnp.sqrt(one_minus_exp(2.0 * dec))
        once = one_minus_exp(seq * dec)
        run = jnp.exp(-float(length) * dec)
        dec_to[where] = dec
        lam_to[where] = jnp.exp(-dec)
        wgt_to[where] = wgt
        wc_to[where] = wgt * once
        once_to[where] = once
        for i in range(3):
            run_to[(i, *where)] = run
            run = run * run

    near_coefs = (dec_t, lam_t, wgt_t, wc_t, once_t, run_t)
    far_coefs = (dec_d, lam_d, wgt_d, wc_d, once_d, run_d)
    loads[0].wait()
    loads[1].wait()
    for g in range(groups):
        lanes = slice(g * LANES, (g + 1) * LANES)
        coefficients(dec_v[:, lanes], res_v[:, lanes], sub_len, near_coefs, g)

    def turn_near(g):
        kv_loads[g].wait()
        for s in range(SUBS):
            turned = kv_v[g * LANES:(g + 1) * LANES, s * sub_len:(s + 1) * sub_len].T.astype(f32)
            xs[g, pl.ds(s, sub_len, stride=SUBS), :] = turned

    row = lax.broadcasted_iota(jnp.int32, (SUBS, LANES), 0)
    row_f = row.astype(f32)

    def wide(ref, *where):
        *lead, m = where
        return jnp.broadcast_to(ref[(*lead, slice(m, m + 1), slice(None))], (SUBS, LANES))

    zeros = tuple(jnp.zeros((SUBS, LANES), f32) for _ in range(modes))

    def first_pass(g):
        lam = [wide(lam_t, g, m) for m in range(modes)]

        def step(t, states):
            x = xs[g, at(t), :]
            return tuple(l * u + x for l, u in zip(lam, states))

        states = lax.fori_loop(0, sub_len, step, zeros, unroll=UNROLL)
        for m in range(modes):
            ends[g, m] = states[m]
            decayed = states[m] * jnp.exp(-wide(dec_t, g, m) * ((SUBS - 1 - row_f) * float(sub_len)))
            s_own[g, m:m + 1, :] = jnp.sum(decayed, axis=0, keepdims=True)

    for g in range(groups // 2):
        turn_near(g)
        first_pass(g)
    pl.semaphore_wait(barrier, len(partners))
    w_import[0].start()
    far[1][0].start()
    for copy in far[0]:
        copy.start()
    w_sib.start()
    for g in range(groups // 2, groups):
        turn_near(g)
        first_pass(g)

    send_x = remote(s_own, s_x, x_sem.at[0], x_sem.at[1], to_x)
    send_x.start()
    for copy in (far[1][1], far[1][f_dec], far[1][f_res], far[2][0], far[2][1], far[1][f_q], far[2][f_q]):
        copy.start()
    for copy in w_import[1:]:
        copy.start()

    def run_starts(states, coefs, length, *where):
        dec_of, _, _, _, once_of, run_of = coefs
        state = shift_rows(states * wide(once_of, *where), 1, row)
        for i, by in enumerate((1, 2, 4)):
            state += wide(run_of, i, *where) * shift_rows(state, by, row)
        return state, jnp.exp(wide(dec_of, *where) * (row_f * -float(length)))

    def prepare(g, carry, weighted):
        for m in range(modes):
            state, decay = run_starts(ends[g, m], near_coefs, sub_len, g, m)
            wgt = wide(wgt_t, g, m) if weighted else 1.0
            loc[g, m], pw[g, m] = wgt * state, wgt * decay
        return carry

    def second_pass(g):
        lam = [wide(lam_t, g, m) for m in range(modes)]
        gain = [wide(wc_t, g, m) for m in range(modes)]

        def step(t, states):
            x = xs[g, at(t), :]
            states = tuple(l * u + x for l, u in zip(lam, states))
            ys[g, at(t), :] = tree_sum([c * u for c, u in zip(gain, states)])
            return states

        lax.fori_loop(0, sub_len, step, zeros, unroll=UNROLL)

    own_toks = pl.ds(pl.multiple_of(tp * out_toks, out_toks), out_toks)

    def far_pass(r):
        if r:
            for i in (0, 1) if r == 2 else (0, 1, f_dec, f_res):
                far[r - 1][i].wait_recv()
        halves = out_toks // LANES
        for g in range(far_groups):
            lanes = slice(g * LANES, (g + 1) * LANES)
            if r:
                dec, res = dec_far[r - 1, :, lanes], res_far[r - 1, :, lanes]
            else:
                own = slice(far_chans + g * LANES, far_chans + (g + 1) * LANES)
                dec, res = dec_v[:, own], res_v[:, own]
            coefficients(dec, res, far_len, far_coefs, r, g)
            for h in range(halves):
                if r:
                    tile = kv_far[r - 1, lanes, h * LANES:(h + 1) * LANES]
                else:
                    tile = kv_v[own, pl.ds(pl.multiple_of(tp * out_toks + h * LANES, LANES), LANES)]
                turned = tile.T.astype(f32)
                for s in range(SUBS // halves):
                    xd[r, g, pl.ds(h * (SUBS // halves) + s, far_len, stride=SUBS), :] = (
                        turned[s * far_len:(s + 1) * far_len]
                    )

        def of_group(g, carry):
            lam = [wide(lam_d, r, g, m) for m in range(modes)]
            gain = [wide(wc_d, r, g, m) for m in range(modes)]

            def step(t, states):
                x = xd[r, g, at(t), :]
                states = tuple(l * u + x for l, u in zip(lam, states))
                yd[r, g, at(t), :] = tree_sum([c * u for c, u in zip(gain, states)])
                return states

            states = lax.fori_loop(0, far_len, step, zeros, unroll=UNROLL)
            for m in range(modes):
                state, decay = run_starts(states[m], far_coefs, far_len, r, g, m)
                wgt = wide(wgt_d, r, g, m)
                loc_d[r, g, m], pw_d[r, g, m] = wgt * state, wgt * decay
            return carry

        lax.fori_loop(0, far_groups, of_group, 0)

    def turn_query(r):
        for g in range(far_groups):
            for h in range(out_toks // LANES):
                if r:
                    tile = q_far[r - 1, g * LANES:(g + 1) * LANES, h * LANES:(h + 1) * LANES]
                else:
                    own = slice(far_chans + g * LANES, far_chans + (g + 1) * LANES)
                    tile = q_v[own, pl.ds(pl.multiple_of(tp * out_toks + h * LANES, LANES), LANES)]
                qd[r, g, h * LANES:(h + 1) * LANES, :] = tile.T.astype(f32)

    dec = dec_t[...]
    lam1 = jnp.exp(-block * dec)
    second_pass(0)
    second_pass(1)
    far_pass(0)
    lax.fori_loop(0, near_groups, lambda g, carry: prepare(g, carry, True), 0)
    lax.fori_loop(near_groups, groups, lambda g, carry: prepare(g, carry, False), 0)
    send_x.wait_recv()
    same, across = s_own[...], s_x[...]
    g_z[0] = jnp.where(x_hi == 0, across + lam1 * same, same + lam1 * across)
    sends_z = [remote(g_z.at[0], g_z.at[j], z_send.at[j], z_recv.at[j], to_z[j]) for j in range(1, NZ)]
    for send in sends_z:
        send.start()

    loads[2].wait()
    for g in range(near_groups):
        for s in range(SUBS):
            turned = q_v[g * LANES:(g + 1) * LANES, s * sub_len:(s + 1) * sub_len].T.astype(f32)
            qs[g, s * sub_len:(s + 1) * sub_len, :] = turned
    turn_query(0)
    hand_on(0)
    far_pass(1)
    far[1][f_dec].wait_recv()
    far[1][f_res].wait_recv()
    far[2][f_dec].start()
    far[2][f_res].start()
    hand_on(1)
    far_pass(2)
    hand_on(2)
    after = [(NZ - 1 - lax.rem(z + NZ - j, NZ)).astype(f32) * (block * NX) for j in range(NZ)]
    by_total = [jnp.exp(-a * dec) for a in after]
    by_before = [None] + [
        jnp.where(z >= j, jnp.exp(-(block * NX * (j - 1)) * dec), 0.0) for j in range(1, NZ)
    ]
    for send in sends_z:
        send.wait_recv()
    total = by_total[0] * g_z[0]
    before = jnp.zeros_like(dec)
    for j in range(1, NZ):
        part = g_z[j]
        total += by_total[j] * part
        before += by_before[j] * part
    h_y[0] = total
    sends_y = [remote(h_y.at[0], h_y.at[j], y_send.at[j], y_recv.at[j], to_y[j]) for j in range(1, NY)]
    for send in sends_y:
        send.start()

    w_on_y[0].start()
    far_pass(3)
    hand_on(3)
    w_on_y[2].start()
    hand_on(4)
    w_on_y[4].start()

    start_z = z.astype(f32) * (block * NX)
    by_y = [jnp.exp(-(block * NX * NZ * (j - 1) + start_z) * dec) for j in range(1, NY + 1)]
    once = once_t[...]
    before = once * before
    beside = once * s_x[...]
    for send in sends_y:
        send.wait_recv()
    came = before
    for j in range(1, NY + 1):
        came += by_y[j - 1] * h_y[j % NY]
    inc[...] = jnp.where(x_hi == 0, came, lam1 * came + beside)

    for g in range(far_groups):
        for m in range(modes):
            all_g = near_groups + g
            t_rows[g, m * SUBS:(m + 1) * SUBS, :] = loc[all_g, m] + pw[all_g, m] * wide(inc, all_g, m)
        for k in range(NTP):
            t_out[k, g] = t_rows[g, pl.ds(k * (SUBS // NTP), modes, stride=SUBS), :]
    t_sends = [
        remote(t_out.at[partner_tp[r]], t_in.at[r - 1], t_send.at[r - 1], t_recv.at[r - 1], to_tp[r])
        for r in range(1, NTP)
    ]
    for r in (2, 3, 1):
        t_sends[r - 1].start()
    for i in (5, 6):
        hand_on(i)
        w_on_y[i].start()

    g_sends = [
        [
            remote(
                gb.at[g, pl.ds(pl.multiple_of(partner_tp[r] * out_toks, out_toks), out_toks)],
                gin.at[r - 1, g], g_send.at[r - 1, g], g_recv.at[r - 1, g], to_tp[r],
            )
            for r in range(1, NTP)
        ]
        for g in range(near_groups)
    ]
    for g in range(near_groups):
        start = [loc[g, m] + pw[g, m] * wide(inc, g, m) for m in range(modes)]
        lam = [wide(lam_t, g, m) for m in range(modes)]

        def step(t, states):
            states = tuple(l * u for l, u in zip(lam, states))
            yn[g, pl.ds(t, SUBS, stride=sub_len), :] = ys[g, at(t), :] + tree_sum(list(states))
            return states

        lax.fori_loop(0, sub_len, step, tuple(start), unroll=UNROLL)
        gb[g] = (qs[g] * yn[g].astype(bf16).astype(f32)).astype(bf16)
        for r in (2, 3, 1):
            g_sends[g][r - 1].start()
        if g == 0:
            hand_on(7)
            w_on_y[7].start()

    def far_correct(r):
        if r:
            t_sends[r - 1].wait_recv()
            far[r - 1][f_q].wait_recv()
            turn_query(r)

        def of_group(g, carry):
            came = (lambda m: wide(t_in, r - 1, g, m)) if r else (lambda m: wide(t_out, tp, g, m))
            start = [loc_d[r, g, m] + pw_d[r, g, m] * came(m) for m in range(modes)]
            lam = [wide(lam_d, r, g, m) for m in range(modes)]

            def step(t, states):
                states = tuple(l * u for l, u in zip(lam, states))
                ynd[pl.ds(t, SUBS, stride=far_len), :] = yd[r, g, at(t), :] + tree_sum(list(states))
                return states

            lax.fori_loop(0, far_len, step, tuple(start), unroll=UNROLL)
            gd[r, g] = (qd[r, g] * ynd[...].astype(bf16).astype(f32)).astype(bf16)
            return carry

        lax.fori_loop(0, far_groups, of_group, 0)

    far_correct(0)
    hand_across(0, 0, 1, 2)
    far_correct(1)
    hand_across(1, 0, 1)
    far_correct(2)
    hand_across(1, 2)
    hand_across(2, 0, 1)
    far_correct(3)
    hand_across(2, 2)
    hand_across(3, 0, 1, 2)

    loads[3].wait()
    w_sib.wait_recv()
    for g in range(near_groups):
        g_sends[g][0].wait_recv()
    lhs = jnp.concatenate(
        [gb[g, own_toks, :] for g in range(near_groups)] + [gd[0, g] for g in range(far_groups)]
        + [gin[0, g] for g in range(near_groups)] + [gd[1, g] for g in range(far_groups)], axis=1
    )
    acc[...] = jnp.dot(lhs, jnp.concatenate([wf[0], wf[1]], axis=0), preferred_element_type=f32)
    for per_piece in w_across:
        for copy in per_piece:
            copy.wait_recv()
    lhs = jnp.concatenate([gd[r, g] for r in (2, 3) for g in range(far_groups)], axis=1)
    rhs = jnp.concatenate([wf[r, far_chans:, :] for r in (2, 3)], axis=0)
    acc[...] += jnp.dot(lhs, rhs, preferred_element_type=f32)
    for g in range(near_groups):
        rows = slice(g * LANES, (g + 1) * LANES)
        g_sends[g][1].wait_recv()
        g_sends[g][2].wait_recv()
        lhs = jnp.concatenate([gin[1, g], gin[2, g]], axis=1)
        rhs = jnp.concatenate([wf[2, rows, :], wf[3, rows, :]], axis=0)
        part = acc[...] + jnp.dot(lhs, rhs, preferred_element_type=f32)
        if g == near_groups - 1:
            out_ref[...] = part.astype(bf16)
        else:
            acc[...] = part

    for copy in [w_sib, send_x] + sends_z + sends_y + t_sends + w_import + list(w_on_y.values()):
        copy.wait_send()
    for family in (far, w_on_z, w_across, g_sends):
        for part in family:
            for copy in part:
                copy.wait_send()


def shards(kv_product, query, decay_rate, residue, out_weight):
    chans, toks = kv_product.shape
    modes = decay_rate.shape[1]
    cols = out_weight.shape[1]
    groups = chans // LANES
    near, far = groups // 2, groups - groups // 2
    out_toks = toks // NTP
    bf16, f32 = jnp.bfloat16, jnp.float32
    small = (groups, modes, LANES)
    runs = (groups, modes, SUBS, LANES)
    far_block = (NTP - 1, chans // 2, out_toks)
    far_coef = (NTP - 1, modes, chans // 2)
    pieces = W_PIECES
    vmem, dma = pltpu.VMEM, pltpu.SemaphoreType.DMA
    operands = (kv_product, query, decay_rate.T, residue.T, out_weight)
    return pl.pallas_call(
        kernel,
        out_shape=jax.ShapeDtypeStruct((out_toks, cols), bf16),
        in_specs=[pl.BlockSpec(memory_space=pltpu.HBM)] * 5,
        out_specs=pl.BlockSpec(memory_space=pltpu.VMEM),
        scratch_shapes=[
            vmem((chans, toks), bf16), vmem((chans, toks), bf16), vmem((modes, chans), f32), vmem((modes, chans), f32),
            vmem(far_block, bf16), vmem(far_block, bf16), vmem(far_coef, f32), vmem(far_coef, f32),
            vmem((NTP, chans, cols), bf16),
            vmem((groups, toks, LANES), f32), vmem((near, toks, LANES), f32),
            vmem((near, toks, LANES), f32), vmem((near, toks, LANES), f32),
            vmem(small, f32), vmem(small, f32), vmem(small, f32), vmem(small, f32), vmem(small, f32),
            vmem((3,) + small, f32),
            vmem(runs, f32), vmem(runs, f32), vmem(runs, f32),
            vmem(small, f32), vmem(small, f32), vmem((NZ,) + small, f32), vmem((NY,) + small, f32), vmem(small, f32),
            vmem((far, modes * SUBS, LANES), f32),
            vmem((NTP, far, modes, LANES), f32), vmem((NTP - 1, far, modes, LANES), f32),
            vmem((NTP, far, out_toks, LANES), f32), vmem((NTP, far, out_toks, LANES), f32),
            vmem((NTP, far, out_toks, LANES), f32), vmem((out_toks, LANES), f32),
            vmem((NTP, far, modes, LANES), f32), vmem((NTP, far, modes, LANES), f32),
            vmem((NTP, far, modes, LANES), f32), vmem((NTP, far, modes, LANES), f32),
            vmem((NTP, far, modes, LANES), f32), vmem((3, NTP, far, modes, LANES), f32),
            vmem((NTP, far, modes, SUBS, LANES), f32), vmem((NTP, far, modes, SUBS, LANES), f32),
            vmem((near, toks, LANES), bf16), vmem((NTP - 1, near, out_toks, LANES), bf16),
            vmem((NTP, far, out_toks, LANES), bf16), vmem((out_toks, cols), f32),
            dma((4 + groups,)), dma((2,)), dma((NZ,)), dma((NZ,)), dma((NY,)), dma((NY,)),
            dma((NTP - 1, far + 3)), dma((NTP - 1, far + 3)), dma((NTP - 1,)), dma((NTP - 1,)),
            dma((2,)), dma((pieces,)), dma((pieces,)), dma((3, pieces)), dma((3, pieces)),
            dma((4, len(W_UNITS_CORE))), dma((4, len(W_UNITS_CORE))), dma((NTP - 1, near)), dma((NTP - 1, near)),
        ],
        compiler_params=pltpu.CompilerParams(
            collective_id=0, has_side_effects=True, vmem_limit_bytes=50 * 1024 * 1024
        ),
        cost_estimate=pl.CostEstimate(
            flops=2 * out_toks * cols * chans * NTP, bytes_accessed=6 * 1024 * 1024, transcendentals=0
        ),
    )(*(pltpu.with_memory_space_constraint(a, pltpu.HBM) for a in operands))


def solution(mesh):
    in_specs = (P("tp", "ctx"), P("tp", "ctx"), P("tp", None), P("tp", None), P("tp", None))
    out_specs = P(("ctx", "tp"), None)
    return jax.shard_map(shards, mesh=mesh, in_specs=in_specs, out_specs=out_specs, check_vma=False)
```

```python
import jax
import jax.numpy as jnp
from jax import lax
from jax.experimental import pallas as pl
from jax.experimental.pallas import tpu as pltpu
from jax.sharding import PartitionSpec as P

NY, NZ, NX, NTP = 4, 4, 2, 4
SUBS, LANES = 8, 128
W_PIECES = 8
W_ORDER = (0, 4, 1, 5, 2, 6, 3, 7)
W_UNITS = ((0, 2), (2, 1), (3, 1), (4, 2), (6, 1), (7, 1))
UNROLL = 16
MESH = pl.DeviceIdType.MESH


def one_minus_exp(z):
    series = jnp.ones_like(z)
    for n in range(10, 1, -1):
        series = 1.0 - (z * (1.0 / n)) * series
    return jnp.where(z < 0.5, z * series, 1.0 - jnp.exp(-z))


def shift_rows(value, by, row):
    return jnp.where(row >= by, pltpu.roll(value, by, 0), 0.0)


def tree_sum(terms):
    while len(terms) > 1:
        terms = [a + b for a, b in zip(terms[::2], terms[1::2])]
    return terms[0]


def at(t):
    return pl.ds(pl.multiple_of(t * SUBS, SUBS), SUBS)


def kernel(
    kv_hbm, q_hbm, dec_hbm, res_hbm, w_hbm, out_ref,
    kv_v, q_v, dec_v, res_v, kv_far, q_far, dec_far, res_far, wf,
    xs, qs, ys, yn, dec_t, lam_t, wgt_t, wc_t, once_t, run_t, ends, loc, pw,
    s_own, s_x, g_z, h_y, inc, t_rows, t_out, t_in,
    xd, qd, yd, ynd, dec_d, lam_d, wgt_d, wc_d, once_d, run_d, loc_d, pw_d,
    gb, gin, gd, acc,
    loc_sem, x_sem, z_send, z_recv, y_send, y_recv, far_send, far_recv, t_send, t_recv,
    wsib_sem, wi_send, wi_recv, wn_send, wn_recv, wa_send, wa_recv, g_send, g_recv,
):
    chans, toks = kv_v.shape
    modes = dec_v.shape[0]
    groups = chans // LANES
    near_groups = groups // 2
    far_chans = chans // 2
    far_groups = groups - near_groups
    sub_len = toks // SUBS
    out_toks, cols = out_ref.shape
    far_len = out_toks // SUBS
    seq = float(toks * NY * NZ * NX)
    block = float(toks)
    f32, bf16 = jnp.float32, jnp.bfloat16

    ctx, tp = lax.axis_index("ctx"), lax.axis_index("tp")
    x_hi = lax.rem(ctx, NX)
    z = lax.rem(ctx // NX, NZ)
    y = ctx // (NX * NZ)
    x_lo, core = tp // 2, lax.rem(tp, 2)

    def ctx_of(yy, zz, xx):
        return (yy * NZ + zz) * NX + xx

    partner_tp = [tp, x_lo * 2 + (1 - core), (1 - x_lo) * 2 + core, (1 - x_lo) * 2 + (1 - core)]
    to_x = {"ctx": ctx_of(y, z, 1 - x_hi), "tp": tp}
    to_z = [{"ctx": ctx_of(y, lax.rem(z + j, NZ), x_hi), "tp": tp} for j in range(NZ)]
    to_y = [{"ctx": ctx_of(lax.rem(y + j, NY), z, x_hi), "tp": tp} for j in range(NY)]
    to_tp = [{"ctx": ctx, "tp": t} for t in partner_tp]
    to_wrap = {"ctx": ctx_of(y, z, 1 - x_hi), "tp": partner_tp[2]}

    loads = [
        pltpu.make_async_copy(dec_hbm, dec_v, loc_sem.at[0]),
        pltpu.make_async_copy(res_hbm, res_v, loc_sem.at[1]),
        pltpu.make_async_copy(q_hbm, q_v, loc_sem.at[2]),
        pltpu.make_async_copy(w_hbm, wf.at[0], loc_sem.at[3]),
    ]
    kv_rows = [pl.ds(g * LANES, LANES) for g in range(groups)]
    kv_loads = [
        pltpu.make_async_copy(kv_hbm.at[rows], kv_v.at[rows], loc_sem.at[4 + g]) for g, rows in enumerate(kv_rows)
    ]
    for load in loads[:2] + kv_loads + loads[2:]:
        load.start()

    barrier = pltpu.get_barrier_semaphore()
    partners = [to_x] + to_z[1:] + to_y[1:] + to_tp[1:] + [to_wrap]
    for partner in partners:
        pl.semaphore_signal(barrier, inc=1, device_id=partner, device_id_type=MESH)

    def remote(src, dst, send, recv, to):
        return pltpu.make_async_remote_copy(
            src_ref=src, dst_ref=dst, send_sem=send, recv_sem=recv, device_id=to, device_id_type=MESH
        )

    far_rows, far_cols = pl.ds(far_chans, far_chans), pl.ds(near_groups * LANES, far_chans)
    far = []
    for r in range(1, NTP):
        there = pl.ds(pl.multiple_of(partner_tp[r] * out_toks, out_toks), out_toks)
        pairs = [
            (kv_hbm.at[pl.ds(far_chans + g * LANES, LANES), there], kv_far.at[r - 1, pl.ds(g * LANES, LANES)])
            for g in range(far_groups)
        ] + [
            (dec_hbm.at[:, far_cols], dec_far.at[r - 1]), (res_hbm.at[:, far_cols], res_far.at[r - 1]),
            (q_hbm.at[far_rows, there], q_far.at[r - 1]),
        ]
        far.append(
            [
                remote(src, dst, far_send.at[r - 1, i], far_recv.at[r - 1, i], to_tp[r])
                for i, (src, dst) in enumerate(pairs)
            ]
        )
    f_dec, f_res, f_q = far_groups, far_groups + 1, far_groups + 2

    for i, array in ((f_dec, dec_far), (f_res, res_far)):
        far[2][i] = remote(array.at[1], array.at[2], far_send.at[2, i], far_recv.at[2, i], to_tp[1])

    quarter = chans // 4
    piece = quarter // W_PIECES

    def rows_of(which, first, count):
        return pl.ds(pl.multiple_of(which * quarter + first * piece, 16), count * piece)

    w_sib = remote(w_hbm, wf.at[1], wsib_sem.at[0], wsib_sem.at[1], to_tp[1])
    holds = []
    for mine in (lax.rem(z + 2 * y, 4), lax.rem(y + 2 * z, 4)):
        holds.append((lax.rem(mine + 3, 4), lax.rem(mine + 1, 4), lax.rem(mine + 2, 4), mine))
    w_import, w_on, w_got = [], [], []
    for i in range(W_PIECES):
        by_y = i // (W_PIECES // 2)
        turn_to, half_to = ((to_z, to_y), (to_y, to_z))[by_y]
        ways = (turn_to[1], turn_to[NZ - 1], half_to[1 if i % 2 == 0 else NY - 1])
        mine = rows_of(holds[by_y][3], i, 1)
        w_import.append(remote(w_hbm.at[mine], wf.at[2, mine], wi_send.at[i], wi_recv.at[i], to_wrap))
        w_on.append([])
        w_got.append([])
        for way, to in enumerate(ways):
            theirs = rows_of(holds[by_y][way], i, 1)
            w_on[i].append(remote(wf.at[2, mine], wf.at[2, mine], wn_send.at[way, i], wn_recv.at[way, i], to))
            w_got[i].append(remote(wf.at[2, theirs], wf.at[2, theirs], wn_send.at[way, i], wn_recv.at[way, i], to))
    w_across = []
    for u, (first, count) in enumerate(W_UNITS):
        w_across.append([])
        for way, which in enumerate(holds[first // (W_PIECES // 2)]):
            rows = rows_of(which, first, count)
            w_across[u].append(
                remote(wf.at[2, rows], wf.at[3, rows], wa_send.at[way, u], wa_recv.at[way, u], to_tp[1])
            )

    def on_by_y(i):
        for way in ((2,), (0, 1))[i // (W_PIECES // 2)]:
            w_on[i][way].start()

    def hand_on(i):
        w_import[i].wait_recv()
        for way in ((0, 1), (2,))[i // (W_PIECES // 2)]:
            w_on[i][way].start()
        for u, (first, count) in enumerate(W_UNITS):
            if i == first + count - 1:
                w_across[u][3].start()

    def hand_across(u):
        first, count = W_UNITS[u]
        for way in range(3):
            for i in range(first, first + count):
                w_got[i][way].wait_recv()
            w_across[u][way].start()

    def coefficients(dec, res, length, *where):
        refs, where = where[0], where[1:]
        dec_to, lam_to, wgt_to, wc_to, once_to, run_to = refs
        wgt = res * jnp.sqrt(one_minus_exp(2.0 * dec))
        once = one_minus_exp(seq * dec)
        run = jnp.exp(-float(length) * dec)
        dec_to[where] = dec
        lam_to[where] = jnp.exp(-dec)
        wgt_to[where] = wgt
        wc_to[where] = wgt * once
        once_to[where] = once
        for i in range(3):
            run_to[(i, *where)] = run
            run = run * run

    near_coefs = (dec_t, lam_t, wgt_t, wc_t, once_t, run_t)
    far_coefs = (dec_d, lam_d, wgt_d, wc_d, once_d, run_d)
    loads[0].wait()
    loads[1].wait()
    for g in range(groups):
        lanes = slice(g * LANES, (g + 1) * LANES)
        coefficients(dec_v[:, lanes], res_v[:, lanes], sub_len, near_coefs, g)

    def turn_near(g):
        kv_loads[g].wait()
        for s in range(SUBS):
            turned = kv_v[g * LANES:(g + 1) * LANES, s * sub_len:(s + 1) * sub_len].T.astype(f32)
            xs[g, pl.ds(s, sub_len, stride=SUBS), :] = turned

    row = lax.broadcasted_iota(jnp.int32, (SUBS, LANES), 0)
    row_f = row.astype(f32)

    def wide(ref, *where):
        *lead, m = where
        return jnp.broadcast_to(ref[(*lead, slice(m, m + 1), slice(None))], (SUBS, LANES))

    zeros = tuple(jnp.zeros((SUBS, LANES), f32) for _ in range(modes))

    def first_pass(g):
        lam = [wide(lam_t, g, m) for m in range(modes)]

        def step(t, states):
            x = xs[g, at(t), :]
            return tuple(l * u + x for l, u in zip(lam, states))

        states = lax.fori_loop(0, sub_len, step, zeros, unroll=UNROLL)
        for m in range(modes):
            ends[g, m] = states[m]
            decayed = states[m] * jnp.exp(-wide(dec_t, g, m) * ((SUBS - 1 - row_f) * float(sub_len)))
            s_own[g, m:m + 1, :] = jnp.sum(decayed, axis=0, keepdims=True)

    for g in range(groups // 2):
        turn_near(g)
        first_pass(g)
    pl.semaphore_wait(barrier, len(partners))
    w_import[W_ORDER[0]].start()
    far[1][0].start()
    for copy in far[0]:
        copy.start()
    w_sib.start()
    for g in range(groups // 2, groups):
        turn_near(g)
        first_pass(g)

    send_x = remote(s_own, s_x, x_sem.at[0], x_sem.at[1], to_x)
    send_x.start()
    rest = (far[1][1], far[1][f_dec], far[1][f_res], far[2][0], far[2][1], far[1][f_q], far[2][f_q])
    for i, copy in zip(W_ORDER[1:], rest):
        w_import[i].start()
        copy.start()

    def run_starts(states, coefs, length, *where):
        dec_of, _, _, _, once_of, run_of = coefs
        state = shift_rows(states * wide(once_of, *where), 1, row)
        for i, by in enumerate((1, 2, 4)):
            state += wide(run_of, i, *where) * shift_rows(state, by, row)
        return state, jnp.exp(wide(dec_of, *where) * (row_f * -float(length)))

    def prepare(g, carry, weighted):
        for m in range(modes):
            state, decay = run_starts(ends[g, m], near_coefs, sub_len, g, m)
            wgt = wide(wgt_t, g, m) if weighted else 1.0
            loc[g, m], pw[g, m] = wgt * state, wgt * decay
        return carry

    def second_pass(g):
        lam = [wide(lam_t, g, m) for m in range(modes)]
        gain = [wide(wc_t, g, m) for m in range(modes)]

        def step(t, states):
            x = xs[g, at(t), :]
            states = tuple(l * u + x for l, u in zip(lam, states))
            ys[g, at(t), :] = tree_sum([c * u for c, u in zip(gain, states)])
            return states

        lax.fori_loop(0, sub_len, step, zeros, unroll=UNROLL)

    own_toks = pl.ds(pl.multiple_of(tp * out_toks, out_toks), out_toks)

    def far_pass(r):
        if r:
            for i in (0, 1) if r == 2 else (0, 1, f_dec, f_res):
                far[r - 1][i].wait_recv()
        halves = out_toks // LANES
        for g in range(far_groups):
            lanes = slice(g * LANES, (g + 1) * LANES)
            if r:
                dec, res = dec_far[r - 1, :, lanes], res_far[r - 1, :, lanes]
            else:
                own = slice(far_chans + g * LANES, far_chans + (g + 1) * LANES)
                dec, res = dec_v[:, own], res_v[:, own]
            coefficients(dec, res, far_len, far_coefs, r, g)
            for h in range(halves):
                if r:
                    tile = kv_far[r - 1, lanes, h * LANES:(h + 1) * LANES]
                else:
                    tile = kv_v[own, pl.ds(pl.multiple_of(tp * out_toks + h * LANES, LANES), LANES)]
                turned = tile.T.astype(f32)
                for s in range(SUBS // halves):
                    xd[r, g, pl.ds(h * (SUBS // halves) + s, far_len, stride=SUBS), :] = (
                        turned[s * far_len:(s + 1) * far_len]
                    )

        def of_group(g, carry):
            lam = [wide(lam_d, r, g, m) for m in range(modes)]
            gain = [wide(wc_d, r, g, m) for m in range(modes)]

            def step(t, states):
                x = xd[r, g, at(t), :]
                states = tuple(l * u + x for l, u in zip(lam, states))
                yd[r, g, at(t), :] = tree_sum([c * u for c, u in zip(gain, states)])
                return states

            states = lax.fori_loop(0, far_len, step, zeros, unroll=UNROLL)
            for m in range(modes):
                state, decay = run_starts(states[m], far_coefs, far_len, r, g, m)
                wgt = wide(wgt_d, r, g, m)
                loc_d[r, g, m], pw_d[r, g, m] = wgt * state, wgt * decay
            return carry

        lax.fori_loop(0, far_groups, of_group, 0)

    def turn_query(r):
        for g in range(far_groups):
            for h in range(out_toks // LANES):
                if r:
                    tile = q_far[r - 1, g * LANES:(g + 1) * LANES, h * LANES:(h + 1) * LANES]
                else:
                    own = slice(far_chans + g * LANES, far_chans + (g + 1) * LANES)
                    tile = q_v[own, pl.ds(pl.multiple_of(tp * out_toks + h * LANES, LANES), LANES)]
                qd[r, g, h * LANES:(h + 1) * LANES, :] = tile.T.astype(f32)

    dec = dec_t[...]
    lam1 = jnp.exp(-block * dec)
    second_pass(0)
    second_pass(1)
    far_pass(0)
    lax.fori_loop(0, near_groups, lambda g, carry: prepare(g, carry, True), 0)
    lax.fori_loop(near_groups, groups, lambda g, carry: prepare(g, carry, False), 0)
    send_x.wait_recv()
    same, across = s_own[...], s_x[...]
    g_z[0] = jnp.where(x_hi == 0, across + lam1 * same, same + lam1 * across)
    sends_z = [remote(g_z.at[0], g_z.at[j], z_send.at[j], z_recv.at[j], to_z[j]) for j in range(1, NZ)]
    for send in sends_z:
        send.start()

    loads[2].wait()
    for g in range(near_groups):
        for s in range(SUBS):
            turned = q_v[g * LANES:(g + 1) * LANES, s * sub_len:(s + 1) * sub_len].T.astype(f32)
            qs[g, s * sub_len:(s + 1) * sub_len, :] = turned
    turn_query(0)
    hand_on(W_ORDER[0])
    on_by_y(W_ORDER[0])
    far_pass(1)
    far[1][f_dec].wait_recv()
    far[1][f_res].wait_recv()
    far[2][f_dec].start()
    far[2][f_res].start()
    hand_on(W_ORDER[1])
    on_by_y(W_ORDER[1])
    far_pass(2)
    hand_on(W_ORDER[2])
    after = [(NZ - 1 - lax.rem(z + NZ - j, NZ)).astype(f32) * (block * NX) for j in range(NZ)]
    by_total = [jnp.exp(-a * dec) for a in after]
    by_before = [None] + [
        jnp.where(z >= j, jnp.exp(-(block * NX * (j - 1)) * dec), 0.0) for j in range(1, NZ)
    ]
    for send in sends_z:
        send.wait_recv()
    total = by_total[0] * g_z[0]
    before = jnp.zeros_like(dec)
    for j in range(1, NZ):
        part = g_z[j]
        total += by_total[j] * part
        before += by_before[j] * part
    h_y[0] = total
    sends_y = [remote(h_y.at[0], h_y.at[j], y_send.at[j], y_recv.at[j], to_y[j]) for j in range(1, NY)]
    for send in sends_y:
        send.start()

    on_by_y(W_ORDER[2])
    far_pass(3)
    for i in W_ORDER[3:5]:
        hand_on(i)
        on_by_y(i)

    start_z = z.astype(f32) * (block * NX)
    by_y = [jnp.exp(-(block * NX * NZ * (j - 1) + start_z) * dec) for j in range(1, NY + 1)]
    once = once_t[...]
    before = once * before
    beside = once * s_x[...]
    for send in sends_y:
        send.wait_recv()
    came = before
    for j in range(1, NY + 1):
        came += by_y[j - 1] * h_y[j % NY]
    inc[...] = jnp.where(x_hi == 0, came, lam1 * came + beside)

    for g in range(far_groups):
        for m in range(modes):
            all_g = near_groups + g
            t_rows[g, m * SUBS:(m + 1) * SUBS, :] = loc[all_g, m] + pw[all_g, m] * wide(inc, all_g, m)
        for k in range(NTP):
            t_out[k, g] = t_rows[g, pl.ds(k * (SUBS // NTP), modes, stride=SUBS), :]
    t_sends = [
        remote(t_out.at[partner_tp[r]], t_in.at[r - 1], t_send.at[r - 1], t_recv.at[r - 1], to_tp[r])
        for r in range(1, NTP)
    ]
    for r in (2, 3, 1):
        t_sends[r - 1].start()
    for i in W_ORDER[5:7]:
        hand_on(i)
        on_by_y(i)

    g_sends = [
        [
            remote(
                gb.at[g, pl.ds(pl.multiple_of(partner_tp[r] * out_toks, out_toks), out_toks)],
                gin.at[r - 1, g], g_send.at[r - 1, g], g_recv.at[r - 1, g], to_tp[r],
            )
            for r in range(1, NTP)
        ]
        for g in range(near_groups)
    ]
    for g in range(near_groups):
        start = [loc[g, m] + pw[g, m] * wide(inc, g, m) for m in range(modes)]
        lam = [wide(lam_t, g, m) for m in range(modes)]

        def step(t, states):
            states = tuple(l * u for l, u in zip(lam, states))
            yn[g, pl.ds(t, SUBS, stride=sub_len), :] = ys[g, at(t), :] + tree_sum(list(states))
            return states

        lax.fori_loop(0, sub_len, step, tuple(start), unroll=UNROLL)
        gb[g] = (qs[g] * yn[g].astype(bf16).astype(f32)).astype(bf16)
        for r in (2, 3, 1):
            g_sends[g][r - 1].start()
        if g == 0:
            hand_on(W_ORDER[7])
            on_by_y(W_ORDER[7])

    def far_correct(r):
        if r:
            t_sends[r - 1].wait_recv()
            far[r - 1][f_q].wait_recv()
            turn_query(r)

        def of_group(g, carry):
            came = (lambda m: wide(t_in, r - 1, g, m)) if r else (lambda m: wide(t_out, tp, g, m))
            start = [loc_d[r, g, m] + pw_d[r, g, m] * came(m) for m in range(modes)]
            lam = [wide(lam_d, r, g, m) for m in range(modes)]

            def step(t, states):
                states = tuple(l * u for l, u in zip(lam, states))
                ynd[pl.ds(t, SUBS, stride=far_len), :] = yd[r, g, at(t), :] + tree_sum(list(states))
                return states

            lax.fori_loop(0, far_len, step, tuple(start), unroll=UNROLL)
            gd[r, g] = (qd[r, g] * ynd[...].astype(bf16).astype(f32)).astype(bf16)
            return carry

        lax.fori_loop(0, far_groups, of_group, 0)

    far_correct(0)
    hand_across(0)
    far_correct(1)
    hand_across(3)
    far_correct(2)
    hand_across(1)
    hand_across(4)
    far_correct(3)
    hand_across(2)
    hand_across(5)

    loads[3].wait()
    w_sib.wait_recv()
    for g in range(near_groups):
        g_sends[g][0].wait_recv()
    lhs = jnp.concatenate(
        [gb[g, own_toks, :] for g in range(near_groups)] + [gd[0, g] for g in range(far_groups)]
        + [gin[0, g] for g in range(near_groups)] + [gd[1, g] for g in range(far_groups)], axis=1
    )
    acc[...] = jnp.dot(lhs, jnp.concatenate([wf[0], wf[1]], axis=0), preferred_element_type=f32)
    for per_piece in w_across:
        for copy in per_piece:
            copy.wait_recv()
    lhs = jnp.concatenate([gd[r, g] for r in (2, 3) for g in range(far_groups)], axis=1)
    rhs = jnp.concatenate([wf[r, far_chans:, :] for r in (2, 3)], axis=0)
    acc[...] += jnp.dot(lhs, rhs, preferred_element_type=f32)
    for g in range(near_groups):
        rows = slice(g * LANES, (g + 1) * LANES)
        g_sends[g][1].wait_recv()
        g_sends[g][2].wait_recv()
        lhs = jnp.concatenate([gin[1, g], gin[2, g]], axis=1)
        rhs = jnp.concatenate([wf[2, rows, :], wf[3, rows, :]], axis=0)
        part = acc[...] + jnp.dot(lhs, rhs, preferred_element_type=f32)
        if g == near_groups - 1:
            out_ref[...] = part.astype(bf16)
        else:
            acc[...] = part

    for copy in [w_sib, send_x] + sends_z + sends_y + t_sends + w_import:
        copy.wait_send()
    for family in (far, w_on, w_across, g_sends):
        for part in family:
            for copy in part:
                copy.wait_send()


def shards(kv_product, query, decay_rate, residue, out_weight):
    chans, toks = kv_product.shape
    modes = decay_rate.shape[1]
    cols = out_weight.shape[1]
    groups = chans // LANES
    near, far = groups // 2, groups - groups // 2
    out_toks = toks // NTP
    bf16, f32 = jnp.bfloat16, jnp.float32
    small = (groups, modes, LANES)
    runs = (groups, modes, SUBS, LANES)
    far_block = (NTP - 1, chans // 2, out_toks)
    far_coef = (NTP - 1, modes, chans // 2)
    pieces = W_PIECES
    vmem, dma = pltpu.VMEM, pltpu.SemaphoreType.DMA
    operands = (kv_product, query, decay_rate.T, residue.T, out_weight)
    return pl.pallas_call(
        kernel,
        out_shape=jax.ShapeDtypeStruct((out_toks, cols), bf16),
        in_specs=[pl.BlockSpec(memory_space=pltpu.HBM)] * 5,
        out_specs=pl.BlockSpec(memory_space=pltpu.VMEM),
        scratch_shapes=[
            vmem((chans, toks), bf16), vmem((chans, toks), bf16), vmem((modes, chans), f32), vmem((modes, chans), f32),
            vmem(far_block, bf16), vmem(far_block, bf16), vmem(far_coef, f32), vmem(far_coef, f32),
            vmem((NTP, chans, cols), bf16),
            vmem((groups, toks, LANES), f32), vmem((near, toks, LANES), f32),
            vmem((near, toks, LANES), f32), vmem((near, toks, LANES), f32),
            vmem(small, f32), vmem(small, f32), vmem(small, f32), vmem(small, f32), vmem(small, f32),
            vmem((3,) + small, f32),
            vmem(runs, f32), vmem(runs, f32), vmem(runs, f32),
            vmem(small, f32), vmem(small, f32), vmem((NZ,) + small, f32), vmem((NY,) + small, f32), vmem(small, f32),
            vmem((far, modes * SUBS, LANES), f32),
            vmem((NTP, far, modes, LANES), f32), vmem((NTP - 1, far, modes, LANES), f32),
            vmem((NTP, far, out_toks, LANES), f32), vmem((NTP, far, out_toks, LANES), f32),
            vmem((NTP, far, out_toks, LANES), f32), vmem((out_toks, LANES), f32),
            vmem((NTP, far, modes, LANES), f32), vmem((NTP, far, modes, LANES), f32),
            vmem((NTP, far, modes, LANES), f32), vmem((NTP, far, modes, LANES), f32),
            vmem((NTP, far, modes, LANES), f32), vmem((3, NTP, far, modes, LANES), f32),
            vmem((NTP, far, modes, SUBS, LANES), f32), vmem((NTP, far, modes, SUBS, LANES), f32),
            vmem((near, toks, LANES), bf16), vmem((NTP - 1, near, out_toks, LANES), bf16),
            vmem((NTP, far, out_toks, LANES), bf16), vmem((out_toks, cols), f32),
            dma((4 + groups,)), dma((2,)), dma((NZ,)), dma((NZ,)), dma((NY,)), dma((NY,)),
            dma((NTP - 1, far + 3)), dma((NTP - 1, far + 3)), dma((NTP - 1,)), dma((NTP - 1,)),
            dma((2,)), dma((pieces,)), dma((pieces,)), dma((3, pieces)), dma((3, pieces)),
            dma((4, len(W_UNITS))), dma((4, len(W_UNITS))), dma((NTP - 1, near)), dma((NTP - 1, near)),
        ],
        compiler_params=pltpu.CompilerParams(
            collective_id=0, has_side_effects=True, vmem_limit_bytes=50 * 1024 * 1024
        ),
        cost_estimate=pl.CostEstimate(
            flops=2 * out_toks * cols * chans * NTP, bytes_accessed=6 * 1024 * 1024, transcendentals=0
        ),
    )(*(pltpu.with_memory_space_constraint(a, pltpu.HBM) for a in operands))


def solution(mesh):
    in_specs = (P("tp", "ctx"), P("tp", "ctx"), P("tp", None), P("tp", None), P("tp", None))
    out_specs = P(("ctx", "tp"), None)
    return jax.shard_map(shards, mesh=mesh, in_specs=in_specs, out_specs=out_specs, check_vma=False)
```

```python
import jax
import jax.numpy as jnp
from jax import lax
from jax.experimental import pallas as pl
from jax.experimental.pallas import tpu as pltpu
from jax.sharding import PartitionSpec as P

NY, NZ, NX, NTP = 4, 4, 2, 4
SUBS, LANES = 8, 128
W_PIECES = 8
W_ORDER = (0, 4, 1, 5, 2, 6, 3, 7)
W_UNITS = ((0, 2), (2, 1), (3, 1), (4, 2), (6, 1), (7, 1))
UNROLL = 32
MESH = pl.DeviceIdType.MESH


def one_minus_exp(z):
    series = jnp.ones_like(z)
    for n in range(10, 1, -1):
        series = 1.0 - (z * (1.0 / n)) * series
    return jnp.where(z < 0.5, z * series, 1.0 - jnp.exp(-z))


def shift_rows(value, by, row):
    return jnp.where(row >= by, pltpu.roll(value, by, 0), 0.0)


def tree_sum(terms):
    while len(terms) > 1:
        terms = [a + b for a, b in zip(terms[::2], terms[1::2])]
    return terms[0]


def at(t):
    return pl.ds(pl.multiple_of(t * SUBS, SUBS), SUBS)


def kernel(
    kv_hbm, q_hbm, dec_hbm, res_hbm, w_hbm, out_ref,
    kv_v, q_v, dec_v, res_v, kv_far, q_far, dec_far, res_far, wf,
    xs, qs, ys, yn, dec_t, lam_t, wgt_t, wc_t, once_t, run_t, ends, loc, pw,
    s_own, s_x, g_z, h_y, inc, t_rows, t_out, t_in,
    xd, qd, yd, ynd, dec_d, lam_d, wgt_d, wc_d, once_d, run_d, loc_d, pw_d,
    gb, gin, gd, acc,
    loc_sem, x_sem, z_send, z_recv, y_send, y_recv, far_send, far_recv, t_send, t_recv,
    wsib_sem, wi_send, wi_recv, wn_send, wn_recv, wa_send, wa_recv, g_send, g_recv,
):
    chans, toks = kv_v.shape
    modes = dec_v.shape[0]
    groups = chans // LANES
    near_groups = groups // 2
    far_chans = chans // 2
    far_groups = groups - near_groups
    sub_len = toks // SUBS
    out_toks, cols = out_ref.shape
    far_len = out_toks // SUBS
    seq = float(toks * NY * NZ * NX)
    block = float(toks)
    f32, bf16 = jnp.float32, jnp.bfloat16

    ctx, tp = lax.axis_index("ctx"), lax.axis_index("tp")
    x_hi = lax.rem(ctx, NX)
    z = lax.rem(ctx // NX, NZ)
    y = ctx // (NX * NZ)
    x_lo, core = tp // 2, lax.rem(tp, 2)

    def ctx_of(yy, zz, xx):
        return (yy * NZ + zz) * NX + xx

    partner_tp = [tp, x_lo * 2 + (1 - core), (1 - x_lo) * 2 + core, (1 - x_lo) * 2 + (1 - core)]
    to_x = {"ctx": ctx_of(y, z, 1 - x_hi), "tp": tp}
    to_z = [{"ctx": ctx_of(y, lax.rem(z + j, NZ), x_hi), "tp": tp} for j in range(NZ)]
    to_y = [{"ctx": ctx_of(lax.rem(y + j, NY), z, x_hi), "tp": tp} for j in range(NY)]
    to_tp = [{"ctx": ctx, "tp": t} for t in partner_tp]
    to_wrap = {"ctx": ctx_of(y, z, 1 - x_hi), "tp": partner_tp[2]}

    loads = [
        pltpu.make_async_copy(dec_hbm, dec_v, loc_sem.at[0]),
        pltpu.make_async_copy(res_hbm, res_v, loc_sem.at[1]),
        pltpu.make_async_copy(q_hbm, q_v, loc_sem.at[2]),
        pltpu.make_async_copy(w_hbm, wf.at[0], loc_sem.at[3]),
    ]
    kv_rows = [pl.ds(g * LANES, LANES) for g in range(groups)]
    kv_loads = [
        pltpu.make_async_copy(kv_hbm.at[rows], kv_v.at[rows], loc_sem.at[4 + g]) for g, rows in enumerate(kv_rows)
    ]
    for load in loads[:2] + kv_loads + loads[2:]:
        load.start()

    barrier = pltpu.get_barrier_semaphore()
    partners = [to_x] + to_z[1:] + to_y[1:] + to_tp[1:] + [to_wrap]
    for partner in partners:
        pl.semaphore_signal(barrier, inc=1, device_id=partner, device_id_type=MESH)

    def remote(src, dst, send, recv, to):
        return pltpu.make_async_remote_copy(
            src_ref=src, dst_ref=dst, send_sem=send, recv_sem=recv, device_id=to, device_id_type=MESH
        )

    far_rows, far_cols = pl.ds(far_chans, far_chans), pl.ds(near_groups * LANES, far_chans)
    far = []
    for r in range(1, NTP):
        there = pl.ds(pl.multiple_of(partner_tp[r] * out_toks, out_toks), out_toks)
        pairs = [
            (kv_hbm.at[pl.ds(far_chans + g * LANES, LANES), there], kv_far.at[r - 1, pl.ds(g * LANES, LANES)])
            for g in range(far_groups)
        ] + [
            (dec_hbm.at[:, far_cols], dec_far.at[r - 1]), (res_hbm.at[:, far_cols], res_far.at[r - 1]),
            (q_hbm.at[far_rows, there], q_far.at[r - 1]),
        ]
        far.append(
            [
                remote(src, dst, far_send.at[r - 1, i], far_recv.at[r - 1, i], to_tp[r])
                for i, (src, dst) in enumerate(pairs)
            ]
        )
    f_dec, f_res, f_q = far_groups, far_groups + 1, far_groups + 2

    for i, array in ((f_dec, dec_far), (f_res, res_far)):
        far[2][i] = remote(array.at[1], array.at[2], far_send.at[2, i], far_recv.at[2, i], to_tp[1])

    quarter = chans // 4
    piece = quarter // W_PIECES

    def rows_of(which, first, count):
        return pl.ds(pl.multiple_of(which * quarter + first * piece, 16), count * piece)

    w_sib = remote(w_hbm, wf.at[1], wsib_sem.at[0], wsib_sem.at[1], to_tp[1])
    holds = []
    for mine in (lax.rem(z + 2 * y, 4), lax.rem(y + 2 * z, 4)):
        holds.append((lax.rem(mine + 3, 4), lax.rem(mine + 1, 4), lax.rem(mine + 2, 4), mine))
    w_import, w_on, w_got = [], [], []
    for i in range(W_PIECES):
        by_y = i // (W_PIECES // 2)
        turn_to, half_to = ((to_z, to_y), (to_y, to_z))[by_y]
        ways = (turn_to[1], turn_to[NZ - 1], half_to[1 if i % 2 == 0 else NY - 1])
        mine = rows_of(holds[by_y][3], i, 1)
        w_import.append(remote(w_hbm.at[mine], wf.at[2, mine], wi_send.at[i], wi_recv.at[i], to_wrap))
        w_on.append([])
        w_got.append([])
        for way, to in enumerate(ways):
            theirs = rows_of(holds[by_y][way], i, 1)
            w_on[i].append(remote(wf.at[2, mine], wf.at[2, mine], wn_send.at[way, i], wn_recv.at[way, i], to))
            w_got[i].append(remote(wf.at[2, theirs], wf.at[2, theirs], wn_send.at[way, i], wn_recv.at[way, i], to))
    w_across = []
    for u, (first, count) in enumerate(W_UNITS):
        w_across.append([])
        for way, which in enumerate(holds[first // (W_PIECES // 2)]):
            rows = rows_of(which, first, count)
            w_across[u].append(
                remote(wf.at[2, rows], wf.at[3, rows], wa_send.at[way, u], wa_recv.at[way, u], to_tp[1])
            )

    def on_by_y(i):
        for way in ((2,), (0, 1))[i // (W_PIECES // 2)]:
            w_on[i][way].start()

    def hand_on(i):
        w_import[i].wait_recv()
        for way in ((0, 1), (2,))[i // (W_PIECES // 2)]:
            w_on[i][way].start()
        for u, (first, count) in enumerate(W_UNITS):
            if i == first + count - 1:
                w_across[u][3].start()

    def hand_across(u):
        first, count = W_UNITS[u]
        for way in range(3):
            for i in range(first, first + count):
                w_got[i][way].wait_recv()
            w_across[u][way].start()

    def coefficients(dec, res, length, *where):
        refs, where = where[0], where[1:]
        dec_to, lam_to, wgt_to, wc_to, once_to, run_to = refs
        wgt = res * jnp.sqrt(one_minus_exp(2.0 * dec))
        once = one_minus_exp(seq * dec)
        run = jnp.exp(-float(length) * dec)
        dec_to[where] = dec
        lam_to[where] = jnp.exp(-dec)
        wgt_to[where] = wgt
        wc_to[where] = wgt * once
        once_to[where] = once
        for i in range(3):
            run_to[(i, *where)] = run
            run = run * run

    near_coefs = (dec_t, lam_t, wgt_t, wc_t, once_t, run_t)
    far_coefs = (dec_d, lam_d, wgt_d, wc_d, once_d, run_d)
    loads[0].wait()
    loads[1].wait()
    for g in range(groups):
        lanes = slice(g * LANES, (g + 1) * LANES)
        coefficients(dec_v[:, lanes], res_v[:, lanes], sub_len, near_coefs, g)

    def turn_near(g):
        kv_loads[g].wait()
        for s in range(SUBS):
            turned = kv_v[g * LANES:(g + 1) * LANES, s * sub_len:(s + 1) * sub_len].T.astype(f32)
            xs[g, pl.ds(s, sub_len, stride=SUBS), :] = turned

    row = lax.broadcasted_iota(jnp.int32, (SUBS, LANES), 0)
    row_f = row.astype(f32)

    def wide(ref, *where):
        *lead, m = where
        return jnp.broadcast_to(ref[(*lead, slice(m, m + 1), slice(None))], (SUBS, LANES))

    zeros = tuple(jnp.zeros((SUBS, LANES), f32) for _ in range(modes))

    def first_pass(g):
        lam = [wide(lam_t, g, m) for m in range(modes)]

        def step(t, states):
            x = xs[g, at(t), :]
            return tuple(l * u + x for l, u in zip(lam, states))

        states = lax.fori_loop(0, sub_len, step, zeros, unroll=UNROLL)
        for m in range(modes):
            ends[g, m] = states[m]
            decayed = states[m] * jnp.exp(-wide(dec_t, g, m) * ((SUBS - 1 - row_f) * float(sub_len)))
            s_own[g, m:m + 1, :] = jnp.sum(decayed, axis=0, keepdims=True)

    for g in range(groups // 2):
        turn_near(g)
        first_pass(g)
    pl.semaphore_wait(barrier, len(partners))
    w_import[W_ORDER[0]].start()
    far[1][0].start()
    for copy in far[0]:
        copy.start()
    w_sib.start()
    for g in range(groups // 2, groups):
        turn_near(g)
        first_pass(g)

    send_x = remote(s_own, s_x, x_sem.at[0], x_sem.at[1], to_x)
    send_x.start()
    rest = (far[1][1], far[1][f_dec], far[1][f_res], far[2][0], far[2][1], far[1][f_q], far[2][f_q])
    for i, copy in zip(W_ORDER[1:], rest):
        w_import[i].start()
        copy.start()

    def run_starts(states, coefs, length, *where):
        dec_of, _, _, _, once_of, run_of = coefs
        state = shift_rows(states * wide(once_of, *where), 1, row)
        for i, by in enumerate((1, 2, 4)):
            state += wide(run_of, i, *where) * shift_rows(state, by, row)
        return state, jnp.exp(wide(dec_of, *where) * (row_f * -float(length)))

    def prepare(g, carry, weighted):
        for m in range(modes):
            state, decay = run_starts(ends[g, m], near_coefs, sub_len, g, m)
            wgt = wide(wgt_t, g, m) if weighted else 1.0
            loc[g, m], pw[g, m] = wgt * state, wgt * decay
        return carry

    def second_pass(g):
        lam = [wide(lam_t, g, m) for m in range(modes)]
        gain = [wide(wc_t, g, m) for m in range(modes)]

        def step(t, states):
            x = xs[g, at(t), :]
            states = tuple(l * u + x for l, u in zip(lam, states))
            ys[g, at(t), :] = tree_sum([c * u for c, u in zip(gain, states)])
            return states

        lax.fori_loop(0, sub_len, step, zeros, unroll=UNROLL)

    own_toks = pl.ds(pl.multiple_of(tp * out_toks, out_toks), out_toks)

    def far_pass(r):
        if r:
            for i in (0, 1) if r == 2 else (0, 1, f_dec, f_res):
                far[r - 1][i].wait_recv()
        halves = out_toks // LANES
        for g in range(far_groups):
            lanes = slice(g * LANES, (g + 1) * LANES)
            if r:
                dec, res = dec_far[r - 1, :, lanes], res_far[r - 1, :, lanes]
            else:
                own = slice(far_chans + g * LANES, far_chans + (g + 1) * LANES)
                dec, res = dec_v[:, own], res_v[:, own]
            coefficients(dec, res, far_len, far_coefs, r, g)
            for h in range(halves):
                if r:
                    tile = kv_far[r - 1, lanes, h * LANES:(h + 1) * LANES]
                else:
                    tile = kv_v[own, pl.ds(pl.multiple_of(tp * out_toks + h * LANES, LANES), LANES)]
                turned = tile.T.astype(f32)
                for s in range(SUBS // halves):
                    xd[r, g, pl.ds(h * (SUBS // halves) + s, far_len, stride=SUBS), :] = (
                        turned[s * far_len:(s + 1) * far_len]
                    )

        def of_group(g, carry):
            lam = [wide(lam_d, r, g, m) for m in range(modes)]
            gain = [wide(wc_d, r, g, m) for m in range(modes)]

            def step(t, states):
                x = xd[r, g, at(t), :]
                states = tuple(l * u + x for l, u in zip(lam, states))
                yd[r, g, at(t), :] = tree_sum([c * u for c, u in zip(gain, states)])
                return states

            states = lax.fori_loop(0, far_len, step, zeros, unroll=UNROLL)
            for m in range(modes):
                state, decay = run_starts(states[m], far_coefs, far_len, r, g, m)
                wgt = wide(wgt_d, r, g, m)
                loc_d[r, g, m], pw_d[r, g, m] = wgt * state, wgt * decay
            return carry

        lax.fori_loop(0, far_groups, of_group, 0)

    def turn_query(r):
        for g in range(far_groups):
            for h in range(out_toks // LANES):
                if r:
                    tile = q_far[r - 1, g * LANES:(g + 1) * LANES, h * LANES:(h + 1) * LANES]
                else:
                    own = slice(far_chans + g * LANES, far_chans + (g + 1) * LANES)
                    tile = q_v[own, pl.ds(pl.multiple_of(tp * out_toks + h * LANES, LANES), LANES)]
                qd[r, g, h * LANES:(h + 1) * LANES, :] = tile.T.astype(f32)

    dec = dec_t[...]
    lam1 = jnp.exp(-block * dec)
    second_pass(0)
    second_pass(1)
    far_pass(0)
    lax.fori_loop(0, near_groups, lambda g, carry: prepare(g, carry, True), 0)
    lax.fori_loop(near_groups, groups, lambda g, carry: prepare(g, carry, False), 0)
    send_x.wait_recv()
    same, across = s_own[...], s_x[...]
    g_z[0] = jnp.where(x_hi == 0, across + lam1 * same, same + lam1 * across)
    sends_z = [remote(g_z.at[0], g_z.at[j], z_send.at[j], z_recv.at[j], to_z[j]) for j in range(1, NZ)]
    for send in sends_z:
        send.start()

    loads[2].wait()
    for g in range(near_groups):
        for s in range(SUBS):
            turned = q_v[g * LANES:(g + 1) * LANES, s * sub_len:(s + 1) * sub_len].T.astype(f32)
            qs[g, s * sub_len:(s + 1) * sub_len, :] = turned
    turn_query(0)
    hand_on(W_ORDER[0])
    on_by_y(W_ORDER[0])
    far_pass(1)
    far[1][f_dec].wait_recv()
    far[1][f_res].wait_recv()
    far[2][f_dec].start()
    far[2][f_res].start()
    hand_on(W_ORDER[1])
    on_by_y(W_ORDER[1])
    far_pass(2)
    after = [(NZ - 1 - lax.rem(z + NZ - j, NZ)).astype(f32) * (block * NX) for j in range(NZ)]
    by_total = [jnp.exp(-a * dec) for a in after]
    by_before = [None] + [
        jnp.where(z >= j, jnp.exp(-(block * NX * (j - 1)) * dec), 0.0) for j in range(1, NZ)
    ]
    for send in sends_z:
        send.wait_recv()
    total = by_total[0] * g_z[0]
    before = jnp.zeros_like(dec)
    for j in range(1, NZ):
        part = g_z[j]
        total += by_total[j] * part
        before += by_before[j] * part
    h_y[0] = total
    sends_y = [remote(h_y.at[0], h_y.at[j], y_send.at[j], y_recv.at[j], to_y[j]) for j in range(1, NY)]
    for send in sends_y:
        send.start()

    hand_on(W_ORDER[2])
    on_by_y(W_ORDER[2])
    far_pass(3)
    for i in W_ORDER[3:5]:
        hand_on(i)
        on_by_y(i)

    start_z = z.astype(f32) * (block * NX)
    by_y = [jnp.exp(-(block * NX * NZ * (j - 1) + start_z) * dec) for j in range(1, NY + 1)]
    once = once_t[...]
    before = once * before
    beside = once * s_x[...]
    for send in sends_y:
        send.wait_recv()
    came = before
    for j in range(1, NY + 1):
        came += by_y[j - 1] * h_y[j % NY]
    inc[...] = jnp.where(x_hi == 0, came, lam1 * came + beside)

    for g in range(far_groups):
        for m in range(modes):
            all_g = near_groups + g
            t_rows[g, m * SUBS:(m + 1) * SUBS, :] = loc[all_g, m] + pw[all_g, m] * wide(inc, all_g, m)
        for k in range(NTP):
            t_out[k, g] = t_rows[g, pl.ds(k * (SUBS // NTP), modes, stride=SUBS), :]
    t_sends = [
        remote(t_out.at[partner_tp[r]], t_in.at[r - 1], t_send.at[r - 1], t_recv.at[r - 1], to_tp[r])
        for r in range(1, NTP)
    ]
    for r in (2, 3, 1):
        t_sends[r - 1].start()
    for i in W_ORDER[5:7]:
        hand_on(i)
        on_by_y(i)

    g_sends = [
        [
            remote(
                gb.at[g, pl.ds(pl.multiple_of(partner_tp[r] * out_toks, out_toks), out_toks)],
                gin.at[r - 1, g], g_send.at[r - 1, g], g_recv.at[r - 1, g], to_tp[r],
            )
            for r in range(1, NTP)
        ]
        for g in range(near_groups)
    ]
    for g in range(near_groups):
        start = [loc[g, m] + pw[g, m] * wide(inc, g, m) for m in range(modes)]
        lam = [wide(lam_t, g, m) for m in range(modes)]

        def step(t, states):
            states = tuple(l * u for l, u in zip(lam, states))
            yn[g, pl.ds(t, SUBS, stride=sub_len), :] = ys[g, at(t), :] + tree_sum(list(states))
            return states

        lax.fori_loop(0, sub_len, step, tuple(start), unroll=UNROLL)
        gb[g] = (qs[g] * yn[g].astype(bf16).astype(f32)).astype(bf16)
        for r in (2, 3, 1):
            g_sends[g][r - 1].start()
        if g == 0:
            hand_on(W_ORDER[7])
            on_by_y(W_ORDER[7])

    def far_correct(r):
        if r:
            t_sends[r - 1].wait_recv()
            far[r - 1][f_q].wait_recv()
            turn_query(r)

        def of_group(g, carry):
            came = (lambda m: wide(t_in, r - 1, g, m)) if r else (lambda m: wide(t_out, tp, g, m))
            start = [loc_d[r, g, m] + pw_d[r, g, m] * came(m) for m in range(modes)]
            lam = [wide(lam_d, r, g, m) for m in range(modes)]

            def step(t, states):
                states = tuple(l * u for l, u in zip(lam, states))
                ynd[pl.ds(t, SUBS, stride=far_len), :] = yd[r, g, at(t), :] + tree_sum(list(states))
                return states

            lax.fori_loop(0, far_len, step, tuple(start), unroll=UNROLL)
            gd[r, g] = (qd[r, g] * ynd[...].astype(bf16).astype(f32)).astype(bf16)
            return carry

        lax.fori_loop(0, far_groups, of_group, 0)

    far_correct(0)
    hand_across(0)
    far_correct(1)
    hand_across(3)
    far_correct(2)
    hand_across(1)
    hand_across(4)
    far_correct(3)
    hand_across(2)
    hand_across(5)

    loads[3].wait()
    w_sib.wait_recv()
    for g in range(near_groups):
        g_sends[g][0].wait_recv()
    lhs = jnp.concatenate(
        [gb[g, own_toks, :] for g in range(near_groups)] + [gd[0, g] for g in range(far_groups)]
        + [gin[0, g] for g in range(near_groups)] + [gd[1, g] for g in range(far_groups)], axis=1
    )
    acc[...] = jnp.dot(lhs, jnp.concatenate([wf[0], wf[1]], axis=0), preferred_element_type=f32)
    for per_piece in w_across:
        for copy in per_piece:
            copy.wait_recv()
    lhs = jnp.concatenate([gd[r, g] for r in (2, 3) for g in range(far_groups)], axis=1)
    rhs = jnp.concatenate([wf[r, far_chans:, :] for r in (2, 3)], axis=0)
    acc[...] += jnp.dot(lhs, rhs, preferred_element_type=f32)
    for g in range(near_groups):
        rows = slice(g * LANES, (g + 1) * LANES)
        g_sends[g][1].wait_recv()
        g_sends[g][2].wait_recv()
        lhs = jnp.concatenate([gin[1, g], gin[2, g]], axis=1)
        rhs = jnp.concatenate([wf[2, rows, :], wf[3, rows, :]], axis=0)
        part = acc[...] + jnp.dot(lhs, rhs, preferred_element_type=f32)
        if g == near_groups - 1:
            out_ref[...] = part.astype(bf16)
        else:
            acc[...] = part

    for copy in [w_sib, send_x] + sends_z + sends_y + t_sends + w_import:
        copy.wait_send()
    for family in (far, w_on, w_across, g_sends):
        for part in family:
            for copy in part:
                copy.wait_send()


def shards(kv_product, query, decay_rate, residue, out_weight):
    chans, toks = kv_product.shape
    modes = decay_rate.shape[1]
    cols = out_weight.shape[1]
    groups = chans // LANES
    near, far = groups // 2, groups - groups // 2
    out_toks = toks // NTP
    bf16, f32 = jnp.bfloat16, jnp.float32
    small = (groups, modes, LANES)
    runs = (groups, modes, SUBS, LANES)
    far_block = (NTP - 1, chans // 2, out_toks)
    far_coef = (NTP - 1, modes, chans // 2)
    pieces = W_PIECES
    vmem, dma = pltpu.VMEM, pltpu.SemaphoreType.DMA
    operands = (kv_product, query, decay_rate.T, residue.T, out_weight)
    return pl.pallas_call(
        kernel,
        out_shape=jax.ShapeDtypeStruct((out_toks, cols), bf16),
        in_specs=[pl.BlockSpec(memory_space=pltpu.HBM)] * 5,
        out_specs=pl.BlockSpec(memory_space=pltpu.VMEM),
        scratch_shapes=[
            vmem((chans, toks), bf16), vmem((chans, toks), bf16), vmem((modes, chans), f32), vmem((modes, chans), f32),
            vmem(far_block, bf16), vmem(far_block, bf16), vmem(far_coef, f32), vmem(far_coef, f32),
            vmem((NTP, chans, cols), bf16),
            vmem((groups, toks, LANES), f32), vmem((near, toks, LANES), f32),
            vmem((near, toks, LANES), f32), vmem((near, toks, LANES), f32),
            vmem(small, f32), vmem(small, f32), vmem(small, f32), vmem(small, f32), vmem(small, f32),
            vmem((3,) + small, f32),
            vmem(runs, f32), vmem(runs, f32), vmem(runs, f32),
            vmem(small, f32), vmem(small, f32), vmem((NZ,) + small, f32), vmem((NY,) + small, f32), vmem(small, f32),
            vmem((far, modes * SUBS, LANES), f32),
            vmem((NTP, far, modes, LANES), f32), vmem((NTP - 1, far, modes, LANES), f32),
            vmem((NTP, far, out_toks, LANES), f32), vmem((NTP, far, out_toks, LANES), f32),
            vmem((NTP, far, out_toks, LANES), f32), vmem((out_toks, LANES), f32),
            vmem((NTP, far, modes, LANES), f32), vmem((NTP, far, modes, LANES), f32),
            vmem((NTP, far, modes, LANES), f32), vmem((NTP, far, modes, LANES), f32),
            vmem((NTP, far, modes, LANES), f32), vmem((3, NTP, far, modes, LANES), f32),
            vmem((NTP, far, modes, SUBS, LANES), f32), vmem((NTP, far, modes, SUBS, LANES), f32),
            vmem((near, toks, LANES), bf16), vmem((NTP - 1, near, out_toks, LANES), bf16),
            vmem((NTP, far, out_toks, LANES), bf16), vmem((out_toks, cols), f32),
            dma((4 + groups,)), dma((2,)), dma((NZ,)), dma((NZ,)), dma((NY,)), dma((NY,)),
            dma((NTP - 1, far + 3)), dma((NTP - 1, far + 3)), dma((NTP - 1,)), dma((NTP - 1,)),
            dma((2,)), dma((pieces,)), dma((pieces,)), dma((3, pieces)), dma((3, pieces)),
            dma((4, len(W_UNITS))), dma((4, len(W_UNITS))), dma((NTP - 1, near)), dma((NTP - 1, near)),
        ],
        compiler_params=pltpu.CompilerParams(
            collective_id=0, has_side_effects=True, vmem_limit_bytes=50 * 1024 * 1024
        ),
        cost_estimate=pl.CostEstimate(
            flops=2 * out_toks * cols * chans * NTP, bytes_accessed=6 * 1024 * 1024, transcendentals=0
        ),
    )(*(pltpu.with_memory_space_constraint(a, pltpu.HBM) for a in operands))


def solution(mesh):
    in_specs = (P("tp", "ctx"), P("tp", "ctx"), P("tp", None), P("tp", None), P("tp", None))
    out_specs = P(("ctx", "tp"), None)
    return jax.shard_map(shards, mesh=mesh, in_specs=in_specs, out_specs=out_specs, check_vma=False)
```

```python
import jax
import jax.numpy as jnp
from jax import lax
from jax.experimental import pallas as pl
from jax.experimental.pallas import tpu as pltpu
from jax.sharding import PartitionSpec as P

NY, NZ, NX, NTP = 4, 4, 2, 4
SUBS, LANES = 8, 128
W_PIECES = 8
W_ORDER = (0, 4, 1, 5, 2, 6, 3, 7)
W_UNITS = ((0, 2), (2, 1), (3, 1), (4, 2), (6, 1), (7, 1))
UNROLL = 32
MESH = pl.DeviceIdType.MESH


def one_minus_exp(z):
    series = jnp.ones_like(z)
    for n in range(10, 1, -1):
        series = 1.0 - (z * (1.0 / n)) * series
    return jnp.where(z < 0.5, z * series, 1.0 - jnp.exp(-z))


def shift_rows(value, by, row):
    return jnp.where(row >= by, pltpu.roll(value, by, 0), 0.0)


def tree_sum(terms):
    while len(terms) > 1:
        terms = [a + b for a, b in zip(terms[::2], terms[1::2])]
    return terms[0]


def at(t):
    return pl.ds(pl.multiple_of(t * SUBS, SUBS), SUBS)


def kernel(
    kv_hbm, q_hbm, dec_hbm, res_hbm, w_hbm, out_ref,
    kv_v, q_v, dec_v, res_v, kv_far, q_far, dec_far, res_far, wf,
    xs, qs, ys, yn, dec_t, lam_t, wgt_t, wc_t, once_t, run_t, ends, loc, pw,
    s_own, s_x, g_z, h_y, inc, t_rows, t_out, t_in,
    xd, qd, yd, ynd, dec_d, lam_d, wgt_d, wc_d, once_d, run_d, loc_d, pw_d,
    gb, gin, gd, acc,
    loc_sem, x_sem, z_send, z_recv, y_send, y_recv, far_send, far_recv, t_send, t_recv,
    wsib_sem, wi_send, wi_recv, wn_send, wn_recv, wa_send, wa_recv, g_send, g_recv,
):
    chans, toks = kv_v.shape
    modes = dec_v.shape[0]
    groups = chans // LANES
    near_groups = groups // 2
    far_chans = chans // 2
    far_groups = groups - near_groups
    sub_len = toks // SUBS
    out_toks, cols = out_ref.shape
    far_len = out_toks // SUBS
    seq = float(toks * NY * NZ * NX)
    block = float(toks)
    f32, bf16 = jnp.float32, jnp.bfloat16

    ctx, tp = lax.axis_index("ctx"), lax.axis_index("tp")
    x_hi = lax.rem(ctx, NX)
    z = lax.rem(ctx // NX, NZ)
    y = ctx // (NX * NZ)
    x_lo, core = tp // 2, lax.rem(tp, 2)

    def ctx_of(yy, zz, xx):
        return (yy * NZ + zz) * NX + xx

    partner_tp = [tp, x_lo * 2 + (1 - core), (1 - x_lo) * 2 + core, (1 - x_lo) * 2 + (1 - core)]
    to_x = {"ctx": ctx_of(y, z, 1 - x_hi), "tp": tp}
    to_z = [{"ctx": ctx_of(y, lax.rem(z + j, NZ), x_hi), "tp": tp} for j in range(NZ)]
    to_y = [{"ctx": ctx_of(lax.rem(y + j, NY), z, x_hi), "tp": tp} for j in range(NY)]
    to_tp = [{"ctx": ctx, "tp": t} for t in partner_tp]
    to_wrap = {"ctx": ctx_of(y, z, 1 - x_hi), "tp": partner_tp[2]}

    loads = [
        pltpu.make_async_copy(dec_hbm, dec_v, loc_sem.at[0]),
        pltpu.make_async_copy(res_hbm, res_v, loc_sem.at[1]),
        pltpu.make_async_copy(q_hbm, q_v, loc_sem.at[2]),
        pltpu.make_async_copy(w_hbm, wf.at[0], loc_sem.at[3]),
    ]
    kv_rows = [pl.ds(g * LANES, LANES) for g in range(groups)]
    kv_loads = [
        pltpu.make_async_copy(kv_hbm.at[rows], kv_v.at[rows], loc_sem.at[4 + g]) for g, rows in enumerate(kv_rows)
    ]
    for load in loads[:2] + kv_loads + loads[2:]:
        load.start()

    barrier = pltpu.get_barrier_semaphore()
    partners = [to_x] + to_z[1:] + to_y[1:] + to_tp[1:] + [to_wrap]
    for partner in partners:
        pl.semaphore_signal(barrier, inc=1, device_id=partner, device_id_type=MESH)

    def remote(src, dst, send, recv, to):
        return pltpu.make_async_remote_copy(
            src_ref=src, dst_ref=dst, send_sem=send, recv_sem=recv, device_id=to, device_id_type=MESH
        )

    far_rows, far_cols = pl.ds(far_chans, far_chans), pl.ds(near_groups * LANES, far_chans)
    far = []
    for r in range(1, NTP):
        there = pl.ds(pl.multiple_of(partner_tp[r] * out_toks, out_toks), out_toks)
        pairs = [
            (kv_hbm.at[pl.ds(far_chans + g * LANES, LANES), there], kv_far.at[r - 1, pl.ds(g * LANES, LANES)])
            for g in range(far_groups)
        ] + [
            (dec_hbm.at[:, far_cols], dec_far.at[r - 1]), (res_hbm.at[:, far_cols], res_far.at[r - 1]),
            (q_hbm.at[far_rows, there], q_far.at[r - 1]),
        ]
        far.append(
            [
                remote(src, dst, far_send.at[r - 1, i], far_recv.at[r - 1, i], to_tp[r])
                for i, (src, dst) in enumerate(pairs)
            ]
        )
    f_dec, f_res, f_q = far_groups, far_groups + 1, far_groups + 2

    for i, array in ((f_dec, dec_far), (f_res, res_far)):
        far[2][i] = remote(array.at[1], array.at[2], far_send.at[2, i], far_recv.at[2, i], to_tp[1])

    quarter = chans // 4
    piece = quarter // W_PIECES

    def rows_of(which, first, count):
        return pl.ds(pl.multiple_of(which * quarter + first * piece, 16), count * piece)

    w_sib = remote(w_hbm, wf.at[1], wsib_sem.at[0], wsib_sem.at[1], to_tp[1])
    holds = []
    for mine in (lax.rem(z + 2 * y, 4), lax.rem(y + 2 * z, 4)):
        holds.append((lax.rem(mine + 3, 4), lax.rem(mine + 1, 4), lax.rem(mine + 2, 4), mine))
    w_import, w_on, w_got = [], [], []
    for i in range(W_PIECES):
        by_y = i // (W_PIECES // 2)
        turn_to, half_to = ((to_z, to_y), (to_y, to_z))[by_y]
        ways = (turn_to[1], turn_to[NZ - 1], half_to[1 if i % 2 == 0 else NY - 1])
        mine = rows_of(holds[by_y][3], i, 1)
        w_import.append(remote(w_hbm.at[mine], wf.at[2, mine], wi_send.at[i], wi_recv.at[i], to_wrap))
        w_on.append([])
        w_got.append([])
        for way, to in enumerate(ways):
            theirs = rows_of(holds[by_y][way], i, 1)
            w_on[i].append(remote(wf.at[2, mine], wf.at[2, mine], wn_send.at[way, i], wn_recv.at[way, i], to))
            w_got[i].append(remote(wf.at[2, theirs], wf.at[2, theirs], wn_send.at[way, i], wn_recv.at[way, i], to))
    w_across = []
    for u, (first, count) in enumerate(W_UNITS):
        w_across.append([])
        for way, which in enumerate(holds[first // (W_PIECES // 2)]):
            rows = rows_of(which, first, count)
            w_across[u].append(
                remote(wf.at[2, rows], wf.at[3, rows], wa_send.at[way, u], wa_recv.at[way, u], to_tp[1])
            )

    def on_by_y(i):
        for way in ((2,), (0, 1))[i // (W_PIECES // 2)]:
            w_on[i][way].start()

    def hand_on(i):
        w_import[i].wait_recv()
        for way in ((0, 1), (2,))[i // (W_PIECES // 2)]:
            w_on[i][way].start()
        for u, (first, count) in enumerate(W_UNITS):
            if i == first + count - 1:
                w_across[u][3].start()

    def hand_across(u):
        first, count = W_UNITS[u]
        for way in range(3):
            for i in range(first, first + count):
                w_got[i][way].wait_recv()
            w_across[u][way].start()

    def coefficients(dec, res, length, *where):
        refs, where = where[0], where[1:]
        dec_to, lam_to, wgt_to, wc_to, once_to, run_to = refs
        wgt = res * jnp.sqrt(one_minus_exp(2.0 * dec))
        once = one_minus_exp(seq * dec)
        run = jnp.exp(-float(length) * dec)
        dec_to[where] = dec
        lam_to[where] = jnp.exp(-dec)
        wgt_to[where] = wgt
        wc_to[where] = wgt * once
        once_to[where] = once
        for i in range(3):
            run_to[(i, *where)] = run
            run = run * run

    near_coefs = (dec_t, lam_t, wgt_t, wc_t, once_t, run_t)
    far_coefs = (dec_d, lam_d, wgt_d, wc_d, once_d, run_d)
    loads[0].wait()
    loads[1].wait()
    for g in range(groups):
        lanes = slice(g * LANES, (g + 1) * LANES)
        coefficients(dec_v[:, lanes], res_v[:, lanes], sub_len, near_coefs, g)

    def turn_near(g):
        kv_loads[g].wait()
        for s in range(SUBS):
            turned = kv_v[g * LANES:(g + 1) * LANES, s * sub_len:(s + 1) * sub_len].T.astype(f32)
            xs[g, pl.ds(s, sub_len, stride=SUBS), :] = turned

    row = lax.broadcasted_iota(jnp.int32, (SUBS, LANES), 0)
    row_f = row.astype(f32)

    def wide(ref, *where):
        *lead, m = where
        return jnp.broadcast_to(ref[(*lead, slice(m, m + 1), slice(None))], (SUBS, LANES))

    zeros = tuple(jnp.zeros((SUBS, LANES), f32) for _ in range(modes))

    def first_pass(g):
        lam = [wide(lam_t, g, m) for m in range(modes)]

        def step(t, states):
            x = xs[g, at(t), :]
            return tuple(l * u + x for l, u in zip(lam, states))

        states = lax.fori_loop(0, sub_len, step, zeros, unroll=UNROLL)
        for m in range(modes):
            ends[g, m] = states[m]
            decayed = states[m] * jnp.exp(-wide(dec_t, g, m) * ((SUBS - 1 - row_f) * float(sub_len)))
            s_own[g, m:m + 1, :] = jnp.sum(decayed, axis=0, keepdims=True)

    for g in range(4):
        turn_near(g)
        first_pass(g)
    pl.semaphore_wait(barrier, len(partners))
    for g in range(4, groups):
        turn_near(g)
        first_pass(g)

    send_x = remote(s_own, s_x, x_sem.at[0], x_sem.at[1], to_x)
    send_x.start()
    w_import[W_ORDER[0]].start()
    w_import[W_ORDER[1]].start()
    far[1][0].start()
    for copy in far[0]:
        copy.start()
    w_sib.start()
    rest = (far[1][1], far[1][f_dec], far[1][f_res], far[2][0], far[2][1], far[1][f_q], far[2][f_q])
    for i in W_ORDER[2:]:
        w_import[i].start()
    for copy in rest:
        copy.start()

    def run_starts(states, coefs, length, *where):
        dec_of, _, _, _, once_of, run_of = coefs
        state = shift_rows(states * wide(once_of, *where), 1, row)
        for i, by in enumerate((1, 2, 4)):
            state += wide(run_of, i, *where) * shift_rows(state, by, row)
        return state, jnp.exp(wide(dec_of, *where) * (row_f * -float(length)))

    def prepare(g, carry, weighted):
        for m in range(modes):
            state, decay = run_starts(ends[g, m], near_coefs, sub_len, g, m)
            wgt = wide(wgt_t, g, m) if weighted else 1.0
            loc[g, m], pw[g, m] = wgt * state, wgt * decay
        return carry

    def second_pass(g):
        lam = [wide(lam_t, g, m) for m in range(modes)]
        gain = [wide(wc_t, g, m) for m in range(modes)]

        def step(t, states):
            x = xs[g, at(t), :]
            states = tuple(l * u + x for l, u in zip(lam, states))
            ys[g, at(t), :] = tree_sum([c * u for c, u in zip(gain, states)])
            return states

        lax.fori_loop(0, sub_len, step, zeros, unroll=UNROLL)

    own_toks = pl.ds(pl.multiple_of(tp * out_toks, out_toks), out_toks)

    def far_pass(r):
        if r:
            for i in (0, 1) if r == 2 else (0, 1, f_dec, f_res):
                far[r - 1][i].wait_recv()
        halves = out_toks // LANES
        for g in range(far_groups):
            lanes = slice(g * LANES, (g + 1) * LANES)
            if r:
                dec, res = dec_far[r - 1, :, lanes], res_far[r - 1, :, lanes]
            else:
                own = slice(far_chans + g * LANES, far_chans + (g + 1) * LANES)
                dec, res = dec_v[:, own], res_v[:, own]
            coefficients(dec, res, far_len, far_coefs, r, g)
            for h in range(halves):
                if r:
                    tile = kv_far[r - 1, lanes, h * LANES:(h + 1) * LANES]
                else:
                    tile = kv_v[own, pl.ds(pl.multiple_of(tp * out_toks + h * LANES, LANES), LANES)]
                turned = tile.T.astype(f32)
                for s in range(SUBS // halves):
                    xd[r, g, pl.ds(h * (SUBS // halves) + s, far_len, stride=SUBS), :] = (
                        turned[s * far_len:(s + 1) * far_len]
                    )

        def of_group(g, carry):
            lam = [wide(lam_d, r, g, m) for m in range(modes)]
            gain = [wide(wc_d, r, g, m) for m in range(modes)]

            def step(t, states):
                x = xd[r, g, at(t), :]
                states = tuple(l * u + x for l, u in zip(lam, states))
                yd[r, g, at(t), :] = tree_sum([c * u for c, u in zip(gain, states)])
                return states

            states = lax.fori_loop(0, far_len, step, zeros, unroll=UNROLL)
            for m in range(modes):
                state, decay = run_starts(states[m], far_coefs, far_len, r, g, m)
                wgt = wide(wgt_d, r, g, m)
                loc_d[r, g, m], pw_d[r, g, m] = wgt * state, wgt * decay
            return carry

        lax.fori_loop(0, far_groups, of_group, 0)

    def turn_query(r):
        for g in range(far_groups):
            for h in range(out_toks // LANES):
                if r:
                    tile = q_far[r - 1, g * LANES:(g + 1) * LANES, h * LANES:(h + 1) * LANES]
                else:
                    own = slice(far_chans + g * LANES, far_chans + (g + 1) * LANES)
                    tile = q_v[own, pl.ds(pl.multiple_of(tp * out_toks + h * LANES, LANES), LANES)]
                qd[r, g, h * LANES:(h + 1) * LANES, :] = tile.T.astype(f32)

    dec = dec_t[...]
    lam1 = jnp.exp(-block * dec)
    second_pass(0)
    second_pass(1)
    far_pass(0)
    lax.fori_loop(0, near_groups, lambda g, carry: prepare(g, carry, True), 0)
    lax.fori_loop(near_groups, groups, lambda g, carry: prepare(g, carry, False), 0)
    send_x.wait_recv()
    same, across = s_own[...], s_x[...]
    g_z[0] = jnp.where(x_hi == 0, across + lam1 * same, same + lam1 * across)
    sends_z = [remote(g_z.at[0], g_z.at[j], z_send.at[j], z_recv.at[j], to_z[j]) for j in range(1, NZ)]
    for send in sends_z:
        send.start()

    loads[2].wait()
    for g in range(near_groups):
        for s in range(SUBS):
            turned = q_v[g * LANES:(g + 1) * LANES, s * sub_len:(s + 1) * sub_len].T.astype(f32)
            qs[g, s * sub_len:(s + 1) * sub_len, :] = turned
    turn_query(0)
    hand_on(W_ORDER[0])
    on_by_y(W_ORDER[0])
    far_pass(1)
    far[1][f_dec].wait_recv()
    far[1][f_res].wait_recv()
    far[2][f_dec].start()
    far[2][f_res].start()
    hand_on(W_ORDER[1])
    on_by_y(W_ORDER[1])
    far_pass(2)
    after = [(NZ - 1 - lax.rem(z + NZ - j, NZ)).astype(f32) * (block * NX) for j in range(NZ)]
    by_total = [jnp.exp(-a * dec) for a in after]
    by_before = [None] + [
        jnp.where(z >= j, jnp.exp(-(block * NX * (j - 1)) * dec), 0.0) for j in range(1, NZ)
    ]
    for send in sends_z:
        send.wait_recv()
    total = by_total[0] * g_z[0]
    before = jnp.zeros_like(dec)
    for j in range(1, NZ):
        part = g_z[j]
        total += by_total[j] * part
        before += by_before[j] * part
    h_y[0] = total
    sends_y = [remote(h_y.at[0], h_y.at[j], y_send.at[j], y_recv.at[j], to_y[j]) for j in range(1, NY)]
    for send in sends_y:
        send.start()

    hand_on(W_ORDER[2])
    on_by_y(W_ORDER[2])
    far_pass(3)
    for i in W_ORDER[3:5]:
        hand_on(i)
        on_by_y(i)

    start_z = z.astype(f32) * (block * NX)
    by_y = [jnp.exp(-(block * NX * NZ * (j - 1) + start_z) * dec) for j in range(1, NY + 1)]
    once = once_t[...]
    before = once * before
    beside = once * s_x[...]
    for send in sends_y:
        send.wait_recv()
    came = before
    for j in range(1, NY + 1):
        came += by_y[j - 1] * h_y[j % NY]
    inc[...] = jnp.where(x_hi == 0, came, lam1 * came + beside)

    for g in range(far_groups):
        for m in range(modes):
            all_g = near_groups + g
            t_rows[g, m * SUBS:(m + 1) * SUBS, :] = loc[all_g, m] + pw[all_g, m] * wide(inc, all_g, m)
        for k in range(NTP):
            t_out[k, g] = t_rows[g, pl.ds(k * (SUBS // NTP), modes, stride=SUBS), :]
    t_sends = [
        remote(t_out.at[partner_tp[r]], t_in.at[r - 1], t_send.at[r - 1], t_recv.at[r - 1], to_tp[r])
        for r in range(1, NTP)
    ]
    for r in (2, 3, 1):
        t_sends[r - 1].start()
    for i in W_ORDER[5:7]:
        hand_on(i)
        on_by_y(i)

    g_sends = [
        [
            remote(
                gb.at[g, pl.ds(pl.multiple_of(partner_tp[r] * out_toks, out_toks), out_toks)],
                gin.at[r - 1, g], g_send.at[r - 1, g], g_recv.at[r - 1, g], to_tp[r],
            )
            for r in range(1, NTP)
        ]
        for g in range(near_groups)
    ]
    for g in range(near_groups):
        start = [loc[g, m] + pw[g, m] * wide(inc, g, m) for m in range(modes)]
        lam = [wide(lam_t, g, m) for m in range(modes)]

        def step(t, states):
            states = tuple(l * u for l, u in zip(lam, states))
            yn[g, pl.ds(t, SUBS, stride=sub_len), :] = ys[g, at(t), :] + tree_sum(list(states))
            return states

        lax.fori_loop(0, sub_len, step, tuple(start), unroll=UNROLL)
        gb[g] = (qs[g] * yn[g].astype(bf16).astype(f32)).astype(bf16)
        for r in (2, 3, 1):
            g_sends[g][r - 1].start()
        if g == 0:
            hand_on(W_ORDER[7])
            on_by_y(W_ORDER[7])

    def far_correct(r):
        if r:
            t_sends[r - 1].wait_recv()
            far[r - 1][f_q].wait_recv()
            turn_query(r)

        def of_group(g, carry):
            came = (lambda m: wide(t_in, r - 1, g, m)) if r else (lambda m: wide(t_out, tp, g, m))
            start = [loc_d[r, g, m] + pw_d[r, g, m] * came(m) for m in range(modes)]
            lam = [wide(lam_d, r, g, m) for m in range(modes)]

            def step(t, states):
                states = tuple(l * u for l, u in zip(lam, states))
                ynd[pl.ds(t, SUBS, stride=far_len), :] = yd[r, g, at(t), :] + tree_sum(list(states))
                return states

            lax.fori_loop(0, far_len, step, tuple(start), unroll=UNROLL)
            gd[r, g] = (qd[r, g] * ynd[...].astype(bf16).astype(f32)).astype(bf16)
            return carry

        lax.fori_loop(0, far_groups, of_group, 0)

    far_correct(0)
    hand_across(0)
    far_correct(1)
    hand_across(3)
    far_correct(2)
    hand_across(1)
    hand_across(4)
    far_correct(3)
    hand_across(2)
    hand_across(5)

    loads[3].wait()
    w_sib.wait_recv()
    for g in range(near_groups):
        g_sends[g][0].wait_recv()
    lhs = jnp.concatenate(
        [gb[g, own_toks, :] for g in range(near_groups)] + [gd[0, g] for g in range(far_groups)]
        + [gin[0, g] for g in range(near_groups)] + [gd[1, g] for g in range(far_groups)], axis=1
    )
    acc[...] = jnp.dot(lhs, jnp.concatenate([wf[0], wf[1]], axis=0), preferred_element_type=f32)
    for per_piece in w_across:
        for copy in per_piece:
            copy.wait_recv()
    lhs = jnp.concatenate([gd[r, g] for r in (2, 3) for g in range(far_groups)], axis=1)
    rhs = jnp.concatenate([wf[r, far_chans:, :] for r in (2, 3)], axis=0)
    acc[...] += jnp.dot(lhs, rhs, preferred_element_type=f32)
    for g in range(near_groups):
        rows = slice(g * LANES, (g + 1) * LANES)
        g_sends[g][1].wait_recv()
        g_sends[g][2].wait_recv()
        lhs = jnp.concatenate([gin[1, g], gin[2, g]], axis=1)
        rhs = jnp.concatenate([wf[2, rows, :], wf[3, rows, :]], axis=0)
        part = acc[...] + jnp.dot(lhs, rhs, preferred_element_type=f32)
        if g == near_groups - 1:
            out_ref[...] = part.astype(bf16)
        else:
            acc[...] = part

    for copy in [w_sib, send_x] + sends_z + sends_y + t_sends + w_import:
        copy.wait_send()
    for family in (far, w_on, w_across, g_sends):
        for part in family:
            for copy in part:
                copy.wait_send()


def shards(kv_product, query, decay_rate, residue, out_weight):
    chans, toks = kv_product.shape
    modes = decay_rate.shape[1]
    cols = out_weight.shape[1]
    groups = chans // LANES
    near, far = groups // 2, groups - groups // 2
    out_toks = toks // NTP
    bf16, f32 = jnp.bfloat16, jnp.float32
    small = (groups, modes, LANES)
    runs = (groups, modes, SUBS, LANES)
    far_block = (NTP - 1, chans // 2, out_toks)
    far_coef = (NTP - 1, modes, chans // 2)
    pieces = W_PIECES
    vmem, dma = pltpu.VMEM, pltpu.SemaphoreType.DMA
    operands = (kv_product, query, decay_rate.T, residue.T, out_weight)
    return pl.pallas_call(
        kernel,
        out_shape=jax.ShapeDtypeStruct((out_toks, cols), bf16),
        in_specs=[pl.BlockSpec(memory_space=pltpu.HBM)] * 5,
        out_specs=pl.BlockSpec(memory_space=pltpu.VMEM),
        scratch_shapes=[
            vmem((chans, toks), bf16), vmem((chans, toks), bf16), vmem((modes, chans), f32), vmem((modes, chans), f32),
            vmem(far_block, bf16), vmem(far_block, bf16), vmem(far_coef, f32), vmem(far_coef, f32),
            vmem((NTP, chans, cols), bf16),
            vmem((groups, toks, LANES), f32), vmem((near, toks, LANES), f32),
            vmem((near, toks, LANES), f32), vmem((near, toks, LANES), f32),
            vmem(small, f32), vmem(small, f32), vmem(small, f32), vmem(small, f32), vmem(small, f32),
            vmem((3,) + small, f32),
            vmem(runs, f32), vmem(runs, f32), vmem(runs, f32),
            vmem(small, f32), vmem(small, f32), vmem((NZ,) + small, f32), vmem((NY,) + small, f32), vmem(small, f32),
            vmem((far, modes * SUBS, LANES), f32),
            vmem((NTP, far, modes, LANES), f32), vmem((NTP - 1, far, modes, LANES), f32),
            vmem((NTP, far, out_toks, LANES), f32), vmem((NTP, far, out_toks, LANES), f32),
            vmem((NTP, far, out_toks, LANES), f32), vmem((out_toks, LANES), f32),
            vmem((NTP, far, modes, LANES), f32), vmem((NTP, far, modes, LANES), f32),
            vmem((NTP, far, modes, LANES), f32), vmem((NTP, far, modes, LANES), f32),
            vmem((NTP, far, modes, LANES), f32), vmem((3, NTP, far, modes, LANES), f32),
            vmem((NTP, far, modes, SUBS, LANES), f32), vmem((NTP, far, modes, SUBS, LANES), f32),
            vmem((near, toks, LANES), bf16), vmem((NTP - 1, near, out_toks, LANES), bf16),
            vmem((NTP, far, out_toks, LANES), bf16), vmem((out_toks, cols), f32),
            dma((4 + groups,)), dma((2,)), dma((NZ,)), dma((NZ,)), dma((NY,)), dma((NY,)),
            dma((NTP - 1, far + 3)), dma((NTP - 1, far + 3)), dma((NTP - 1,)), dma((NTP - 1,)),
            dma((2,)), dma((pieces,)), dma((pieces,)), dma((3, pieces)), dma((3, pieces)),
            dma((4, len(W_UNITS))), dma((4, len(W_UNITS))), dma((NTP - 1, near)), dma((NTP - 1, near)),
        ],
        compiler_params=pltpu.CompilerParams(
            collective_id=0, has_side_effects=True, vmem_limit_bytes=50 * 1024 * 1024
        ),
        cost_estimate=pl.CostEstimate(
            flops=2 * out_toks * cols * chans * NTP, bytes_accessed=6 * 1024 * 1024, transcendentals=0
        ),
    )(*(pltpu.with_memory_space_constraint(a, pltpu.HBM) for a in operands))


def solution(mesh):
    in_specs = (P("tp", "ctx"), P("tp", "ctx"), P("tp", None), P("tp", None), P("tp", None))
    out_specs = P(("ctx", "tp"), None)
    return jax.shard_map(shards, mesh=mesh, in_specs=in_specs, out_specs=out_specs, check_vma=False)
```

```python
import jax
import jax.numpy as jnp
from jax import lax
from jax.experimental import pallas as pl
from jax.experimental.pallas import tpu as pltpu
from jax.sharding import PartitionSpec as P

NY, NZ, NX, NTP = 4, 4, 2, 4
SUBS, LANES = 8, 128
W_PIECES = 8
W_ORDER = (0, 4, 1, 5, 2, 6, 3, 7)
W_UNITS = ((0, 2), (2, 1), (3, 1), (4, 2), (6, 1), (7, 1))
UNROLL = 32
MESH = pl.DeviceIdType.MESH


def one_minus_exp(z):
    series = jnp.ones_like(z)
    for n in range(10, 1, -1):
        series = 1.0 - (z * (1.0 / n)) * series
    return jnp.where(z < 0.5, z * series, 1.0 - jnp.exp(-z))


def shift_rows(value, by, row):
    return jnp.where(row >= by, pltpu.roll(value, by, 0), 0.0)


def tree_sum(terms):
    while len(terms) > 1:
        terms = [a + b for a, b in zip(terms[::2], terms[1::2])]
    return terms[0]


def at(t):
    return pl.ds(pl.multiple_of(t * SUBS, SUBS), SUBS)


def kernel(
    kv_hbm, q_hbm, dec_hbm, res_hbm, w_hbm, out_ref,
    kv_v, q_v, dec_v, res_v, kv_far, q_far, dec_far, res_far, wf,
    xs, qs, ys, yn, dec_t, lam_t, wgt_t, wc_t, once_t, run_t, ends, loc, pw,
    s_own, s_x, g_z, h_y, inc, t_rows, t_out, t_in,
    xd, qd, yd, ynd, dec_d, lam_d, wgt_d, wc_d, once_d, run_d, loc_d, pw_d,
    gb, gin, gd, acc,
    loc_sem, x_sem, z_send, z_recv, y_send, y_recv, far_send, far_recv, t_send, t_recv,
    wsib_sem, wi_send, wi_recv, wn_send, wn_recv, wa_send, wa_recv, g_send, g_recv,
):
    chans, toks = kv_v.shape
    modes = dec_v.shape[0]
    groups = chans // LANES
    near_groups = groups // 2
    far_chans = chans // 2
    far_groups = groups - near_groups
    sub_len = toks // SUBS
    out_toks, cols = out_ref.shape
    far_len = out_toks // SUBS
    seq = float(toks * NY * NZ * NX)
    block = float(toks)
    f32, bf16 = jnp.float32, jnp.bfloat16

    ctx, tp = lax.axis_index("ctx"), lax.axis_index("tp")
    x_hi = lax.rem(ctx, NX)
    z = lax.rem(ctx // NX, NZ)
    y = ctx // (NX * NZ)
    x_lo, core = tp // 2, lax.rem(tp, 2)

    def ctx_of(yy, zz, xx):
        return (yy * NZ + zz) * NX + xx

    partner_tp = [tp, x_lo * 2 + (1 - core), (1 - x_lo) * 2 + core, (1 - x_lo) * 2 + (1 - core)]
    to_x = {"ctx": ctx_of(y, z, 1 - x_hi), "tp": tp}
    to_z = [{"ctx": ctx_of(y, lax.rem(z + j, NZ), x_hi), "tp": tp} for j in range(NZ)]
    to_y = [{"ctx": ctx_of(lax.rem(y + j, NY), z, x_hi), "tp": tp} for j in range(NY)]
    to_tp = [{"ctx": ctx, "tp": t} for t in partner_tp]
    to_wrap = {"ctx": ctx_of(y, z, 1 - x_hi), "tp": partner_tp[2]}

    loads = [
        pltpu.make_async_copy(dec_hbm, dec_v, loc_sem.at[0]),
        pltpu.make_async_copy(res_hbm, res_v, loc_sem.at[1]),
        pltpu.make_async_copy(q_hbm, q_v, loc_sem.at[2]),
        pltpu.make_async_copy(w_hbm, wf.at[0], loc_sem.at[3]),
    ]
    kv_rows = [pl.ds(g * LANES, LANES) for g in range(groups)]
    kv_loads = [
        pltpu.make_async_copy(kv_hbm.at[rows], kv_v.at[rows], loc_sem.at[4 + g]) for g, rows in enumerate(kv_rows)
    ]
    for load in loads[:2] + kv_loads + loads[2:]:
        load.start()

    barrier = pltpu.get_barrier_semaphore()
    partners = [to_x] + to_z[1:] + to_y[1:] + to_tp[1:] + [to_wrap]
    for partner in partners:
        pl.semaphore_signal(barrier, inc=1, device_id=partner, device_id_type=MESH)

    def remote(src, dst, send, recv, to):
        return pltpu.make_async_remote_copy(
            src_ref=src, dst_ref=dst, send_sem=send, recv_sem=recv, device_id=to, device_id_type=MESH
        )

    far_rows, far_cols = pl.ds(far_chans, far_chans), pl.ds(near_groups * LANES, far_chans)
    far = []
    for r in range(1, NTP):
        there = pl.ds(pl.multiple_of(partner_tp[r] * out_toks, out_toks), out_toks)
        pairs = [
            (kv_hbm.at[pl.ds(far_chans + g * LANES, LANES), there], kv_far.at[r - 1, pl.ds(g * LANES, LANES)])
            for g in range(far_groups)
        ] + [
            (dec_hbm.at[:, far_cols], dec_far.at[r - 1]), (res_hbm.at[:, far_cols], res_far.at[r - 1]),
            (q_hbm.at[far_rows, there], q_far.at[r - 1]),
        ]
        far.append(
            [
                remote(src, dst, far_send.at[r - 1, i], far_recv.at[r - 1, i], to_tp[r])
                for i, (src, dst) in enumerate(pairs)
            ]
        )
    f_dec, f_res, f_q = far_groups, far_groups + 1, far_groups + 2

    for i, array in ((f_dec, dec_far), (f_res, res_far)):
        far[2][i] = remote(array.at[1], array.at[2], far_send.at[2, i], far_recv.at[2, i], to_tp[1])

    quarter = chans // 4
    piece = quarter // W_PIECES

    def rows_of(which, first, count):
        return pl.ds(pl.multiple_of(which * quarter + first * piece, 16), count * piece)

    w_sib = remote(w_hbm, wf.at[1], wsib_sem.at[0], wsib_sem.at[1], to_tp[1])
    holds = []
    for mine in (lax.rem(z + 2 * y, 4), lax.rem(y + 2 * z, 4)):
        holds.append((lax.rem(mine + 3, 4), lax.rem(mine + 1, 4), lax.rem(mine + 2, 4), mine))
    w_import, w_on, w_got = [], [], []
    for i in range(W_PIECES):
        by_y = i // (W_PIECES // 2)
        turn_to, half_to = ((to_z, to_y), (to_y, to_z))[by_y]
        ways = (turn_to[1], turn_to[NZ - 1], half_to[1 if i % 2 == 0 else NY - 1])
        mine = rows_of(holds[by_y][3], i, 1)
        w_import.append(remote(w_hbm.at[mine], wf.at[2, mine], wi_send.at[i], wi_recv.at[i], to_wrap))
        w_on.append([])
        w_got.append([])
        for way, to in enumerate(ways):
            theirs = rows_of(holds[by_y][way], i, 1)
            w_on[i].append(remote(wf.at[2, mine], wf.at[2, mine], wn_send.at[way, i], wn_recv.at[way, i], to))
            w_got[i].append(remote(wf.at[2, theirs], wf.at[2, theirs], wn_send.at[way, i], wn_recv.at[way, i], to))
    w_across = []
    for u, (first, count) in enumerate(W_UNITS):
        w_across.append([])
        for way, which in enumerate(holds[first // (W_PIECES // 2)]):
            rows = rows_of(which, first, count)
            w_across[u].append(
                remote(wf.at[2, rows], wf.at[3, rows], wa_send.at[way, u], wa_recv.at[way, u], to_tp[1])
            )

    def on_by_y(i):
        for way in ((2,), (0, 1))[i // (W_PIECES // 2)]:
            w_on[i][way].start()

    def hand_on(i):
        w_import[i].wait_recv()
        for way in ((0, 1), (2,))[i // (W_PIECES // 2)]:
            w_on[i][way].start()
        for u, (first, count) in enumerate(W_UNITS):
            if i == first + count - 1:
                w_across[u][3].start()

    def hand_across(u):
        first, count = W_UNITS[u]
        for way in range(3):
            for i in range(first, first + count):
                w_got[i][way].wait_recv()
            w_across[u][way].start()

    def coefficients(dec, res, length, *where):
        refs, where = where[0], where[1:]
        dec_to, lam_to, wgt_to, wc_to, once_to, run_to = refs
        wgt = res * jnp.sqrt(one_minus_exp(2.0 * dec))
        once = one_minus_exp(seq * dec)
        run = jnp.exp(-float(length) * dec)
        dec_to[where] = dec
        lam_to[where] = jnp.exp(-dec)
        wgt_to[where] = wgt
        wc_to[where] = wgt * once
        once_to[where] = once
        for i in range(3):
            run_to[(i, *where)] = run
            run = run * run

    near_coefs = (dec_t, lam_t, wgt_t, wc_t, once_t, run_t)
    far_coefs = (dec_d, lam_d, wgt_d, wc_d, once_d, run_d)
    loads[0].wait()
    loads[1].wait()
    for g in range(groups):
        lanes = slice(g * LANES, (g + 1) * LANES)
        coefficients(dec_v[:, lanes], res_v[:, lanes], sub_len, near_coefs, g)

    def turn_near(g):
        kv_loads[g].wait()
        for s in range(SUBS):
            turned = kv_v[g * LANES:(g + 1) * LANES, s * sub_len:(s + 1) * sub_len].T.astype(f32)
            xs[g, pl.ds(s, sub_len, stride=SUBS), :] = turned

    row = lax.broadcasted_iota(jnp.int32, (SUBS, LANES), 0)
    row_f = row.astype(f32)

    def wide(ref, *where):
        *lead, m = where
        return jnp.broadcast_to(ref[(*lead, slice(m, m + 1), slice(None))], (SUBS, LANES))

    zeros = tuple(jnp.zeros((SUBS, LANES), f32) for _ in range(modes))

    def first_pass(g):
        lam = [wide(lam_t, g, m) for m in range(modes)]

        def step(t, states):
            x = xs[g, at(t), :]
            return tuple(l * u + x for l, u in zip(lam, states))

        states = lax.fori_loop(0, sub_len, step, zeros, unroll=UNROLL)
        for m in range(modes):
            ends[g, m] = states[m]
            decayed = states[m] * jnp.exp(-wide(dec_t, g, m) * ((SUBS - 1 - row_f) * float(sub_len)))
            s_own[g, m:m + 1, :] = jnp.sum(decayed, axis=0, keepdims=True)

    for g in range(4):
        turn_near(g)
        first_pass(g)
    pl.semaphore_wait(barrier, len(partners))
    for g in range(4, groups):
        turn_near(g)
        first_pass(g)

    send_x = remote(s_own, s_x, x_sem.at[0], x_sem.at[1], to_x)
    send_x.start()
    w_import[W_ORDER[0]].start()
    w_import[W_ORDER[1]].start()
    far[1][0].start()
    rest = (far[1][1], far[1][f_dec], far[1][f_res], far[2][0], far[2][1], far[1][f_q], far[2][f_q])
    for i in W_ORDER[2:]:
        w_import[i].start()
    for copy in rest:
        copy.start()
    for copy in far[0]:
        copy.start()
    w_sib.start()

    def run_starts(states, coefs, length, *where):
        dec_of, _, _, _, once_of, run_of = coefs
        state = shift_rows(states * wide(once_of, *where), 1, row)
        for i, by in enumerate((1, 2, 4)):
            state += wide(run_of, i, *where) * shift_rows(state, by, row)
        return state, jnp.exp(wide(dec_of, *where) * (row_f * -float(length)))

    def prepare(g, carry, weighted):
        for m in range(modes):
            state, decay = run_starts(ends[g, m], near_coefs, sub_len, g, m)
            wgt = wide(wgt_t, g, m) if weighted else 1.0
            loc[g, m], pw[g, m] = wgt * state, wgt * decay
        return carry

    def second_pass(g):
        lam = [wide(lam_t, g, m) for m in range(modes)]
        gain = [wide(wc_t, g, m) for m in range(modes)]

        def step(t, states):
            x = xs[g, at(t), :]
            states = tuple(l * u + x for l, u in zip(lam, states))
            ys[g, at(t), :] = tree_sum([c * u for c, u in zip(gain, states)])
            return states

        lax.fori_loop(0, sub_len, step, zeros, unroll=UNROLL)

    own_toks = pl.ds(pl.multiple_of(tp * out_toks, out_toks), out_toks)

    def far_pass(r):
        if r:
            for i in (0, 1) if r == 2 else (0, 1, f_dec, f_res):
                far[r - 1][i].wait_recv()
        halves = out_toks // LANES
        for g in range(far_groups):
            lanes = slice(g * LANES, (g + 1) * LANES)
            if r:
                dec, res = dec_far[r - 1, :, lanes], res_far[r - 1, :, lanes]
            else:
                own = slice(far_chans + g * LANES, far_chans + (g + 1) * LANES)
                dec, res = dec_v[:, own], res_v[:, own]
            coefficients(dec, res, far_len, far_coefs, r, g)
            for h in range(halves):
                if r:
                    tile = kv_far[r - 1, lanes, h * LANES:(h + 1) * LANES]
                else:
                    tile = kv_v[own, pl.ds(pl.multiple_of(tp * out_toks + h * LANES, LANES), LANES)]
                turned = tile.T.astype(f32)
                for s in range(SUBS // halves):
                    xd[r, g, pl.ds(h * (SUBS // halves) + s, far_len, stride=SUBS), :] = (
                        turned[s * far_len:(s + 1) * far_len]
                    )

        def of_group(g, carry):
            lam = [wide(lam_d, r, g, m) for m in range(modes)]
            gain = [wide(wc_d, r, g, m) for m in range(modes)]

            def step(t, states):
                x = xd[r, g, at(t), :]
                states = tuple(l * u + x for l, u in zip(lam, states))
                yd[r, g, at(t), :] = tree_sum([c * u for c, u in zip(gain, states)])
                return states

            states = lax.fori_loop(0, far_len, step, zeros, unroll=UNROLL)
            for m in range(modes):
                state, decay = run_starts(states[m], far_coefs, far_len, r, g, m)
                wgt = wide(wgt_d, r, g, m)
                loc_d[r, g, m], pw_d[r, g, m] = wgt * state, wgt * decay
            return carry

        lax.fori_loop(0, far_groups, of_group, 0)

    def turn_query(r):
        for g in range(far_groups):
            for h in range(out_toks // LANES):
                if r:
                    tile = q_far[r - 1, g * LANES:(g + 1) * LANES, h * LANES:(h + 1) * LANES]
                else:
                    own = slice(far_chans + g * LANES, far_chans + (g + 1) * LANES)
                    tile = q_v[own, pl.ds(pl.multiple_of(tp * out_toks + h * LANES, LANES), LANES)]
                qd[r, g, h * LANES:(h + 1) * LANES, :] = tile.T.astype(f32)

    dec = dec_t[...]
    lam1 = jnp.exp(-block * dec)
    second_pass(0)
    second_pass(1)
    far_pass(0)
    lax.fori_loop(0, near_groups, lambda g, carry: prepare(g, carry, True), 0)
    lax.fori_loop(near_groups, groups, lambda g, carry: prepare(g, carry, False), 0)
    send_x.wait_recv()
    same, across = s_own[...], s_x[...]
    g_z[0] = jnp.where(x_hi == 0, across + lam1 * same, same + lam1 * across)
    sends_z = [remote(g_z.at[0], g_z.at[j], z_send.at[j], z_recv.at[j], to_z[j]) for j in range(1, NZ)]
    for send in sends_z:
        send.start()

    loads[2].wait()
    for g in range(near_groups):
        for s in range(SUBS):
            turned = q_v[g * LANES:(g + 1) * LANES, s * sub_len:(s + 1) * sub_len].T.astype(f32)
            qs[g, s * sub_len:(s + 1) * sub_len, :] = turned
    turn_query(0)
    hand_on(W_ORDER[0])
    on_by_y(W_ORDER[0])
    far_pass(1)
    far[1][f_dec].wait_recv()
    far[1][f_res].wait_recv()
    far[2][f_dec].start()
    far[2][f_res].start()
    hand_on(W_ORDER[1])
    on_by_y(W_ORDER[1])
    far_pass(2)
    after = [(NZ - 1 - lax.rem(z + NZ - j, NZ)).astype(f32) * (block * NX) for j in range(NZ)]
    by_total = [jnp.exp(-a * dec) for a in after]
    by_before = [None] + [
        jnp.where(z >= j, jnp.exp(-(block * NX * (j - 1)) * dec), 0.0) for j in range(1, NZ)
    ]
    for send in sends_z:
        send.wait_recv()
    total = by_total[0] * g_z[0]
    before = jnp.zeros_like(dec)
    for j in range(1, NZ):
        part = g_z[j]
        total += by_total[j] * part
        before += by_before[j] * part
    h_y[0] = total
    sends_y = [remote(h_y.at[0], h_y.at[j], y_send.at[j], y_recv.at[j], to_y[j]) for j in range(1, NY)]
    for send in sends_y:
        send.start()

    hand_on(W_ORDER[2])
    on_by_y(W_ORDER[2])
    far_pass(3)
    for i in W_ORDER[3:5]:
        hand_on(i)
        on_by_y(i)

    start_z = z.astype(f32) * (block * NX)
    by_y = [jnp.exp(-(block * NX * NZ * (j - 1) + start_z) * dec) for j in range(1, NY + 1)]
    once = once_t[...]
    before = once * before
    beside = once * s_x[...]
    for send in sends_y:
        send.wait_recv()
    came = before
    for j in range(1, NY + 1):
        came += by_y[j - 1] * h_y[j % NY]
    inc[...] = jnp.where(x_hi == 0, came, lam1 * came + beside)

    for g in range(far_groups):
        for m in range(modes):
            all_g = near_groups + g
            t_rows[g, m * SUBS:(m + 1) * SUBS, :] = loc[all_g, m] + pw[all_g, m] * wide(inc, all_g, m)
        for k in range(NTP):
            t_out[k, g] = t_rows[g, pl.ds(k * (SUBS // NTP), modes, stride=SUBS), :]
    t_sends = [
        remote(t_out.at[partner_tp[r]], t_in.at[r - 1], t_send.at[r - 1], t_recv.at[r - 1], to_tp[r])
        for r in range(1, NTP)
    ]
    for r in (2, 3, 1):
        t_sends[r - 1].start()
    for i in W_ORDER[5:7]:
        hand_on(i)
        on_by_y(i)

    g_sends = [
        [
            remote(
                gb.at[g, pl.ds(pl.multiple_of(partner_tp[r] * out_toks, out_toks), out_toks)],
                gin.at[r - 1, g], g_send.at[r - 1, g], g_recv.at[r - 1, g], to_tp[r],
            )
            for r in range(1, NTP)
        ]
        for g in range(near_groups)
    ]
    for g in range(near_groups):
        start = [loc[g, m] + pw[g, m] * wide(inc, g, m) for m in range(modes)]
        lam = [wide(lam_t, g, m) for m in range(modes)]

        def step(t, states):
            states = tuple(l * u for l, u in zip(lam, states))
            yn[g, pl.ds(t, SUBS, stride=sub_len), :] = ys[g, at(t), :] + tree_sum(list(states))
            return states

        lax.fori_loop(0, sub_len, step, tuple(start), unroll=UNROLL)
        gb[g] = (qs[g] * yn[g].astype(bf16).astype(f32)).astype(bf16)
        for r in (2, 3, 1):
            g_sends[g][r - 1].start()
        if g == 0:
            hand_on(W_ORDER[7])
            on_by_y(W_ORDER[7])

    def far_correct(r):
        if r:
            t_sends[r - 1].wait_recv()
            far[r - 1][f_q].wait_recv()
            turn_query(r)

        def of_group(g, carry):
            came = (lambda m: wide(t_in, r - 1, g, m)) if r else (lambda m: wide(t_out, tp, g, m))
            start = [loc_d[r, g, m] + pw_d[r, g, m] * came(m) for m in range(modes)]
            lam = [wide(lam_d, r, g, m) for m in range(modes)]

            def step(t, states):
                states = tuple(l * u for l, u in zip(lam, states))
                ynd[pl.ds(t, SUBS, stride=far_len), :] = yd[r, g, at(t), :] + tree_sum(list(states))
                return states

            lax.fori_loop(0, far_len, step, tuple(start), unroll=UNROLL)
            gd[r, g] = (qd[r, g] * ynd[...].astype(bf16).astype(f32)).astype(bf16)
            return carry

        lax.fori_loop(0, far_groups, of_group, 0)

    far_correct(0)
    hand_across(0)
    far_correct(1)
    hand_across(3)
    far_correct(2)
    hand_across(1)
    hand_across(4)
    far_correct(3)
    hand_across(2)
    hand_across(5)

    loads[3].wait()
    w_sib.wait_recv()
    for g in range(near_groups):
        g_sends[g][0].wait_recv()
    lhs = jnp.concatenate(
        [gb[g, own_toks, :] for g in range(near_groups)] + [gd[0, g] for g in range(far_groups)]
        + [gin[0, g] for g in range(near_groups)] + [gd[1, g] for g in range(far_groups)], axis=1
    )
    acc[...] = jnp.dot(lhs, jnp.concatenate([wf[0], wf[1]], axis=0), preferred_element_type=f32)
    for per_piece in w_across:
        for copy in per_piece:
            copy.wait_recv()
    lhs = jnp.concatenate([gd[r, g] for r in (2, 3) for g in range(far_groups)], axis=1)
    rhs = jnp.concatenate([wf[r, far_chans:, :] for r in (2, 3)], axis=0)
    acc[...] += jnp.dot(lhs, rhs, preferred_element_type=f32)
    for g in range(near_groups):
        rows = slice(g * LANES, (g + 1) * LANES)
        g_sends[g][1].wait_recv()
        g_sends[g][2].wait_recv()
        lhs = jnp.concatenate([gin[1, g], gin[2, g]], axis=1)
        rhs = jnp.concatenate([wf[2, rows, :], wf[3, rows, :]], axis=0)
        part = acc[...] + jnp.dot(lhs, rhs, preferred_element_type=f32)
        if g == near_groups - 1:
            out_ref[...] = part.astype(bf16)
        else:
            acc[...] = part

    for copy in [w_sib, send_x] + sends_z + sends_y + t_sends + w_import:
        copy.wait_send()
    for family in (far, w_on, w_across, g_sends):
        for part in family:
            for copy in part:
                copy.wait_send()


def shards(kv_product, query, decay_rate, residue, out_weight):
    chans, toks = kv_product.shape
    modes = decay_rate.shape[1]
    cols = out_weight.shape[1]
    groups = chans // LANES
    near, far = groups // 2, groups - groups // 2
    out_toks = toks // NTP
    bf16, f32 = jnp.bfloat16, jnp.float32
    small = (groups, modes, LANES)
    runs = (groups, modes, SUBS, LANES)
    far_block = (NTP - 1, chans // 2, out_toks)
    far_coef = (NTP - 1, modes, chans // 2)
    pieces = W_PIECES
    vmem, dma = pltpu.VMEM, pltpu.SemaphoreType.DMA
    operands = (kv_product, query, decay_rate.T, residue.T, out_weight)
    return pl.pallas_call(
        kernel,
        out_shape=jax.ShapeDtypeStruct((out_toks, cols), bf16),
        in_specs=[pl.BlockSpec(memory_space=pltpu.HBM)] * 5,
        out_specs=pl.BlockSpec(memory_space=pltpu.VMEM),
        scratch_shapes=[
            vmem((chans, toks), bf16), vmem((chans, toks), bf16), vmem((modes, chans), f32), vmem((modes, chans), f32),
            vmem(far_block, bf16), vmem(far_block, bf16), vmem(far_coef, f32), vmem(far_coef, f32),
            vmem((NTP, chans, cols), bf16),
            vmem((groups, toks, LANES), f32), vmem((near, toks, LANES), f32),
            vmem((near, toks, LANES), f32), vmem((near, toks, LANES), f32),
            vmem(small, f32), vmem(small, f32), vmem(small, f32), vmem(small, f32), vmem(small, f32),
            vmem((3,) + small, f32),
            vmem(runs, f32), vmem(runs, f32), vmem(runs, f32),
            vmem(small, f32), vmem(small, f32), vmem((NZ,) + small, f32), vmem((NY,) + small, f32), vmem(small, f32),
            vmem((far, modes * SUBS, LANES), f32),
            vmem((NTP, far, modes, LANES), f32), vmem((NTP - 1, far, modes, LANES), f32),
            vmem((NTP, far, out_toks, LANES), f32), vmem((NTP, far, out_toks, LANES), f32),
            vmem((NTP, far, out_toks, LANES), f32), vmem((out_toks, LANES), f32),
            vmem((NTP, far, modes, LANES), f32), vmem((NTP, far, modes, LANES), f32),
            vmem((NTP, far, modes, LANES), f32), vmem((NTP, far, modes, LANES), f32),
            vmem((NTP, far, modes, LANES), f32), vmem((3, NTP, far, modes, LANES), f32),
            vmem((NTP, far, modes, SUBS, LANES), f32), vmem((NTP, far, modes, SUBS, LANES), f32),
            vmem((near, toks, LANES), bf16), vmem((NTP - 1, near, out_toks, LANES), bf16),
            vmem((NTP, far, out_toks, LANES), bf16), vmem((out_toks, cols), f32),
            dma((4 + groups,)), dma((2,)), dma((NZ,)), dma((NZ,)), dma((NY,)), dma((NY,)),
            dma((NTP - 1, far + 3)), dma((NTP - 1, far + 3)), dma((NTP - 1,)), dma((NTP - 1,)),
            dma((2,)), dma((pieces,)), dma((pieces,)), dma((3, pieces)), dma((3, pieces)),
            dma((4, len(W_UNITS))), dma((4, len(W_UNITS))), dma((NTP - 1, near)), dma((NTP - 1, near)),
        ],
        compiler_params=pltpu.CompilerParams(
            collective_id=0, has_side_effects=True, vmem_limit_bytes=50 * 1024 * 1024
        ),
        cost_estimate=pl.CostEstimate(
            flops=2 * out_toks * cols * chans * NTP, bytes_accessed=6 * 1024 * 1024, transcendentals=0
        ),
    )(*(pltpu.with_memory_space_constraint(a, pltpu.HBM) for a in operands))


def solution(mesh):
    in_specs = (P("tp", "ctx"), P("tp", "ctx"), P("tp", None), P("tp", None), P("tp", None))
    out_specs = P(("ctx", "tp"), None)
    return jax.shard_map(shards, mesh=mesh, in_specs=in_specs, out_specs=out_specs, check_vma=False)
```
